512 devices in a mesh: src: 32 (over y, z_lo), slab: 16 (over z_hi, x, core).
Axes of the slice: x: 4, y: 4, z: 16 (z_hi: 2, z_lo: 8; z = z_hi * 8 + z_lo), core: 2. Of those that a mesh axis runs over, the one named last changes fastest.
Arguments:
- source_field: float32 [32, 16, 25600], P('src', 'slab'), may hold values from -6 to 6
- kappa: float32 [16, 25600], P('slab'), may hold values from 0.5 to 2
- absorb: float32 [16, 25600], P('slab'), may hold values from 0.02 to 0.2
- det_cell: int32 [512], replicated, may hold values from 0 to 409599
- pair_det: int32 [32, 256], P('src'), may hold values from 0 to 511
- pair_count: int32 [32], P('src'), may hold values from 1 to 256, as said below
- measured: float32 [2, 32, 256], P(None, 'src'), may hold values from -6 to 6
Outputs:
- grad_absorb: float32 [16, 25600], P('slab', 'src')
- grad_diffuse: float32 [16, 25600], P('slab', 'src')
The draws below stay inside these ranges and needn't reach their ends.
Inputs may be any that keep to these rules, and one draw needn't show every extreme that they name: `pair_count`: some source has exactly 256 live pairs in every draw.
All inputs are finite; a program needn't handle non-finite values.
Results may differ from the reference program's by a relative error of at most 0.0003.
Values sent between devices are 32-bit elements; how exact they have to be, the bound alone decides.
A program may use at most 128 MiB of HBM per device.

```python
import math
import jax
import jax.numpy as jnp
from jax import lax

NX = 160
NY = 160
SWEEPS = 6
NDET = 512
PAIRS = 256
SOURCES = 32
NZ = 16


def draw_pair_count(key, part):
    key_counts, key_top = jax.random.split(jax.random.fold_in(key, 7))
    counts = jax.random.randint(key_counts, (SOURCES,), 1, PAIRS + 1)
    top_source = jax.random.randint(key_top, (), 0, SOURCES)
    return jnp.where(jnp.arange(SOURCES) == top_source, PAIRS, counts).astype(jnp.int32)


def with_ends(values, stream_key, low, top_value):
    longest = values.shape.index(max(values.shape))
    spots = []
    for shift in (0, 1):
        where = [jax.random.randint(jax.random.fold_in(stream_key, axis), (), 0, length) for axis, length in enumerate(values.shape)]
        where[longest] = (where[longest] + shift) % values.shape[longest]
        spots.append(tuple(where))
    return values.at[spots[0]].set(low).at[spots[1]].set(top_value)


def steps_of(rng, extent, shards, least, high):
    loudness, own = 1.0, jax.random.fold_in(rng, 6)
    for dim, parts in shards:
        draws = jnp.exp(jax.random.uniform(jax.random.fold_in(own, dim), (parts,), jnp.float32, least / len(shards), high / len(shards)))
        loudness = loudness * jnp.repeat(draws, extent[dim] // parts).reshape([-1 if axis == dim else 1 for axis in range(len(extent))])
    return loudness


def normal_values(rng, shape, spread, limit, cuts=(), dtype=jnp.bfloat16):
    loudness = steps_of(rng, shape, cuts, -0.22, 0.18) if cuts else 1.0
    result = jax.random.normal(rng, shape, jnp.float32) * spread * loudness
    return jnp.minimum(jnp.maximum(result, -limit), limit).astype(dtype)


def setup_inputs(seed: int = 0) -> dict:
    key_list = jax.random.split(jax.random.key(seed), 8)
    source_field = normal_values(key_list[0], (SOURCES, NZ, NX * NY), 1.0, 6.0, ((0, 32), (1, 16)), jnp.float32)
    kappa = jnp.clip(jnp.exp(math.log(2.0) - 1.3862944 * jax.random.uniform(key_list[1], (NZ, NX * NY), jnp.float32) ** steps_of(key_list[1], (NZ, NX * NY), ((0, 16),), -0.2, 0.2)), 0.5, 2.0)
    absorb = jnp.clip(jnp.exp(math.log(0.2) - 2.3025851 * jax.random.uniform(key_list[2], (NZ, NX * NY), jnp.float32) ** steps_of(key_list[2], (NZ, NX * NY), ((0, 16),), -0.2, 0.2)), 0.02, 0.2)
    det_cell = with_ends(jax.random.randint(key_list[3], (NDET,), 0, NZ * NX * NY), jax.random.fold_in(key_list[3], 1), 0, (NZ * NX * NY) - 1).astype(jnp.int32)
    pair_det = with_ends(jax.random.randint(key_list[4], (SOURCES, PAIRS), 0, NDET), jax.random.fold_in(key_list[4], 1), 0, NDET - 1).astype(jnp.int32)
    pair_count = draw_pair_count(jax.random.fold_in(key_list[7], 71), 0)
    measured = normal_values(key_list[6], (2, SOURCES, PAIRS), 1.0, 6.0, ((1, 32),), jnp.float32)
    return dict(source_field=source_field, kappa=kappa, absorb=absorb, det_cell=det_cell, pair_det=pair_det, pair_count=pair_count, measured=measured)


spectrum_low = 0.02
spectrum_high = 25.0
frequency_shift = 0.3


def chebyshev_terms():
    theta = (spectrum_high + spectrum_low) / 2.0
    delta = (spectrum_high - spectrum_low) / 2.0
    sigma = theta / delta
    rho = 1.0 / sigma
    keeps = []
    pushes = []
    for sweep in range(SWEEPS - 1):
        rho_new = 1.0 / (2.0 * sigma - rho)
        keeps.append(rho_new * rho)
        pushes.append(2.0 * rho_new / delta)
        rho = rho_new
    return 1.0 / theta, keeps, pushes


def neighbours(padded):
    return [padded[..., :-2, 1:-1, 1:-1], padded[..., 2:, 1:-1, 1:-1],
            padded[..., 1:-1, :-2, 1:-1], padded[..., 1:-1, 2:, 1:-1],
            padded[..., 1:-1, 1:-1, :-2], padded[..., 1:-1, 1:-1, 2:]]


def pad_field(field):
    return jnp.pad(field, ((0, 0), (1, 1), (1, 1), (1, 1)))


def apply_operator(field, faces, diagonal):
    beside = neighbours(pad_field(field))
    offdiag = faces[0] * beside[0]
    for which in range(1, 6):
        offdiag = offdiag + faces[which] * beside[which]
    turned = jnp.stack([-field[1], field[0]])
    return diagonal * field - offdiag + frequency_shift * turned


def chebyshev(right, faces, diagonal):
    first, keeps, pushes = chebyshev_terms()
    solution = jnp.zeros_like(right)
    residual_field = right
    direction = right * first
    for sweep in range(SWEEPS):
        solution = solution + direction
        residual_field = residual_field - apply_operator(direction, faces, diagonal)
        if sweep < SWEEPS - 1:
            direction = keeps[sweep] * direction + pushes[sweep] * residual_field
    return solution


def reference(source_field, kappa, absorb, det_cell, pair_det, pair_count, measured):
    cells = NZ * NX * NY
    kappa_grid = kappa.reshape(NZ, NX, NY)
    kappa_pad = jnp.pad(kappa_grid, 1)
    faces = [(kappa_grid + side) * 0.5 for side in neighbours(kappa_pad)]
    diagonal = faces[0] + faces[1] + faces[2] + faces[3] + faces[4] + faces[5] + absorb.reshape(NZ, NX, NY)
    measured_t = jnp.moveaxis(measured, 1, 0)

    def one_source(carry, input_arrays):
        source_index, source_detector_pairs, detector_count, measurement_data = input_arrays
        right = jnp.stack([source_index.reshape(NZ, NX, NY), jnp.zeros((NZ, NX, NY), jnp.float32)])
        forward = chebyshev(right, faces, diagonal)
        readings = forward.reshape(2, cells)[:, det_cell]
        optical_model = readings[:, source_detector_pairs]
        active_flag = (jnp.arange(PAIRS) < detector_count).astype(jnp.float32)
        residual_field = (optical_model - measurement_data) * active_flag[None, :]
        conj = jnp.stack([residual_field[0], -residual_field[1]])
        onehot = (source_detector_pairs[:, None] == jnp.arange(NDET)[None, :]).astype(jnp.float32)
        weights = jnp.dot(conj, onehot, precision=lax.Precision.HIGHEST)
        adjoint_right = jnp.zeros((2, cells), jnp.float32).at[:, det_cell].add(weights).reshape(2, NZ, NX, NY)
        adjoint = chebyshev(adjoint_right, faces, diagonal)
        g_abs = -(forward[0] * adjoint[0] - forward[1] * adjoint[1])
        fwd_side = neighbours(pad_field(forward))
        adj_side = neighbours(pad_field(adjoint))
        total = jnp.zeros((2, NZ, NX, NY), jnp.float32)
        for which in range(6):
            total = total + (forward - fwd_side[which]) * (adjoint - adj_side[which])
        g_dif = -0.5 * (total[0] - total[1])
        return (carry[0] + g_abs, carry[1] + g_dif), None

    start = (jnp.zeros((NZ, NX, NY), jnp.float32), jnp.zeros((NZ, NX, NY), jnp.float32))
    sums, unused = lax.scan(one_source, start, (source_field, pair_det, pair_count, measured_t))
    return sums[0].reshape(NZ, NX * NY), sums[1].reshape(NZ, NX * NY)
```

```python
import jax
import jax.numpy as jnp
from jax import lax
from jax.experimental import pallas as pl
from jax.experimental.pallas import tpu as pltpu
from jax.sharding import PartitionSpec as P

NY = 160
SWEEPS = 6
NDET = 512
PAIRS = 256
SLABS = 16
OWN = 10
HALO = 6
SLOT = 32
LANES = 128
MESH = pl.DeviceIdType.MESH
F32 = jnp.float32
BF16 = jnp.bfloat16

spectrum_low = 0.02
spectrum_high = 25.0
frequency_shift = 0.3


def chebyshev_terms():
    theta = (spectrum_high + spectrum_low) / 2.0
    delta = (spectrum_high - spectrum_low) / 2.0
    sigma = theta / delta
    rho = 1.0 / sigma
    keeps = []
    pushes = []
    for sweep in range(SWEEPS - 1):
        rho_new = 1.0 / (2.0 * sigma - rho)
        keeps.append(rho_new * rho)
        pushes.append(2.0 * rho_new / delta)
        rho = rho_new
    return (1.0 / theta, keeps, pushes)


def parts_of(value):
    high = value.astype(BF16)
    rest = value - high.astype(F32)
    middle = rest.astype(BF16)
    low = (rest - middle.astype(F32)).astype(BF16)
    return (high, middle, low)


def dot_parts(lhs_parts, rhs_parts, dims):
    total = None
    for lhs in lhs_parts:
        for rhs in rhs_parts:
            term = lax.dot_general(lhs, rhs, (dims, ((), ())), preferred_element_type=F32)
            total = term if total is None else total + term
    return total


def pick(table, index):
    value = jnp.float32(table[0])
    for which in range(1, len(table)):
        value = jnp.where(index == which, jnp.float32(table[which]), value)
    return value


def kernel(
    count_ref, source_ref, kappa_ref, absorb_ref, cell_ref, pair_ref, measured_ref,
    out_abs_ref, out_dif_ref,
    plain, half, send, recv, coef, direc, resid, field, grads,
    place, lane_hot, pair_hot, reads, ysend, yrecv, fsend, frecv,
    a_send, a_recv, r_send, r_recv, y_send, y_recv, f_send, f_recv,
):
    src = lax.axis_index("src")
    slab = lax.axis_index("slab")
    my_y = src // 8
    my_zlo = src % 8

    def is_me(dev):
        return (dev[0] == src) & (dev[1] == slab)

    slab_peers = [(src, lax.rem(slab + j, SLABS)) for j in range(1, SLABS)]
    y_peers = [(lax.rem(my_y + j, 4) * 8 + my_zlo, slab) for j in range(1, 4)]
    final_to = [[(2 * slab + h, 4 * my_y + t) for h in range(2)] for t in range(4)]
    final_from = [((slab // 4) * 8 + m, src // 2) for m in range(8)]

    barrier = pltpu.get_barrier_semaphore()
    for dev in slab_peers + y_peers:
        pl.semaphore_signal(barrier, inc=1, device_id=dev, device_id_type=MESH)
    for dev in final_from:
        mine = is_me(dev)

        @pl.when(jnp.logical_not(mine))
        def _():
            pl.semaphore_signal(barrier, inc=1, device_id=dev, device_id_type=MESH)

    to_self = jnp.where((src // 8 == slab // 4) & (slab == src // 2), 1, 0)

    lane = lax.broadcasted_iota(jnp.int32, (SLOT, LANES), 1)
    flat = lax.broadcasted_iota(jnp.int32, (SLOT, LANES), 0) * LANES + lane
    row = ((flat >> 5) * 205) >> 10
    col = flat - row * NY
    real_row = row + (OWN * slab - HALO)
    row_in = (real_row >= 0) & (real_row < 160)
    xp_in = (row_in & (real_row < 159)).astype(F32)
    xm_in = (row_in & (real_row > 0)).astype(F32)
    yp_in = (col < NY - 1).astype(F32)
    ym_in = (col > 0).astype(F32)

    def x_plus(ref, base):
        near, far = ref[pl.ds(base + 1, SLOT), :], ref[pl.ds(base + 2, SLOT), :]
        return pltpu.roll(jnp.where(lane >= 32, near, far), 96, 1)

    def x_minus(ref, base):
        near, far = ref[pl.ds(base - 1, SLOT), :], ref[pl.ds(base - 2, SLOT), :]
        return pltpu.roll(jnp.where(lane < 96, near, far), 32, 1)

    def y_plus(ref, base, here):
        return pltpu.roll(jnp.where(lane >= 1, here, ref[pl.ds(base + 1, SLOT), :]), 127, 1)

    def y_minus(ref, base, here):
        return pltpu.roll(jnp.where(lane < 127, here, ref[pl.ds(base - 1, SLOT), :]), 1, 1)

    def at(p):
        return pl.multiple_of(p * SLOT, SLOT)

    tall = plain.shape[1]
    rows_in = kappa_ref.shape[0]
    for which, ref in enumerate((kappa_ref, absorb_ref, source_ref)):
        plane = ref[...]
        plain[which, pl.ds(0, rows_in), :] = plane
        plain[which, pl.ds(rows_in, tall - rows_in), :] = jnp.zeros((tall - rows_in, LANES), F32)
        half[which, pl.ds(0, 8), :] = jnp.zeros((8, LANES), F32)
        half[which, pl.ds(8, rows_in), :] = pltpu.roll(plane, 64, 1)
        half[which, pl.ds(8 + rows_in, tall - rows_in - 8), :] = jnp.zeros((tall - rows_in - 8, LANES), F32)
        for m in range(8):
            send[2 * m, which] = jnp.where(
                lane < 64, half[which, pl.ds(25 * m, SLOT), :], half[which, pl.ds(25 * m + 1, SLOT), :]
            )
            send[2 * m + 1, which] = plain[which, pl.ds(25 * m + 5, SLOT), :]

    pl.semaphore_wait(barrier, 15 + 3 + 8 - to_self)
    copies = []
    for j, dev in enumerate(slab_peers):
        copy = pltpu.make_async_remote_copy(
            src_ref=send.at[dev[1]],
            dst_ref=recv.at[:, pl.ds(at(slab + 1), SLOT), :],
            send_sem=a_send.at[j],
            recv_sem=a_recv.at[j],
            device_id=dev,
            device_id_type=MESH,
        )
        copy.start()
        copies.append(copy)

    guard = jnp.zeros((SLOT, LANES), F32)
    last = (SLABS + 1) * SLOT
    for start in (0, last):
        recv[0, pl.ds(start, SLOT), :] = guard
        for a in range(2):
            for b in range(2):
                direc[a, b, pl.ds(start, SLOT), :] = guard
                field[a, b, pl.ds(start, SLOT), :] = guard
    recv[:, pl.ds(at(slab + 1), SLOT), :] = send[slab]

    cell = cell_ref[...]
    det_z = ((cell >> 10) * 1311) >> 15
    in_plane = cell - det_z * 25600
    det_x = ((in_plane >> 5) * 6554) >> 15
    det_y = in_plane - det_x * NY
    det_row = det_x - (OWN * slab - HALO)
    in_window = (det_row >= 0) & (det_row < OWN + 2 * HALO)
    owned = ((det_row >= HALO) & (det_row < HALO + OWN)).astype(F32)
    spot = det_row * NY + det_y
    det_sub = jnp.where(in_window, det_z * SLOT + (spot >> 7), -1)
    det_lane = spot & 127

    @pl.loop(0, SLABS)
    def _(p):
        subs = lax.broadcasted_iota(jnp.int32, (SLOT, NDET), 0) + p * SLOT
        place[pl.ds(at(p), SLOT), :] = (subs == det_sub).astype(F32).astype(BF16)

    lane_hot[...] = (lax.broadcasted_iota(jnp.int32, (LANES, NDET), 0) == det_lane).astype(F32)
    pair_hot[...] = (
        lax.broadcasted_iota(jnp.int32, (NDET, PAIRS), 0) == pair_ref[...]
    ).astype(F32).astype(BF16)

    for copy in copies:
        copy.wait()

    first, keeps, pushes = chebyshev_terms()
    kappa, absorb, source = recv.at[0], recv.at[1], recv.at[2]

    @pl.loop(0, SLABS)
    def _(p):
        base, here = at(p + 1), at(p)
        k = kappa[pl.ds(base, SLOT), :]
        diagonal = absorb[pl.ds(base, SLOT), :]
        beside = (
            (x_plus(kappa, base), xp_in),
            (x_minus(kappa, base), xm_in),
            (y_plus(kappa, base, k) * yp_in, yp_in),
            (y_minus(kappa, base, k) * ym_in, ym_in),
            (kappa[pl.ds(base + SLOT, SLOT), :], jnp.where(p < SLABS - 1, 1.0, 0.0).astype(F32)),
            (kappa[pl.ds(base - SLOT, SLOT), :], jnp.where(p > 0, 1.0, 0.0).astype(F32)),
        )
        for which, (side, inside) in enumerate(beside):
            face = (k + side) * 0.5
            diagonal = diagonal + face
            coef[which, pl.ds(here, SLOT), :] = face * inside
        coef[6, pl.ds(here, SLOT), :] = diagonal
        b = source[pl.ds(base, SLOT), :]
        resid[0, pl.ds(here, SLOT), :] = b
        resid[1, pl.ds(here, SLOT), :] = jnp.zeros_like(b)
        direc[0, 0, pl.ds(base, SLOT), :] = b * first
        direc[0, 1, pl.ds(base, SLOT), :] = jnp.zeros_like(b)
        field[0, 0, pl.ds(base, SLOT), :] = b * first
        field[0, 1, pl.ds(base, SLOT), :] = jnp.zeros_like(b)

    def solve(out):
        @pl.loop(0, SWEEPS - 1)
        def _(sweep):
            keep, push = pick(keeps, sweep), pick(pushes, sweep)
            now, later = sweep % 2, (sweep + 1) % 2

            @pl.loop(0, SLABS)
            def _(p):
                base, here = at(p + 1), at(p)
                cs = [coef[which, pl.ds(here, SLOT), :] for which in range(7)]
                ds = [direc[now, c, pl.ds(base, SLOT), :] for c in range(2)]
                turned = (-ds[1], ds[0])
                for c in range(2):
                    ref = direc.at[now, c]
                    off = (
                        cs[0] * x_plus(ref, base)
                        + cs[1] * x_minus(ref, base)
                        + cs[2] * y_plus(ref, base, ds[c])
                        + cs[3] * y_minus(ref, base, ds[c])
                        + cs[4] * ref[pl.ds(base + SLOT, SLOT), :]
                        + cs[5] * ref[pl.ds(base - SLOT, SLOT), :]
                    )
                    applied = cs[6] * ds[c] - off + frequency_shift * turned[c]
                    left = resid[c, pl.ds(here, SLOT), :] - applied
                    resid[c, pl.ds(here, SLOT), :] = left
                    new = keep * ds[c] + push * left
                    direc[later, c, pl.ds(base, SLOT), :] = new
                    field[out, c, pl.ds(base, SLOT), :] = field[out, c, pl.ds(base, SLOT), :] + new

    solve(0)

    whole = pl.ds(SLOT, SLABS * SLOT)
    for c in range(2):
        spread = dot_parts(parts_of(field[0, c, whole, :]), (place[...],), ((0,), (0,)))
        reads[slab, pl.ds(c, 1), :] = jnp.sum(spread * lane_hot[...], axis=0, keepdims=True) * owned
    copies = []
    for j, dev in enumerate(slab_peers):
        copy = pltpu.make_async_remote_copy(
            src_ref=reads.at[slab],
            dst_ref=reads.at[slab],
            send_sem=r_send.at[j],
            recv_sem=r_recv.at[j],
            device_id=dev,
            device_id_type=MESH,
        )
        copy.start()
        copies.append(copy)
    for copy in copies:
        copy.wait()
    readings = jnp.sum(reads[...], axis=0)
    wide = jnp.concatenate([readings, jnp.zeros((6, NDET), F32)], axis=0)
    model = dot_parts(parts_of(wide), (pair_hot[...],), ((1,), (0,)))
    active = (lax.broadcasted_iota(jnp.int32, (1, PAIRS), 1) < count_ref[0]).astype(F32)
    conj = jnp.concatenate(
        [
            (model[0:1] - measured_ref[0]) * active,
            (measured_ref[1] - model[1:2]) * active,
            jnp.zeros((6, PAIRS), F32),
        ],
        axis=0,
    )
    weights = dot_parts(parts_of(conj), (pair_hot[...],), ((1,), (1,)))
    for c in range(2):
        hot = lane_hot[...]
        pieces = [(hot * part.astype(F32)).astype(BF16) for part in parts_of(weights[c : c + 1])]
        right = dot_parts((place[...],), pieces, ((1,), (1,)))
        resid[c] = right
        direc[0, c, whole, :] = right * first
        field[1, c, whole, :] = right * first

    solve(1)

    @pl.loop(0, SLABS)
    def _(p):
        base = at(p + 1)
        refs = [[field.at[a, c] for c in range(2)] for a in range(2)]
        here = [[refs[a][c][pl.ds(base, SLOT), :] for c in range(2)] for a in range(2)]
        sides = (
            x_plus,
            x_minus,
            lambda ref, b: y_plus(ref, b, ref[pl.ds(b, SLOT), :]) * yp_in,
            lambda ref, b: y_minus(ref, b, ref[pl.ds(b, SLOT), :]) * ym_in,
            lambda ref, b: ref[pl.ds(b + SLOT, SLOT), :],
            lambda ref, b: ref[pl.ds(b - SLOT, SLOT), :],
        )
        total = jnp.zeros((SLOT, LANES), F32)
        for side in sides:
            gap = [[here[a][c] - side(refs[a][c], base) for c in range(2)] for a in range(2)]
            total = total + gap[0][0] * gap[1][0] - gap[0][1] * gap[1][1]
        grads[0] = here[0][1] * here[1][1] - here[0][0] * here[1][0]
        grads[1] = -0.5 * total
        for out in range(2):
            low, high = grads[out, pl.ds(7, 16), :], grads[out, pl.ds(8, 16), :]
            ysend[p, out] = pltpu.roll(jnp.where(lane[0:16] >= 64, low, high), 64, 1)

    copies = []
    for j, dev in enumerate(y_peers):
        copy = pltpu.make_async_remote_copy(
            src_ref=ysend.at[pl.ds((dev[0] // 8) * 4, 4)],
            dst_ref=yrecv.at[j],
            send_sem=y_send.at[j],
            recv_sem=y_recv.at[j],
            device_id=dev,
            device_id_type=MESH,
        )
        copy.start()
        copies.append(copy)
    for copy in copies:
        copy.wait()
    for t in range(4):
        for out in range(2):
            total = ysend[my_y * 4 + t, out] + yrecv[0, t, out] + yrecv[1, t, out] + yrecv[2, t, out]
            fsend[t, 0, out] = total[0:8]
            grads[out, pl.ds(0, 16), :] = total
            low, high = grads[out, pl.ds(6, 8), :], grads[out, pl.ds(7, 8), :]
            fsend[t, 1, out] = pltpu.roll(jnp.where(lane[0:8] >= 32, low, high), 96, 1)

    def final_copy(t, h):
        return pltpu.make_async_remote_copy(
            src_ref=fsend.at[t, h],
            dst_ref=frecv.at[my_zlo],
            send_sem=f_send.at[2 * t + h],
            recv_sem=f_recv.at[my_zlo],
            device_id=final_to[t][h],
            device_id_type=MESH,
        )

    for t in range(4):
        for h in range(2):
            mine = is_me(final_to[t][h])

            @pl.when(jnp.logical_not(mine))
            def _():
                final_copy(t, h).start()

            @pl.when(mine)
            def _():
                pltpu.make_async_copy(fsend.at[t, h], frecv.at[my_zlo], f_recv.at[my_zlo]).start()

    for m in range(8):
        pltpu.make_async_copy(frecv.at[m], frecv.at[m], f_recv.at[m]).wait()
    for out, out_ref in enumerate((out_abs_ref, out_dif_ref)):
        total = frecv[0, out]
        for m in range(1, 8):
            total = total + frecv[m, out]
        for k in range(6):
            out_ref[0:1, pl.ds(128 * k, 128)] = total[k : k + 1]
        out_ref[0:1, pl.ds(768, 32)] = total[6:7, 0:32]
    for t in range(4):
        for h in range(2):

            @pl.when(jnp.logical_not(is_me(final_to[t][h])))
            def _():
                final_copy(t, h).wait_send()


def body(source_field, kappa, absorb, det_cell, pair_det, pair_count, measured):
    tall = 216
    vmem = pl.BlockSpec(memory_space=pltpu.VMEM)
    stacked = (SLABS + 2) * SLOT
    flat = SLABS * SLOT
    out = jax.ShapeDtypeStruct((1, 800), F32)
    dma = pltpu.SemaphoreType.DMA
    return pl.pallas_call(
        kernel,
        out_shape=(out, out),
        in_specs=[pl.BlockSpec(memory_space=pltpu.SMEM)] + [vmem] * 6,
        out_specs=(vmem, vmem),
        scratch_shapes=[
            pltpu.VMEM((3, tall, LANES), F32),
            pltpu.VMEM((3, tall, LANES), F32),
            pltpu.VMEM((SLABS, 3, SLOT, LANES), F32),
            pltpu.VMEM((3, stacked, LANES), F32),
            pltpu.VMEM((7, flat, LANES), F32),
            pltpu.VMEM((2, 2, stacked, LANES), F32),
            pltpu.VMEM((2, flat, LANES), F32),
            pltpu.VMEM((2, 2, stacked, LANES), F32),
            pltpu.VMEM((2, SLOT, LANES), F32),
            pltpu.VMEM((flat, NDET), BF16),
            pltpu.VMEM((LANES, NDET), F32),
            pltpu.VMEM((NDET, PAIRS), BF16),
            pltpu.VMEM((SLABS, 2, NDET), F32),
            pltpu.VMEM((SLABS, 2, 16, LANES), F32),
            pltpu.VMEM((3, 4, 2, 16, LANES), F32),
            pltpu.VMEM((4, 2, 2, 8, LANES), F32),
            pltpu.VMEM((8, 2, 8, LANES), F32),
            dma((15,)), dma((15,)), dma((15,)), dma((15,)),
            dma((3,)), dma((3,)), dma((8,)), dma((8,)),
        ],
        compiler_params=pltpu.CompilerParams(
            collective_id=0, has_side_effects=True, vmem_limit_bytes=40 * 1024 * 1024
        ),
    )(
        pair_count,
        source_field.reshape(200, LANES),
        kappa.reshape(200, LANES),
        absorb.reshape(200, LANES),
        det_cell.reshape(1, NDET),
        pair_det,
        measured,
    )


def solution(mesh):
    placed = (
        P("src", "slab", None),
        P("slab", None),
        P("slab", None),
        P(),
        P("src", None),
        P("src"),
        P(None, "src", None),
    )
    return jax.shard_map(
        body,
        mesh=mesh,
        in_specs=placed,
        out_specs=(P("slab", "src"), P("slab", "src")),
        check_vma=False,
    )
```

```python
import jax
import jax.numpy as jnp
from jax import lax
from jax.experimental import pallas as pl
from jax.experimental.pallas import tpu as pltpu
from jax.sharding import PartitionSpec as P

NY = 160
SWEEPS = 6
NDET = 512
PAIRS = 256
SLABS = 16
OWN = 10
HALO = 6
SLOT = 32
LANES = 128
MESH = pl.DeviceIdType.MESH
F32 = jnp.float32
BF16 = jnp.bfloat16

spectrum_low = 0.02
spectrum_high = 25.0
frequency_shift = 0.3


def chebyshev_terms():
    theta = (spectrum_high + spectrum_low) / 2.0
    delta = (spectrum_high - spectrum_low) / 2.0
    sigma = theta / delta
    rho = 1.0 / sigma
    keeps = []
    pushes = []
    for sweep in range(SWEEPS - 1):
        rho_new = 1.0 / (2.0 * sigma - rho)
        keeps.append(rho_new * rho)
        pushes.append(2.0 * rho_new / delta)
        rho = rho_new
    return (1.0 / theta, keeps, pushes)


def parts_of(value):
    high = value.astype(BF16)
    rest = value - high.astype(F32)
    middle = rest.astype(BF16)
    low = (rest - middle.astype(F32)).astype(BF16)
    return (high, middle, low)


def dot_parts(lhs_parts, rhs_parts, dims):
    total = None
    for lhs in lhs_parts:
        for rhs in rhs_parts:
            term = lax.dot_general(lhs, rhs, (dims, ((), ())), preferred_element_type=F32)
            total = term if total is None else total + term
    return total


def pick(table, index):
    value = jnp.float32(table[0])
    for which in range(1, len(table)):
        value = jnp.where(index == which, jnp.float32(table[which]), value)
    return value


def kernel(
    count_ref, source_ref, kappa_ref, absorb_ref, cell_ref, pair_ref, measured_ref,
    out_abs_ref, out_dif_ref,
    plain, half_lane, send, coef_recv, source, kappa, coef, direc_a, direc_b, resid, field, grads,
    place, lane_hot, pair_hot, pair_send, pair_recv, reads, ysend, yrecv, fsend, frecv,
    s_send, s_recv, k_send, k_recv, o_send, o_recv, g_send, g_recv, p_send, p_recv,
    r_send, r_recv, y_send, y_recv, f_send, f_recv,
):
    src = lax.axis_index("src")
    slab = lax.axis_index("slab")
    my_y = src // 8
    my_z = (slab // 8) * 8 + src % 8
    my_spot = slab % 8
    parity = my_z % 2
    pair_z = my_z - parity
    group = parity * 8 + my_spot
    solved = jnp.where((pair_z >= 4) & (pair_z <= 10), pair_z - 4, lax.rem(pair_z + 5, 16))
    own_zlo = src % 8
    goal_z = jnp.where(own_zlo % 2 == 0, own_zlo + 4, lax.rem(own_zlo + 11, 16))
    other_half = 1 - my_z // 8
    swap_z = jnp.where(src % 8 < 4, lax.rem(my_z + 12, 16), lax.rem(my_z + 4, 16))

    def device(y, z, spot):
        return (y * 8 + lax.rem(z, 8), (z // 8) * 8 + spot)

    def is_me(dev):
        return (dev[0] == src) & (dev[1] == slab)

    source_to = [device(my_y, goal_z + i // 8, i % 8) for i in range(SLABS)]
    source_from = [(my_y * 8 + solved, p) for p in range(SLABS)]
    near = [device(my_y, my_z, lax.rem(my_spot + j, 8)) for j in range(1, 8)]
    beyond = [device(my_y, swap_z, spot) for spot in range(8)]
    twin = [device(my_y, pair_z + 1 - parity, spot) for spot in range(8)]
    y_peers = [(lax.rem(my_y + j, 4) * 8 + src % 8, slab) for j in range(1, 4)]
    final_to = [[(2 * group + h, 4 * my_y + t) for h in range(2)] for t in range(4)]
    final_from = [device(slab // 4, 2 * m + src // 16, (src // 2) % 8) for m in range(8)]

    barrier = pltpu.get_barrier_semaphore()
    for dev in source_from + near + beyond + twin + y_peers:
        pl.semaphore_signal(barrier, inc=1, device_id=dev, device_id_type=MESH)
    to_self = jnp.int32(0)
    for dev in final_from:
        to_self = to_self + jnp.where(is_me(dev), 1, 0)

        @pl.when(jnp.logical_not(is_me(dev)))
        def _():
            pl.semaphore_signal(barrier, inc=1, device_id=dev, device_id_type=MESH)

    lane = lax.broadcasted_iota(jnp.int32, (SLOT, LANES), 1)
    flat = lax.broadcasted_iota(jnp.int32, (SLOT, LANES), 0) * LANES + lane
    row = ((flat >> 5) * 205) >> 10
    col = flat - row * NY
    real_row = row + (OWN * group - HALO)
    row_in = (real_row >= 0) & (real_row < 160)
    xp_in = (row_in & (real_row < 159)).astype(F32)
    xm_in = (row_in & (real_row > 0)).astype(F32)
    yp_in = (col < NY - 1).astype(F32)
    ym_in = (col > 0).astype(F32)

    def x_plus(ref, base):
        near, far = ref[pl.ds(base + 1, SLOT), :], ref[pl.ds(base + 2, SLOT), :]
        return pltpu.roll(jnp.where(lane >= 32, near, far), 96, 1)

    def x_minus(ref, base):
        near, far = ref[pl.ds(base - 1, SLOT), :], ref[pl.ds(base - 2, SLOT), :]
        return pltpu.roll(jnp.where(lane < 96, near, far), 32, 1)

    def y_plus(ref, base, here):
        return pltpu.roll(jnp.where(lane >= 1, here, ref[pl.ds(base + 1, SLOT), :]), 127, 1)

    def y_minus(ref, base, here):
        return pltpu.roll(jnp.where(lane < 127, here, ref[pl.ds(base - 1, SLOT), :]), 1, 1)

    def at(p):
        return pl.multiple_of(p * SLOT, SLOT)

    tall = plain.shape[1]
    rows_in = kappa_ref.shape[0]
    for which, ref in enumerate((kappa_ref, absorb_ref, source_ref)):
        plane = ref[...]
        plain[which, pl.ds(0, rows_in), :] = plane
        plain[which, pl.ds(rows_in, tall - rows_in), :] = jnp.zeros((tall - rows_in, LANES), F32)
        half_lane[which, pl.ds(0, 8), :] = jnp.zeros((8, LANES), F32)
        half_lane[which, pl.ds(8, rows_in), :] = pltpu.roll(plane, 64, 1)
        half_lane[which, pl.ds(8 + rows_in, tall - rows_in - 8), :] = jnp.zeros((tall - rows_in - 8, LANES), F32)
        for m in range(8):
            send[2 * m, which] = jnp.where(
                lane < 64, half_lane[which, pl.ds(25 * m, SLOT), :], half_lane[which, pl.ds(25 * m + 1, SLOT), :]
            )
            send[2 * m + 1, which] = plain[which, pl.ds(25 * m + 5, SLOT), :]

    active = (lax.broadcasted_iota(jnp.int32, (1, PAIRS), 1) < count_ref[0]).astype(F32)
    pair_send[...] = jnp.concatenate(
        [pair_ref[...].astype(F32), measured_ref[0], measured_ref[1], active, jnp.zeros((4, PAIRS), F32)],
        axis=0,
    )

    def remote(src_ref, dst_ref, send_sem, recv_sem, dev):
        copy = pltpu.make_async_remote_copy(
            src_ref=src_ref, dst_ref=dst_ref, send_sem=send_sem, recv_sem=recv_sem,
            device_id=dev, device_id_type=MESH,
        )
        copy.start()
        return copy

    def arrived(ref, sem):
        pltpu.make_async_copy(ref, ref, sem).wait()

    strip = pl.ds(pl.multiple_of(8 * my_y, 8), 8)
    two = pl.ds(0, 2)
    pl.semaphore_wait(barrier, 16 + 7 + 8 + 8 + 3 + 8 - to_self)
    sent = []
    for spot, dev in enumerate(beyond):
        sent.append(remote(
            send.at[parity * 8 + spot, two, strip, :], coef_recv.at[:, slab, strip, :],
            o_send.at[spot], o_recv.at[my_spot], dev,
        ))
    for i, dev in enumerate(source_to):
        sent.append(remote(send.at[i, 2], source.at[slab], s_send.at[i], s_recv.at[slab], dev))
    close = []
    for j, dev in enumerate(near):
        close.append(remote(
            send.at[parity * 8 + dev[1] % 8, two], coef_recv.at[:, slab], k_send.at[j], k_recv.at[j], dev
        ))
    sent.append(remote(
        pair_send, pair_recv, p_send.at[0], p_recv.at[0],
        device(my_y, goal_z + slab // 8, slab % 8),
    ))

    guard = jnp.zeros((SLOT, LANES), F32)
    last = (SLABS + 1) * SLOT
    for start in (0, last):
        kappa[pl.ds(start, SLOT), :] = guard
        for c in range(2):
            direc_a[c, pl.ds(start, SLOT), :] = guard
            direc_b[c, pl.ds(start, SLOT), :] = guard
            for a in range(2):
                field[a, c, pl.ds(start, SLOT), :] = guard
    for a in range(2):
        coef_recv[a, slab] = send[group, a]

    cell = cell_ref[...]
    det_z = ((cell >> 10) * 1311) >> 15
    in_plane = cell - det_z * 25600
    det_x = ((in_plane >> 5) * 6554) >> 15
    det_y = in_plane - det_x * NY
    det_row = det_x - (OWN * group - HALO)
    in_window = (det_row >= 0) & (det_row < OWN + 2 * HALO)
    owned = ((det_row >= HALO) & (det_row < HALO + OWN)).astype(F32)
    spot = det_row * NY + det_y
    det_sub = jnp.where(in_window, det_z * SLOT + (spot >> 7), -1)
    det_lane = spot & 127

    @pl.loop(0, SLABS)
    def _(p):
        subs = lax.broadcasted_iota(jnp.int32, (SLOT, NDET), 0) + p * SLOT
        place[pl.ds(at(p), SLOT), :] = (subs == det_sub).astype(F32).astype(BF16)

    lane_hot[...] = (lax.broadcasted_iota(jnp.int32, (LANES, NDET), 0) == det_lane).astype(F32)
    for spot in range(8):
        arrived(coef_recv.at[:, other_half * 8 + spot, strip, :], o_recv.at[spot])
    eight = pl.ds(pl.multiple_of(other_half * 8, 8), 8)
    strips = coef_recv.at[:, eight, strip, :]
    across = [remote(strips, strips, g_send.at[j], g_recv.at[j], dev) for j, dev in enumerate(y_peers)]
    for copy in close:
        copy.wait()
    for p in range(SLABS):
        arrived(source.at[p], s_recv.at[p])
    for copy in across:
        copy.wait()

    first, keeps, pushes = chebyshev_terms()

    @pl.loop(0, SLABS, unroll=4)
    def _(p):
        kappa[pl.ds(at(p + 1), SLOT), :] = coef_recv[0, p]

    @pl.loop(0, SLABS, unroll=4)
    def _(p):
        base, here = at(p + 1), at(p)
        k = kappa[pl.ds(base, SLOT), :]
        diagonal = coef_recv[1, p]
        beside = (
            (x_plus(kappa, base), xp_in),
            (x_minus(kappa, base), xm_in),
            (y_plus(kappa, base, k) * yp_in, yp_in),
            (y_minus(kappa, base, k) * ym_in, ym_in),
            (kappa[pl.ds(base + SLOT, SLOT), :], jnp.where(p < SLABS - 1, 1.0, 0.0).astype(F32)),
            (kappa[pl.ds(base - SLOT, SLOT), :], jnp.where(p > 0, 1.0, 0.0).astype(F32)),
        )
        for which, (side, inside) in enumerate(beside):
            face = (k + side) * 0.5
            diagonal = diagonal + face
            coef[which, pl.ds(here, SLOT), :] = face * inside
        coef[6, pl.ds(here, SLOT), :] = diagonal
        b = source[p]
        resid[0, pl.ds(here, SLOT), :] = b
        resid[1, pl.ds(here, SLOT), :] = jnp.zeros_like(b)
        direc_a[0, pl.ds(base, SLOT), :] = b * first
        direc_a[1, pl.ds(base, SLOT), :] = jnp.zeros_like(b)
        field[0, 0, pl.ds(base, SLOT), :] = b * first
        field[0, 1, pl.ds(base, SLOT), :] = jnp.zeros_like(b)

    size = 2 * SLOT
    lane2 = lax.broadcasted_iota(jnp.int32, (size, LANES), 1)

    def solve(out):
        for sweep in range(SWEEPS - 1):
            keep, push = keeps[sweep], pushes[sweep]
            now, later = (direc_a, direc_b) if sweep % 2 == 0 else (direc_b, direc_a)

            @pl.loop(0, SLABS // 2, unroll=8)
            def _(q):
                here, base = pl.multiple_of(q * size, size), pl.multiple_of(q * size + SLOT, SLOT)
                cs = [coef[which, pl.ds(here, size), :] for which in range(7)]
                ds = [now[c, pl.ds(base, size), :] for c in range(2)]
                turned = (-ds[1], ds[0])
                for c in range(2):

                    def shifted(amount):
                        return now[c, pl.ds(base + amount, size), :]

                    up, down = shifted(1), shifted(-1)
                    off = (
                        cs[0] * pltpu.roll(jnp.where(lane2 >= 32, up, shifted(2)), 96, 1)
                        + cs[1] * pltpu.roll(jnp.where(lane2 < 96, down, shifted(-2)), 32, 1)
                        + cs[2] * pltpu.roll(jnp.where(lane2 >= 1, ds[c], up), 127, 1)
                        + cs[3] * pltpu.roll(jnp.where(lane2 < 127, ds[c], down), 1, 1)
                        + cs[4] * shifted(SLOT)
                        + cs[5] * shifted(-SLOT)
                    )
                    applied = cs[6] * ds[c] - off + frequency_shift * turned[c]
                    left = resid[c, pl.ds(here, size), :] - applied
                    resid[c, pl.ds(here, size), :] = left
                    new = keep * ds[c] + push * left
                    later[c, pl.ds(base, size), :] = new
                    field[out, c, pl.ds(base, size), :] = field[out, c, pl.ds(base, size), :] + new

    solve(0)

    whole = pl.ds(SLOT, SLABS * SLOT)
    for c in range(2):
        spread = dot_parts(parts_of(field[0, c, whole, :]), (place[...],), ((0,), (0,)))
        reads[group, pl.ds(c, 1), :] = jnp.sum(spread * lane_hot[...], axis=0, keepdims=True) * owned
    mine = reads.at[group]
    for j, dev in enumerate(near):
        sent.append(remote(mine, mine, r_send.at[j], r_recv.at[group], dev))
    for spot, dev in enumerate(twin):
        sent.append(remote(mine, mine, r_send.at[7 + spot], r_recv.at[group], dev))
    arrived(pair_recv, p_recv.at[0])
    pair_hot[...] = (
        lax.broadcasted_iota(jnp.int32, (NDET, PAIRS), 0).astype(F32) == pair_recv[0:1]
    ).astype(F32).astype(BF16)
    for j in range(1, SLABS):
        other = lax.rem(group + j, SLABS)
        arrived(reads.at[other], r_recv.at[other])
    readings = jnp.sum(reads[...], axis=0)
    wide = jnp.concatenate([readings, jnp.zeros((6, NDET), F32)], axis=0)
    model = dot_parts(parts_of(wide), (pair_hot[...],), ((1,), (0,)))
    active = pair_recv[3:4]
    conj = jnp.concatenate(
        [
            (model[0:1] - pair_recv[1:2]) * active,
            (pair_recv[2:3] - model[1:2]) * active,
            jnp.zeros((6, PAIRS), F32),
        ],
        axis=0,
    )
    weights = dot_parts(parts_of(conj), (pair_hot[...],), ((1,), (1,)))
    for c in range(2):
        hot = lane_hot[...]
        pieces = [(hot * part.astype(F32)).astype(BF16) for part in parts_of(weights[c : c + 1])]
        right = dot_parts((place[...],), pieces, ((1,), (1,)))
        resid[c] = right
        direc_a[c, whole, :] = right * first
        field[1, c, whole, :] = right * first

    solve(1)

    @pl.loop(0, SLABS, unroll=4)
    def _(p):
        base = at(p + 1)
        refs = [[field.at[a, c] for c in range(2)] for a in range(2)]
        here = [[refs[a][c][pl.ds(base, SLOT), :] for c in range(2)] for a in range(2)]
        sides = (
            x_plus,
            x_minus,
            lambda ref, b: y_plus(ref, b, ref[pl.ds(b, SLOT), :]) * yp_in,
            lambda ref, b: y_minus(ref, b, ref[pl.ds(b, SLOT), :]) * ym_in,
            lambda ref, b: ref[pl.ds(b + SLOT, SLOT), :],
            lambda ref, b: ref[pl.ds(b - SLOT, SLOT), :],
        )
        total = jnp.zeros((SLOT, LANES), F32)
        for side in sides:
            gap = [[here[a][c] - side(refs[a][c], base) for c in range(2)] for a in range(2)]
            total = total + gap[0][0] * gap[1][0] - gap[0][1] * gap[1][1]
        grads[p, 0] = here[0][1] * here[1][1] - here[0][0] * here[1][0]
        grads[p, 1] = -0.5 * total
        for out in range(2):
            low, high = grads[p, out, pl.ds(7, 16), :], grads[p, out, pl.ds(8, 16), :]
            ysend[p, out] = pltpu.roll(jnp.where(lane[0:16] >= 64, low, high), 64, 1)

    across = [
        remote(ysend.at[pl.ds((dev[0] // 8) * 4, 4)], yrecv.at[j], y_send.at[j], y_recv.at[j], dev)
        for j, dev in enumerate(y_peers)
    ]
    for copy in across:
        copy.wait()
    for t in range(4):
        for out in range(2):
            total = ysend[my_y * 4 + t, out] + yrecv[0, t, out] + yrecv[1, t, out] + yrecv[2, t, out]
            fsend[t, 0, out] = total[0:8]
            grads[t, out, pl.ds(0, 16), :] = total
            low, high = grads[t, out, pl.ds(6, 8), :], grads[t, out, pl.ds(7, 8), :]
            fsend[t, 1, out] = pltpu.roll(jnp.where(lane[0:8] >= 32, low, high), 96, 1)

    def final_copy(t, h):
        return pltpu.make_async_remote_copy(
            src_ref=fsend.at[t, h],
            dst_ref=frecv.at[my_z // 2],
            send_sem=f_send.at[2 * t + h],
            recv_sem=f_recv.at[my_z // 2],
            device_id=final_to[t][h],
            device_id_type=MESH,
        )

    for t in range(4):
        for h in range(2):
            mine = is_me(final_to[t][h])

            @pl.when(jnp.logical_not(mine))
            def _():
                final_copy(t, h).start()

            @pl.when(mine)
            def _():
                pltpu.make_async_copy(fsend.at[t, h], frecv.at[my_z // 2], f_recv.at[my_z // 2]).start()

    for m in range(8):
        pltpu.make_async_copy(frecv.at[m], frecv.at[m], f_recv.at[m]).wait()
    for out, out_ref in enumerate((out_abs_ref, out_dif_ref)):
        total = frecv[0, out]
        for m in range(1, 8):
            total = total + frecv[m, out]
        for k in range(6):
            out_ref[0:1, pl.ds(128 * k, 128)] = total[k : k + 1]
        out_ref[0:1, pl.ds(768, 32)] = total[6:7, 0:32]
    for t in range(4):
        for h in range(2):

            @pl.when(jnp.logical_not(is_me(final_to[t][h])))
            def _():
                final_copy(t, h).wait_send()

    for copy in sent:
        copy.wait_send()


def body(source_field, kappa, absorb, det_cell, pair_det, pair_count, measured):
    tall = 216
    vmem = pl.BlockSpec(memory_space=pltpu.VMEM)
    stacked = (SLABS + 2) * SLOT
    flat = SLABS * SLOT
    out = jax.ShapeDtypeStruct((1, 800), F32)
    dma = pltpu.SemaphoreType.DMA
    return pl.pallas_call(
        kernel,
        out_shape=(out, out),
        in_specs=[pl.BlockSpec(memory_space=pltpu.SMEM)] + [vmem] * 6,
        out_specs=(vmem, vmem),
        scratch_shapes=[
            pltpu.VMEM((3, tall, LANES), F32),
            pltpu.VMEM((3, tall, LANES), F32),
            pltpu.VMEM((SLABS, 3, SLOT, LANES), F32),
            pltpu.VMEM((2, SLABS, SLOT, LANES), F32),
            pltpu.VMEM((SLABS, SLOT, LANES), F32),
            pltpu.VMEM((stacked, LANES), F32),
            pltpu.VMEM((7, flat, LANES), F32),
            pltpu.VMEM((2, stacked, LANES), F32),
            pltpu.VMEM((2, stacked, LANES), F32),
            pltpu.VMEM((2, flat, LANES), F32),
            pltpu.VMEM((2, 2, stacked, LANES), F32),
            pltpu.VMEM((SLABS, 2, SLOT, LANES), F32),
            pltpu.VMEM((flat, NDET), BF16),
            pltpu.VMEM((LANES, NDET), F32),
            pltpu.VMEM((NDET, PAIRS), BF16),
            pltpu.VMEM((8, PAIRS), F32),
            pltpu.VMEM((8, PAIRS), F32),
            pltpu.VMEM((SLABS, 2, NDET), F32),
            pltpu.VMEM((SLABS, 2, 16, LANES), F32),
            pltpu.VMEM((3, 4, 2, 16, LANES), F32),
            pltpu.VMEM((4, 2, 2, 8, LANES), F32),
            pltpu.VMEM((8, 2, 8, LANES), F32),
            dma((16,)), dma((16,)), dma((7,)), dma((7,)), dma((8,)), dma((8,)),
            dma((3,)), dma((3,)), dma((1,)), dma((1,)),
            dma((15,)), dma((16,)), dma((3,)), dma((3,)), dma((8,)), dma((8,)),
        ],
        compiler_params=pltpu.CompilerParams(
            collective_id=0, has_side_effects=True, vmem_limit_bytes=40 * 1024 * 1024
        ),
    )(
        pair_count,
        source_field.reshape(200, LANES),
        kappa.reshape(200, LANES),
        absorb.reshape(200, LANES),
        det_cell.reshape(1, NDET),
        pair_det,
        measured,
    )


def solution(mesh):
    placed = (
        P("src", "slab", None),
        P("slab", None),
        P("slab", None),
        P(),
        P("src", None),
        P("src"),
        P(None, "src", None),
    )
    return jax.shard_map(
        body,
        mesh=mesh,
        in_specs=placed,
        out_specs=(P("slab", "src"), P("slab", "src")),
        check_vma=False,
    )
```

```python
import jax
import jax.numpy as jnp
from jax import lax
from jax.experimental import pallas as pl
from jax.experimental.pallas import tpu as pltpu
from jax.sharding import PartitionSpec as P

NY = 160
SWEEPS = 6
NDET = 512
PAIRS = 256
SLABS = 16
HALO = 6
OWN_ROWS = 20
OWN_PLANES = 8
PLANES = OWN_PLANES + HALO
SLOT = 40
LANES = 128
FLAT = PLANES * SLOT
STACKED = FLAT + 2 * SLOT
PLANE_ROWS = 200
TALL = 216
MESH = pl.DeviceIdType.MESH
F32 = jnp.float32
BF16 = jnp.bfloat16

spectrum_low = 0.02
spectrum_high = 25.0
frequency_shift = 0.3


def chebyshev_terms():
    theta = (spectrum_high + spectrum_low) / 2.0
    delta = (spectrum_high - spectrum_low) / 2.0
    sigma = theta / delta
    rho = 1.0 / sigma
    keeps = []
    pushes = []
    for sweep in range(SWEEPS - 1):
        rho_new = 1.0 / (2.0 * sigma - rho)
        keeps.append(rho_new * rho)
        pushes.append(2.0 * rho_new / delta)
        rho = rho_new
    return (1.0 / theta, keeps, pushes)


def parts_of(value):
    high = value.astype(BF16)
    rest = value - high.astype(F32)
    middle = rest.astype(BF16)
    low = (rest - middle.astype(F32)).astype(BF16)
    return (high, middle, low)


def dot_parts(lhs_parts, rhs_parts, dims):
    total = None
    for lhs in lhs_parts:
        for rhs in rhs_parts:
            term = lax.dot_general(lhs, rhs, (dims, ((), ())), preferred_element_type=F32)
            total = term if total is None else total + term
    return total


def slot_of(plane):
    return jnp.where(plane < OWN_PLANES, plane, SLABS - 1 - plane)


def kernel(
    count_ref, source_hbm, kappa_hbm, absorb_hbm, cell_hbm, pair_hbm, measured_hbm,
    out_abs_ref, out_dif_ref,
    planes, cell_ref, pair_ref, measured_ref,
    half_lane, send, coef_recv, source, kappa, coef, direc_a, direc_b, resid, field, grads,
    place, lane_hot, pair_hot, pair_send, pair_recv, reads, ysend, yrecv, fsend, frecv,
    i_sem, s_send, s_recv, k_send, k_recv, o_send, o_recv, g_send, g_recv, p_send, p_recv,
    t_send, t_recv, u_send, u_recv, r_send, r_recv, y_send, y_recv, f_send, f_recv,
):
    src = lax.axis_index("src")
    slab = lax.axis_index("slab")
    my_y = src // 8
    my_z = (slab // 8) * 8 + src % 8
    my_x = (slab % 8) // 2
    core = slab % 2
    upper = my_z // 8
    parity = my_z % 2
    pair_z = my_z - parity
    group = parity * 4 + my_x
    member = group * 2 + core
    solved = jnp.where((pair_z >= 4) & (pair_z <= 10), pair_z - 4, lax.rem(pair_z + 5, 16))
    own_zlo = src % 8
    goal_z = jnp.where(own_zlo % 2 == 0, own_zlo + 4, lax.rem(own_zlo + 11, 16))
    swap_z = jnp.where(own_zlo < 4, lax.rem(my_z + 12, 16), lax.rem(my_z + 4, 16))
    native = core == upper

    def device(y, z, x, c):
        return (y * 8 + lax.rem(z, 8), (z // 8) * 8 + x * 2 + c)

    def is_me(dev):
        return (dev[0] == src) & (dev[1] == slab)

    source_to = [device(my_y, goal_z + g // 4, g % 4, upper) for g in range(8)]
    source_from = [(my_y * 8 + solved, core * 8 + i) for i in range(8)]
    near = [device(my_y, my_z, lax.rem(slab % 8 + j, 8) // 2, lax.rem(slab % 8 + j, 8) % 2) for j in range(1, 8)]
    twin = [device(my_y, pair_z + 1 - parity, i // 2, i % 2) for i in range(8)]
    native_to = [device(my_y, my_z, x, upper) for x in range(4)]
    beyond_to = device(my_y, swap_z, lax.rem(my_x + 4 - my_y, 4), upper)
    beyond_from = [device(my_y, swap_z, lax.rem(my_x + my_y, 4), c) for c in range(2)]
    y_peers = [(lax.rem(my_y + j, 4) * 8 + own_zlo, slab) for j in range(1, 4)]
    other_core = (src, slab + 1 - 2 * core)

    def plane_of(slot, half):
        return jnp.where(half == 0, slot, SLABS - 1 - slot)

    final_to = [[(4 * group + h, plane_of(2 * my_y + t, core)) for h in range(4)] for t in range(2)]
    final_from = [
        device(slot_of(slab) // 2, 2 * m + src // 16, (src // 4) % 4, slab // 8) for m in range(8)
    ]

    barrier = pltpu.get_barrier_semaphore()
    to_self = jnp.int32(0)
    for dev in final_from:
        to_self = to_self + jnp.where(is_me(dev), 1, 0)

        @pl.when(jnp.logical_not(is_me(dev)))
        def _():
            pl.semaphore_signal(barrier, inc=1, device_id=dev, device_id_type=MESH)

    for dev in source_from + twin + y_peers + near:
        pl.semaphore_signal(barrier, inc=1, device_id=dev, device_id_type=MESH)

    @pl.when(jnp.logical_not(native))
    def _():
        for dev in beyond_from:
            pl.semaphore_signal(barrier, inc=1, device_id=dev, device_id_type=MESH)

    loads = [
        pltpu.make_async_copy(ref, dst, i_sem.at[n])
        for n, (ref, dst) in enumerate((
            (kappa_hbm, planes.at[0]), (absorb_hbm, planes.at[1]), (source_hbm, planes.at[2]),
            (cell_hbm, cell_ref), (pair_hbm, pair_ref), (measured_hbm, measured_ref),
        ))
    ]
    for load in loads:
        load.start()

    lane = lax.broadcasted_iota(jnp.int32, (SLOT, LANES), 1)
    flat = lax.broadcasted_iota(jnp.int32, (SLOT, LANES), 0) * LANES + lane
    row = ((flat >> 5) * 205) >> 10
    col = flat - row * NY
    first_row = OWN_ROWS * group - HALO
    real_row = row + first_row
    row_in = (real_row >= 0) & (real_row < 160)
    xp_in = (row_in & (real_row < 159)).astype(F32)
    xm_in = (row_in & (real_row > 0)).astype(F32)
    yp_in = (col < NY - 1).astype(F32)
    ym_in = (col > 0).astype(F32)

    def x_plus(ref, base):
        near_row, far_row = ref[pl.ds(base + 1, SLOT), :], ref[pl.ds(base + 2, SLOT), :]
        return pltpu.roll(jnp.where(lane >= 32, near_row, far_row), 96, 1)

    def x_minus(ref, base):
        near_row, far_row = ref[pl.ds(base - 1, SLOT), :], ref[pl.ds(base - 2, SLOT), :]
        return pltpu.roll(jnp.where(lane < 96, near_row, far_row), 32, 1)

    def y_plus(ref, base, here):
        return pltpu.roll(jnp.where(lane >= 1, here, ref[pl.ds(base + 1, SLOT), :]), 127, 1)

    def y_minus(ref, base, here):
        return pltpu.roll(jnp.where(lane < 127, here, ref[pl.ds(base - 1, SLOT), :]), 1, 1)

    def at(p):
        return pl.multiple_of(p * SLOT, 8)

    for load in loads:
        load.wait()
    for which in range(3):
        half_lane[which, pl.ds(0, 8), :] = jnp.zeros((8, LANES), F32)
        half_lane[which, pl.ds(8, PLANE_ROWS), :] = pltpu.roll(planes[which], 64, 1)
        half_lane[which, pl.ds(8 + PLANE_ROWS, 8), :] = jnp.zeros((8, LANES), F32)
        for g in range(8):
            send[g, which] = jnp.where(
                lane < 64, half_lane[which, pl.ds(25 * g, SLOT), :], half_lane[which, pl.ds(25 * g + 1, SLOT), :]
            )
    active = (lax.broadcasted_iota(jnp.int32, (1, PAIRS), 1) < count_ref[0]).astype(F32)
    pair_send[...] = jnp.concatenate(
        [pair_ref[...].astype(F32), measured_ref[0], measured_ref[1], active, jnp.zeros((4, PAIRS), F32)],
        axis=0,
    )

    def remote_copy(src_ref, dst_ref, send_sem, recv_sem, dev):
        return pltpu.make_async_remote_copy(
            src_ref=src_ref, dst_ref=dst_ref, send_sem=send_sem, recv_sem=recv_sem,
            device_id=dev, device_id_type=MESH,
        )

    def remote(*args):
        copy = remote_copy(*args)
        copy.start()
        return copy

    def arrived(ref, sem):
        pltpu.make_async_copy(ref, ref, sem).wait()

    two = pl.ds(0, 2)
    my_slot = slot_of(slab)
    pl.semaphore_wait(barrier, 8 + 8 + 3 + 7 + 1 + 8 - to_self)
    sent = [remote(
        send.at[parity * 4 + lax.rem(my_x + 4 - my_y, 4), two], coef_recv.at[:, my_slot],
        o_send.at[0], o_recv.at[core], beyond_to,
    )]
    for g, dev in enumerate(source_to):
        sent.append(remote(send.at[g, 2], source.at[my_slot], s_send.at[g], s_recv.at[my_slot], dev))

    def native_copy(x):
        return remote_copy(
            send.at[parity * 4 + x, two], coef_recv.at[:, my_slot], k_send.at[x], k_recv.at[my_slot], native_to[x]
        )

    for x in range(4):

        @pl.when(jnp.logical_not(is_me(native_to[x])))
        def _():
            native_copy(x).start()

    sent.append(remote(
        pair_send, pair_recv, p_send.at[0], p_recv.at[0],
        device(my_y, goal_z + (slab % 8) // 4, slab % 4, upper),
    ))

    guard = jnp.zeros((SLOT, LANES), F32)
    last = (PLANES + 1) * SLOT
    for start in (0, last):
        kappa[pl.ds(start, SLOT), :] = guard
        for c in range(2):
            direc_a[c, pl.ds(start, SLOT), :] = guard
            direc_b[c, pl.ds(start, SLOT), :] = guard
            for a in range(2):
                field[a, c, pl.ds(start, SLOT), :] = guard

    cell = cell_ref[...]
    det_z = ((cell >> 10) * 1311) >> 15
    in_plane = cell - det_z * 25600
    det_x = ((in_plane >> 5) * 6554) >> 15
    det_y = in_plane - det_x * NY
    det_row = det_x - first_row
    det_slot = plane_of(det_z, core)
    in_window = (det_row >= 0) & (det_row < OWN_ROWS + 2 * HALO) & (det_slot < PLANES)
    owned = (
        (det_row >= HALO) & (det_row < HALO + OWN_ROWS) & (det_slot < OWN_PLANES)
    ).astype(F32)
    spot = det_row * NY + det_y
    det_sub = jnp.where(in_window, det_slot * SLOT + (spot >> 7), -1)
    det_lane = spot & 127

    @pl.loop(0, FLAT // 16, unroll=5)
    def _(p):
        subs = lax.broadcasted_iota(jnp.int32, (16, NDET), 0) + p * 16
        place[pl.ds(pl.multiple_of(p * 16, 16), 16), :] = (subs == det_sub).astype(F32).astype(BF16)

    lane_hot[...] = (lax.broadcasted_iota(jnp.int32, (LANES, NDET), 0) == det_lane).astype(F32)

    def pass_on(slot, both):
        n = slot - 2
        if both:
            return remote_copy(
                coef_recv.at[:, slot], coef_recv.at[:, SLABS - 1 - slot], t_send.at[n], t_recv.at[n], other_core
            )
        return remote_copy(
            source.at[slot], source.at[SLABS - 1 - slot], u_send.at[n], u_recv.at[n], other_core
        )

    @pl.when(native)
    def _():
        coef_recv[:, my_slot] = send[group, 0:2]
        for j in range(1, 8):
            slot = lax.rem(my_slot + j, 8)
            arrived(coef_recv.at[:, slot], k_recv.at[slot])

    @pl.when(jnp.logical_not(native))
    def _():
        far_x = lax.rem(my_x + my_y, 4)
        low = jnp.where(core == 0, 2 * far_x, 6 - 2 * far_x)
        for c in range(2):
            slot = jnp.where(core == 0, 2 * far_x + c, 7 - 2 * far_x - c)
            arrived(coef_recv.at[:, slot], o_recv.at[c])
        strips = coef_recv.at[:, pl.ds(low, 2)]
        across = [remote(strips, strips, g_send.at[j], g_recv.at[j], dev) for j, dev in enumerate(y_peers)]
        for copy in across:
            copy.wait()

    for slot in range(2, 8):
        sent.append(pass_on(slot, True))
        sent[-1].start()
    for n in range(6):
        arrived(coef_recv.at[:, OWN_PLANES + 5 - n], t_recv.at[n])

    @pl.loop(0, PLANES, unroll=7)
    def _(p):
        kappa[pl.ds(at(p + 1), SLOT), :] = coef_recv[0, p]

    @pl.loop(0, PLANES, unroll=7)
    def _(p):
        base, here = at(p + 1), at(p)
        k = kappa[pl.ds(base, SLOT), :]
        diagonal = coef_recv[1, p]
        beside = (
            (x_plus(kappa, base), xp_in),
            (x_minus(kappa, base), xm_in),
            (y_plus(kappa, base, k) * yp_in, yp_in),
            (y_minus(kappa, base, k) * ym_in, ym_in),
            (kappa[pl.ds(base + SLOT, SLOT), :], jnp.where(p < PLANES - 1, 1.0, 0.0).astype(F32)),
            (kappa[pl.ds(base - SLOT, SLOT), :], jnp.where(p > 0, 1.0, 0.0).astype(F32)),
        )
        for which, (side, inside) in enumerate(beside):
            face = (k + side) * 0.5
            diagonal = diagonal + face
            coef[which, pl.ds(here, SLOT), :] = face * inside
        coef[6, pl.ds(here, SLOT), :] = diagonal

    for slot in range(8):
        arrived(source.at[slot], s_recv.at[slot])
        if slot >= 2:
            sent.append(pass_on(slot, False))
            sent[-1].start()
    for n in range(6):
        arrived(source.at[OWN_PLANES + 5 - n], u_recv.at[n])

    first, keeps, pushes = chebyshev_terms()

    @pl.loop(0, PLANES, unroll=7)
    def _(p):
        base, here = at(p + 1), at(p)
        b = source[p]
        nothing = jnp.zeros_like(b)
        resid[0, pl.ds(here, SLOT), :] = b
        resid[1, pl.ds(here, SLOT), :] = nothing
        direc_a[0, pl.ds(base, SLOT), :] = b * first
        direc_a[1, pl.ds(base, SLOT), :] = nothing
        field[0, 0, pl.ds(base, SLOT), :] = b * first
        field[0, 1, pl.ds(base, SLOT), :] = nothing

    def solve(out):
        for sweep in range(SWEEPS - 1):
            keep, push = keeps[sweep], pushes[sweep]
            now, later = (direc_a, direc_b) if sweep % 2 == 0 else (direc_b, direc_a)
            count = PLANES - 1 - sweep

            def one_plane(p, kept):
                here, base = at(p), at(p + 1)
                cs = [coef[which, pl.ds(here, SLOT), :] for which in range(7)]
                ds = [now[c, pl.ds(base, SLOT), :] for c in range(2)]
                turned = (-ds[1], ds[0])
                for c in range(2):

                    def shifted(amount):
                        return now[c, pl.ds(base + amount, SLOT), :]

                    up, down = shifted(1), shifted(-1)
                    off = (
                        cs[0] * pltpu.roll(jnp.where(lane >= 32, up, shifted(2)), 96, 1)
                        + cs[1] * pltpu.roll(jnp.where(lane < 96, down, shifted(-2)), 32, 1)
                        + cs[2] * pltpu.roll(jnp.where(lane >= 1, ds[c], up), 127, 1)
                        + cs[3] * pltpu.roll(jnp.where(lane < 127, ds[c], down), 1, 1)
                        + cs[4] * shifted(SLOT)
                        + cs[5] * shifted(-SLOT)
                    )
                    applied = cs[6] * ds[c] - off + frequency_shift * turned[c]
                    left = resid[c, pl.ds(here, SLOT), :] - applied
                    resid[c, pl.ds(here, SLOT), :] = left
                    new = keep * ds[c] + push * left
                    later[c, pl.ds(base, SLOT), :] = new
                    if kept:
                        field[out, c, pl.ds(base, SLOT), :] = field[out, c, pl.ds(base, SLOT), :] + new

            @pl.loop(0, OWN_PLANES + 1, unroll=OWN_PLANES + 1)
            def _(p):
                one_plane(p, True)

            if count > OWN_PLANES + 1:

                @pl.loop(OWN_PLANES + 1, count, unroll=count - OWN_PLANES - 1)
                def _(p):
                    one_plane(p, False)

    solve(0)

    whole = pl.ds(SLOT, FLAT)
    mine_rows = OWN_PLANES * SLOT
    for c in range(2):
        spread = dot_parts(
            parts_of(field[0, c, pl.ds(SLOT, mine_rows), :]), (place[pl.ds(0, mine_rows), :],), ((0,), (0,))
        )
        reads[member, pl.ds(c, 1), :] = jnp.sum(spread * lane_hot[...], axis=0, keepdims=True) * owned
    mine = reads.at[member]
    for i, dev in enumerate(twin + near):
        sent.append(remote(mine, mine, r_send.at[i], r_recv.at[member], dev))
    arrived(pair_recv, p_recv.at[0])
    pair_hot[...] = (
        lax.broadcasted_iota(jnp.int32, (NDET, PAIRS), 0).astype(F32) == pair_recv[0:1]
    ).astype(F32).astype(BF16)
    for j in range(1, SLABS):
        other = lax.rem(member + j, SLABS)
        arrived(reads.at[other], r_recv.at[other])
    readings = jnp.sum(reads[...], axis=0)
    wide = jnp.concatenate([readings, jnp.zeros((6, NDET), F32)], axis=0)
    model = dot_parts(parts_of(wide), (pair_hot[...],), ((1,), (0,)))
    active = pair_recv[3:4]
    conj = jnp.concatenate(
        [
            (model[0:1] - pair_recv[1:2]) * active,
            (pair_recv[2:3] - model[1:2]) * active,
            jnp.zeros((6, PAIRS), F32),
        ],
        axis=0,
    )
    weights = dot_parts(parts_of(conj), (pair_hot[...],), ((1,), (1,)))
    for c in range(2):
        hot = lane_hot[...]
        pieces = [(hot * part.astype(F32)).astype(BF16) for part in parts_of(weights[c : c + 1])]
        right = dot_parts((place[...],), pieces, ((1,), (1,)))
        resid[c] = right
        direc_a[c, whole, :] = right * first
        field[1, c, whole, :] = right * first

    solve(1)

    @pl.loop(0, OWN_PLANES, unroll=4)
    def _(p):
        base = at(p + 1)
        refs = [[field.at[a, c] for c in range(2)] for a in range(2)]
        here = [[refs[a][c][pl.ds(base, SLOT), :] for c in range(2)] for a in range(2)]
        sides = (
            x_plus,
            x_minus,
            lambda ref, b: y_plus(ref, b, ref[pl.ds(b, SLOT), :]) * yp_in,
            lambda ref, b: y_minus(ref, b, ref[pl.ds(b, SLOT), :]) * ym_in,
            lambda ref, b: ref[pl.ds(b + SLOT, SLOT), :],
            lambda ref, b: ref[pl.ds(b - SLOT, SLOT), :],
        )
        total = jnp.zeros((SLOT, LANES), F32)
        for side in sides:
            gap = [[here[a][c] - side(refs[a][c], base) for c in range(2)] for a in range(2)]
            total = total + gap[0][0] * gap[1][0] - gap[0][1] * gap[1][1]
        grads[p, 0] = here[0][1] * here[1][1] - here[0][0] * here[1][0]
        grads[p, 1] = -0.5 * total
        for out in range(2):
            low, high = grads[p, out, pl.ds(7, 32), :], grads[p, out, pl.ds(8, 32), :]
            ysend[p, out] = pltpu.roll(jnp.where(lane[0:32] >= 64, low, high), 64, 1)

    across = [
        remote(ysend.at[pl.ds((dev[0] // 8) * 2, 2)], yrecv.at[j], y_send.at[j], y_recv.at[j], dev)
        for j, dev in enumerate(y_peers)
    ]
    for copy in across:
        copy.wait()
    for t in range(2):
        for out in range(2):
            grads[t, out, pl.ds(0, 32), :] = (
                ysend[my_y * 2 + t, out] + yrecv[0, t, out] + yrecv[1, t, out] + yrecv[2, t, out]
            )
            for h in range(4):
                start = (25 * h) // 4
                low, high = grads[t, out, pl.ds(start, 8), :], grads[t, out, pl.ds(start + 1, 8), :]
                if h == 0:
                    fsend[t, h, out] = low
                else:
                    fsend[t, h, out] = pltpu.roll(jnp.where(lane[0:8] >= 32 * h, low, high), 128 - 32 * h, 1)

    def final_copy(t, h):
        return remote_copy(
            fsend.at[t, h], frecv.at[my_z // 2], f_send.at[4 * t + h], f_recv.at[my_z // 2], final_to[t][h]
        )

    for t in range(2):
        for h in range(4):
            own = is_me(final_to[t][h])

            @pl.when(jnp.logical_not(own))
            def _():
                final_copy(t, h).start()

            @pl.when(own)
            def _():
                pltpu.make_async_copy(fsend.at[t, h], frecv.at[my_z // 2], f_recv.at[my_z // 2]).start()

    for x in range(4):

        @pl.when(jnp.logical_not(is_me(native_to[x])))
        def _():
            native_copy(x).wait_send()

    for copy in sent:
        copy.wait_send()
    for m in range(8):
        arrived(frecv.at[m], f_recv.at[m])
    for out, out_ref in enumerate((out_abs_ref, out_dif_ref)):
        total = frecv[0, out]
        for m in range(1, 8):
            total = total + frecv[m, out]
        for k in range(6):
            out_ref[0:1, pl.ds(128 * k, 128)] = total[k : k + 1]
        out_ref[0:1, pl.ds(768, 32)] = total[6:7, 0:32]
    for t in range(2):
        for h in range(4):

            @pl.when(jnp.logical_not(is_me(final_to[t][h])))
            def _():
                final_copy(t, h).wait_send()


def body(source_field, kappa, absorb, det_cell, pair_det, pair_count, measured):
    vmem = pl.BlockSpec(memory_space=pltpu.VMEM)
    hbm = pl.BlockSpec(memory_space=pltpu.HBM)
    out = jax.ShapeDtypeStruct((1, 800), F32)
    dma = pltpu.SemaphoreType.DMA
    return pl.pallas_call(
        kernel,
        out_shape=(out, out),
        in_specs=[pl.BlockSpec(memory_space=pltpu.SMEM)] + [hbm] * 6,
        out_specs=(vmem, vmem),
        scratch_shapes=[
            pltpu.VMEM((3, PLANE_ROWS, LANES), F32),
            pltpu.VMEM((1, NDET), jnp.int32),
            pltpu.VMEM((1, PAIRS), jnp.int32),
            pltpu.VMEM((2, 1, PAIRS), F32),
            pltpu.VMEM((3, TALL, LANES), F32),
            pltpu.VMEM((8, 3, SLOT, LANES), F32),
            pltpu.VMEM((2, PLANES, SLOT, LANES), F32),
            pltpu.VMEM((PLANES, SLOT, LANES), F32),
            pltpu.VMEM((STACKED, LANES), F32),
            pltpu.VMEM((7, FLAT, LANES), F32),
            pltpu.VMEM((2, STACKED, LANES), F32),
            pltpu.VMEM((2, STACKED, LANES), F32),
            pltpu.VMEM((2, FLAT, LANES), F32),
            pltpu.VMEM((2, 2, STACKED, LANES), F32),
            pltpu.VMEM((OWN_PLANES, 2, SLOT, LANES), F32),
            pltpu.VMEM((FLAT, NDET), BF16),
            pltpu.VMEM((LANES, NDET), F32),
            pltpu.VMEM((NDET, PAIRS), BF16),
            pltpu.VMEM((8, PAIRS), F32),
            pltpu.VMEM((8, PAIRS), F32),
            pltpu.VMEM((SLABS, 2, NDET), F32),
            pltpu.VMEM((OWN_PLANES, 2, 32, LANES), F32),
            pltpu.VMEM((3, 2, 2, 32, LANES), F32),
            pltpu.VMEM((2, 4, 2, 8, LANES), F32),
            pltpu.VMEM((8, 2, 8, LANES), F32),
            dma((6,)), dma((8,)), dma((8,)), dma((4,)), dma((8,)), dma((1,)), dma((2,)),
            dma((3,)), dma((3,)), dma((1,)), dma((1,)),
            dma((6,)), dma((6,)), dma((6,)), dma((6,)),
            dma((15,)), dma((16,)), dma((3,)), dma((3,)), dma((8,)), dma((8,)),
        ],
        compiler_params=pltpu.CompilerParams(
            collective_id=0, has_side_effects=True, vmem_limit_bytes=60 * 1024 * 1024
        ),
    )(
        pair_count,
        source_field.reshape(PLANE_ROWS, LANES),
        kappa.reshape(PLANE_ROWS, LANES),
        absorb.reshape(PLANE_ROWS, LANES),
        det_cell.reshape(1, NDET),
        pair_det,
        measured,
    )


def solution(mesh):
    placed = (
        P("src", "slab", None),
        P("slab", None),
        P("slab", None),
        P(),
        P("src", None),
        P("src"),
        P(None, "src", None),
    )
    return jax.shard_map(
        body,
        mesh=mesh,
        in_specs=placed,
        out_specs=(P("slab", "src"), P("slab", "src")),
        check_vma=False,
    )
```

```python
import jax
import jax.numpy as jnp
from jax import lax
from jax.experimental import pallas as pl
from jax.experimental.pallas import tpu as pltpu
from jax.sharding import PartitionSpec as P

NY = 160
SWEEPS = 6
NDET = 512
PAIRS = 256
SLABS = 16
HALO = 6
OWN_ROWS = 20
OWN_PLANES = 8
PLANES = OWN_PLANES + HALO
SLOT = 40
LANES = 128
FLAT = PLANES * SLOT
STACKED = FLAT + 2 * SLOT
PLANE_ROWS = 200
TALL = 216
MESH = pl.DeviceIdType.MESH
F32 = jnp.float32
BF16 = jnp.bfloat16

spectrum_low = 0.02
spectrum_high = 25.0
frequency_shift = 0.3


def chebyshev_terms():
    theta = (spectrum_high + spectrum_low) / 2.0
    delta = (spectrum_high - spectrum_low) / 2.0
    sigma = theta / delta
    rho = 1.0 / sigma
    keeps = []
    pushes = []
    for sweep in range(SWEEPS - 1):
        rho_new = 1.0 / (2.0 * sigma - rho)
        keeps.append(rho_new * rho)
        pushes.append(2.0 * rho_new / delta)
        rho = rho_new
    return (1.0 / theta, keeps, pushes)


def parts_of(value):
    high = value.astype(BF16)
    rest = value - high.astype(F32)
    middle = rest.astype(BF16)
    low = (rest - middle.astype(F32)).astype(BF16)
    return (high, middle, low)


def dot_parts(lhs_parts, rhs_parts, dims):
    total = None
    for lhs in lhs_parts:
        for rhs in rhs_parts:
            term = lax.dot_general(lhs, rhs, (dims, ((), ())), preferred_element_type=F32)
            total = term if total is None else total + term
    return total


def slot_of(plane):
    return jnp.where(plane < OWN_PLANES, plane, SLABS - 1 - plane)


def kernel(
    count_hbm, source_hbm, kappa_hbm, absorb_hbm, cell_hbm, pair_hbm, measured_hbm,
    out_ref,
    planes, count_ref, cell_ref, pair_ref, measured_ref,
    half_lane, send, coef_recv, source, kappa, coef, direc_a, direc_b, resid, field, grads,
    place, lane_hot, pair_hot, pair_send, pair_recv, reads, ysend, yrecv, ysum, fsend, frecv,
    i_sem, s_send, s_recv, k_send, k_recv, o_send, o_recv, g_send, g_recv, p_send, p_recv,
    t_send, t_recv, u_send, u_recv, r_send, r_recv, y_send, y_recv, f_send, f_recv,
):
    src = lax.axis_index("src")
    slab = lax.axis_index("slab")
    my_y = src // 8
    my_z = (slab // 8) * 8 + src % 8
    my_x = (slab % 8) // 2
    core = slab % 2
    upper = my_z // 8
    parity = my_z % 2
    pair_z = my_z - parity
    group = my_x * 2 + parity
    member = group * 2 + core
    solved = jnp.where((pair_z >= 4) & (pair_z <= 10), pair_z - 4, lax.rem(pair_z + 5, 16))
    own_zlo = src % 8
    goal_z = jnp.where(own_zlo % 2 == 0, own_zlo + 4, lax.rem(own_zlo + 11, 16))
    swap_z = jnp.where(own_zlo < 4, lax.rem(my_z + 12, 16), lax.rem(my_z + 4, 16))
    native = core == upper

    def device(y, z, x, c):
        return (y * 8 + lax.rem(z, 8), (z // 8) * 8 + x * 2 + c)

    def is_me(dev):
        return (dev[0] == src) & (dev[1] == slab)

    source_to = [device(my_y, goal_z + g % 2, g // 2, upper) for g in range(8)]
    source_from = [(my_y * 8 + solved, core * 8 + i) for i in range(8)]
    near = [device(my_y, my_z, lax.rem(slab % 8 + j, 8) // 2, lax.rem(slab % 8 + j, 8) % 2) for j in range(1, 8)]
    twin = [device(my_y, pair_z + 1 - parity, i // 2, i % 2) for i in range(8)]
    native_to = [device(my_y, my_z, x, upper) for x in range(4)]
    beyond_to = device(my_y, swap_z, lax.rem(my_x + 4 - my_y, 4), upper)
    beyond_from = [device(my_y, swap_z, lax.rem(my_x + my_y, 4), c) for c in range(2)]
    y_peers = [(lax.rem(my_y + j, 4) * 8 + own_zlo, slab) for j in range(1, 4)]
    other_core = (src, slab + 1 - 2 * core)

    def plane_of(slot, half):
        return jnp.where(half == 0, slot, SLABS - 1 - slot)

    row_to = []
    for q in range(OWN_PLANES):
        p = plane_of(q, core) % 8
        row_to.append(device(my_x, my_z, p // 2, p % 2))
    row_from = [device(lax.rem(my_y + j, 4), my_z, my_y, c) for j in range(1, 4) for c in range(2)]
    final_to = [[device(my_y, 8 * c + 4 * parity + h, my_x, core) for h in range(4)] for c in range(2)]
    final_from = [device(my_y, 2 * m + own_zlo // 4, my_x, core) for m in range(8)]

    barrier = pltpu.get_barrier_semaphore()
    to_self = jnp.int32(0)
    for dev in final_from:
        to_self = to_self + jnp.where(is_me(dev), 1, 0)

        @pl.when(jnp.logical_not(is_me(dev)))
        def _():
            pl.semaphore_signal(barrier, inc=1, device_id=dev, device_id_type=MESH)

    for dev in source_from + twin + row_from + near:
        pl.semaphore_signal(barrier, inc=1, device_id=dev, device_id_type=MESH)

    @pl.when(jnp.logical_not(native))
    def _():
        for dev in beyond_from + y_peers:
            pl.semaphore_signal(barrier, inc=1, device_id=dev, device_id_type=MESH)

    loads = [
        pltpu.make_async_copy(ref, dst, i_sem.at[n])
        for n, (ref, dst) in enumerate((
            (kappa_hbm, planes.at[0]), (absorb_hbm, planes.at[1]), (source_hbm, planes.at[2]),
            (cell_hbm, cell_ref), (count_hbm, count_ref), (pair_hbm, pair_ref), (measured_hbm, measured_ref),
        ))
    ]
    for load in loads:
        load.start()

    lane = lax.broadcasted_iota(jnp.int32, (SLOT, LANES), 1)
    flat = lax.broadcasted_iota(jnp.int32, (SLOT, LANES), 0) * LANES + lane
    row = ((flat >> 5) * 205) >> 10
    col = flat - row * NY
    first_row = OWN_ROWS * group - HALO
    real_row = row + first_row
    row_in = (real_row >= 0) & (real_row < 160)
    xp_in = (row_in & (real_row < 159)).astype(F32)
    xm_in = (row_in & (real_row > 0)).astype(F32)
    yp_in = (col < NY - 1).astype(F32)
    ym_in = (col > 0).astype(F32)

    def x_plus(ref, base):
        near_row, far_row = ref[pl.ds(base + 1, SLOT), :], ref[pl.ds(base + 2, SLOT), :]
        return pltpu.roll(jnp.where(lane >= 32, near_row, far_row), 96, 1)

    def x_minus(ref, base):
        near_row, far_row = ref[pl.ds(base - 1, SLOT), :], ref[pl.ds(base - 2, SLOT), :]
        return pltpu.roll(jnp.where(lane < 96, near_row, far_row), 32, 1)

    def y_plus(ref, base, here):
        return pltpu.roll(jnp.where(lane >= 1, here, ref[pl.ds(base + 1, SLOT), :]), 127, 1)

    def y_minus(ref, base, here):
        return pltpu.roll(jnp.where(lane < 127, here, ref[pl.ds(base - 1, SLOT), :]), 1, 1)

    def at(p):
        return pl.multiple_of(p * SLOT, 8)

    for load in loads:
        load.wait()
    for which in range(3):
        half_lane[which, pl.ds(0, 8), :] = jnp.zeros((8, LANES), F32)
        half_lane[which, pl.ds(8, PLANE_ROWS), :] = pltpu.roll(planes[which], 64, 1)
        half_lane[which, pl.ds(8 + PLANE_ROWS, 8), :] = jnp.zeros((8, LANES), F32)
        for g in range(8):
            send[g, which] = jnp.where(
                lane < 64, half_lane[which, pl.ds(25 * g, SLOT), :], half_lane[which, pl.ds(25 * g + 1, SLOT), :]
            )
    active = (lax.broadcasted_iota(jnp.int32, (1, PAIRS), 1) < count_ref[0]).astype(F32)
    pair_send[...] = jnp.concatenate(
        [pair_ref[...].astype(F32), measured_ref[0], measured_ref[1], active, jnp.zeros((4, PAIRS), F32)],
        axis=0,
    )

    def remote_copy(src_ref, dst_ref, send_sem, recv_sem, dev):
        return pltpu.make_async_remote_copy(
            src_ref=src_ref, dst_ref=dst_ref, send_sem=send_sem, recv_sem=recv_sem,
            device_id=dev, device_id_type=MESH,
        )

    def remote(*args):
        copy = remote_copy(*args)
        copy.start()
        return copy

    def arrived(ref, sem):
        pltpu.make_async_copy(ref, ref, sem).wait()

    two = pl.ds(0, 2)
    my_slot = slot_of(slab)
    rows_leave = jnp.where(my_x == my_y, 0, 8)
    pl.semaphore_wait(barrier, 8 + 8 + 7 + 1 + 8 - to_self + rows_leave + jnp.where(native, 0, 3))
    sent = [remote(
        send.at[2 * lax.rem(my_x + 4 - my_y, 4) + parity, two], coef_recv.at[:, my_slot],
        o_send.at[0], o_recv.at[core], beyond_to,
    )]
    for g, dev in enumerate(source_to):
        sent.append(remote(send.at[g, 2], source.at[my_slot], s_send.at[g], s_recv.at[my_slot], dev))

    def native_copy(x):
        return remote_copy(
            send.at[2 * x + parity, two], coef_recv.at[:, my_slot], k_send.at[x], k_recv.at[my_slot], native_to[x]
        )

    for x in range(4):

        @pl.when(jnp.logical_not(is_me(native_to[x])))
        def _():
            native_copy(x).start()

    sent.append(remote(
        pair_send, pair_recv, p_send.at[0], p_recv.at[0],
        device(my_y, goal_z + slab % 2, (slab % 8) // 2, upper),
    ))

    guard = jnp.zeros((SLOT, LANES), F32)
    last = (PLANES + 1) * SLOT
    for start in (0, last):
        kappa[pl.ds(start, SLOT), :] = guard
        for c in range(2):
            direc_a[c, pl.ds(start, SLOT), :] = guard
            direc_b[c, pl.ds(start, SLOT), :] = guard
            for a in range(2):
                field[a, c, pl.ds(start, SLOT), :] = guard

    cell = cell_ref[...]
    det_z = ((cell >> 10) * 1311) >> 15
    in_plane = cell - det_z * 25600
    det_x = ((in_plane >> 5) * 6554) >> 15
    det_y = in_plane - det_x * NY
    det_row = det_x - first_row
    det_slot = plane_of(det_z, core)
    in_window = (det_row >= 0) & (det_row < OWN_ROWS + 2 * HALO) & (det_slot < PLANES)
    owned = (
        (det_row >= HALO) & (det_row < HALO + OWN_ROWS) & (det_slot < OWN_PLANES)
    ).astype(F32)
    spot = det_row * NY + det_y
    det_sub = jnp.where(in_window, det_slot * SLOT + (spot >> 7), -1)
    det_lane = spot & 127

    @pl.loop(0, FLAT // 16, unroll=5)
    def _(p):
        subs = lax.broadcasted_iota(jnp.int32, (16, NDET), 0) + p * 16
        place[pl.ds(pl.multiple_of(p * 16, 16), 16), :] = (subs == det_sub).astype(F32).astype(BF16)

    lane_hot[...] = (lax.broadcasted_iota(jnp.int32, (LANES, NDET), 0) == det_lane).astype(F32)

    def pass_on(slot, both):
        n = slot - 2
        if both:
            return remote_copy(
                coef_recv.at[:, slot], coef_recv.at[:, SLABS - 1 - slot], t_send.at[n], t_recv.at[n], other_core
            )
        return remote_copy(
            source.at[slot], source.at[SLABS - 1 - slot], u_send.at[n], u_recv.at[n], other_core
        )

    @pl.when(native)
    def _():
        coef_recv[:, my_slot] = send[group, 0:2]
        for j in range(1, 8):
            slot = lax.rem(my_slot + j, 8)
            arrived(coef_recv.at[:, slot], k_recv.at[slot])

    @pl.when(jnp.logical_not(native))
    def _():
        far_x = lax.rem(my_x + my_y, 4)
        low = jnp.where(core == 0, 2 * far_x, 6 - 2 * far_x)
        for c in range(2):
            slot = jnp.where(core == 0, 2 * far_x + c, 7 - 2 * far_x - c)
            arrived(coef_recv.at[:, slot], o_recv.at[c])
        strips = coef_recv.at[:, pl.ds(low, 2)]
        across = [remote(strips, strips, g_send.at[j], g_recv.at[j], dev) for j, dev in enumerate(y_peers)]
        for copy in across:
            copy.wait()

    for slot in range(2, 8):
        sent.append(pass_on(slot, True))
        sent[-1].start()
    for n in range(6):
        arrived(coef_recv.at[:, OWN_PLANES + 5 - n], t_recv.at[n])

    @pl.loop(0, PLANES, unroll=7)
    def _(p):
        kappa[pl.ds(at(p + 1), SLOT), :] = coef_recv[0, p]

    @pl.loop(0, PLANES, unroll=7)
    def _(p):
        base, here = at(p + 1), at(p)
        k = kappa[pl.ds(base, SLOT), :]
        diagonal = coef_recv[1, p]
        beside = (
            (x_plus(kappa, base), xp_in),
            (x_minus(kappa, base), xm_in),
            (y_plus(kappa, base, k) * yp_in, yp_in),
            (y_minus(kappa, base, k) * ym_in, ym_in),
            (kappa[pl.ds(base + SLOT, SLOT), :], jnp.where(p < PLANES - 1, 1.0, 0.0).astype(F32)),
            (kappa[pl.ds(base - SLOT, SLOT), :], jnp.where(p > 0, 1.0, 0.0).astype(F32)),
        )
        for which, (side, inside) in enumerate(beside):
            face = (k + side) * 0.5
            diagonal = diagonal + face
            coef[which, pl.ds(here, SLOT), :] = face * inside
        coef[6, pl.ds(here, SLOT), :] = diagonal

    for slot in range(8):
        arrived(source.at[slot], s_recv.at[slot])
        if slot >= 2:
            sent.append(pass_on(slot, False))
            sent[-1].start()
    for n in range(6):
        arrived(source.at[OWN_PLANES + 5 - n], u_recv.at[n])

    first, keeps, pushes = chebyshev_terms()

    @pl.loop(0, PLANES, unroll=7)
    def _(p):
        base, here = at(p + 1), at(p)
        b = source[p]
        nothing = jnp.zeros_like(b)
        resid[0, pl.ds(here, SLOT), :] = b
        resid[1, pl.ds(here, SLOT), :] = nothing
        direc_a[0, pl.ds(base, SLOT), :] = b * first
        direc_a[1, pl.ds(base, SLOT), :] = nothing
        field[0, 0, pl.ds(base, SLOT), :] = b * first
        field[0, 1, pl.ds(base, SLOT), :] = nothing

    def solve(out):
        for sweep in range(SWEEPS - 1):
            keep, push = keeps[sweep], pushes[sweep]
            now, later = (direc_a, direc_b) if sweep % 2 == 0 else (direc_b, direc_a)
            count = PLANES - 1 - sweep

            def one_plane(p, kept):
                here, base = at(p), at(p + 1)
                cs = [coef[which, pl.ds(here, SLOT), :] for which in range(7)]
                ds = [now[c, pl.ds(base, SLOT), :] for c in range(2)]
                turned = (-ds[1], ds[0])
                for c in range(2):

                    def shifted(amount):
                        return now[c, pl.ds(base + amount, SLOT), :]

                    up, down = shifted(1), shifted(-1)
                    off = (
                        cs[0] * pltpu.roll(jnp.where(lane >= 32, up, shifted(2)), 96, 1)
                        + cs[1] * pltpu.roll(jnp.where(lane < 96, down, shifted(-2)), 32, 1)
                        + cs[2] * pltpu.roll(jnp.where(lane >= 1, ds[c], up), 127, 1)
                        + cs[3] * pltpu.roll(jnp.where(lane < 127, ds[c], down), 1, 1)
                        + cs[4] * shifted(SLOT)
                        + cs[5] * shifted(-SLOT)
                    )
                    applied = cs[6] * ds[c] - off + frequency_shift * turned[c]
                    left = resid[c, pl.ds(here, SLOT), :] - applied
                    resid[c, pl.ds(here, SLOT), :] = left
                    new = keep * ds[c] + push * left
                    later[c, pl.ds(base, SLOT), :] = new
                    if kept:
                        field[out, c, pl.ds(base, SLOT), :] = field[out, c, pl.ds(base, SLOT), :] + new

            @pl.loop(0, OWN_PLANES + 1, unroll=OWN_PLANES + 1)
            def _(p):
                one_plane(p, True)

            if count > OWN_PLANES + 1:

                @pl.loop(OWN_PLANES + 1, count, unroll=count - OWN_PLANES - 1)
                def _(p):
                    one_plane(p, False)

    solve(0)

    whole = pl.ds(SLOT, FLAT)
    mine_rows = OWN_PLANES * SLOT
    for c in range(2):
        spread = dot_parts(
            parts_of(field[0, c, pl.ds(SLOT, mine_rows), :]), (place[pl.ds(0, mine_rows), :],), ((0,), (0,))
        )
        reads[member, pl.ds(c, 1), :] = jnp.sum(spread * lane_hot[...], axis=0, keepdims=True) * owned
    mine = reads.at[member]
    for i, dev in enumerate(twin + near):
        sent.append(remote(mine, mine, r_send.at[i], r_recv.at[member], dev))
    arrived(pair_recv, p_recv.at[0])
    pair_hot[...] = (
        lax.broadcasted_iota(jnp.int32, (NDET, PAIRS), 0).astype(F32) == pair_recv[0:1]
    ).astype(F32).astype(BF16)
    for j in range(1, SLABS):
        other = lax.rem(member + j, SLABS)
        arrived(reads.at[other], r_recv.at[other])
    readings = jnp.sum(reads[...], axis=0)
    wide = jnp.concatenate([readings, jnp.zeros((6, NDET), F32)], axis=0)
    model = dot_parts(parts_of(wide), (pair_hot[...],), ((1,), (0,)))
    active = pair_recv[3:4]
    conj = jnp.concatenate(
        [
            (model[0:1] - pair_recv[1:2]) * active,
            (pair_recv[2:3] - model[1:2]) * active,
            jnp.zeros((6, PAIRS), F32),
        ],
        axis=0,
    )
    weights = dot_parts(parts_of(conj), (pair_hot[...],), ((1,), (1,)))
    for c in range(2):
        hot = lane_hot[...]
        pieces = [(hot * part.astype(F32)).astype(BF16) for part in parts_of(weights[c : c + 1])]
        right = dot_parts((place[...],), pieces, ((1,), (1,)))
        resid[c] = right
        direc_a[c, whole, :] = right * first
        field[1, c, whole, :] = right * first

    solve(1)

    def row_copy(q):
        return remote_copy(
            ysend.at[q], yrecv.at[core, my_y], y_send.at[q], y_recv.at[core, my_y], row_to[q]
        )

    for q in range(OWN_PLANES):
        base = (q + 1) * SLOT
        refs = [[field.at[a, c] for c in range(2)] for a in range(2)]
        here = [[refs[a][c][pl.ds(base, SLOT), :] for c in range(2)] for a in range(2)]
        sides = (
            x_plus,
            x_minus,
            lambda ref, b: y_plus(ref, b, ref[pl.ds(b, SLOT), :]) * yp_in,
            lambda ref, b: y_minus(ref, b, ref[pl.ds(b, SLOT), :]) * ym_in,
            lambda ref, b: ref[pl.ds(b + SLOT, SLOT), :],
            lambda ref, b: ref[pl.ds(b - SLOT, SLOT), :],
        )
        total = jnp.zeros((SLOT, LANES), F32)
        for side in sides:
            gap = [[here[a][c] - side(refs[a][c], base) for c in range(2)] for a in range(2)]
            total = total + gap[0][0] * gap[1][0] - gap[0][1] * gap[1][1]
        grads[q, 0] = here[0][0] * here[1][0] - here[0][1] * here[1][1]
        grads[q, 1] = total
        for out in range(2):
            low, high = grads[q, out, pl.ds(7, 32), :], grads[q, out, pl.ds(8, 32), :]
            rows = pltpu.roll(jnp.where(lane[0:32] >= 64, low, high), 64, 1)
            ysend[q, pl.ds(25 * out, 25), :] = rows[0:25]
        ysend[q, pl.ds(50, 6), :] = jnp.zeros((6, LANES), F32)
        stays = is_me(row_to[q])

        @pl.when(jnp.logical_not(stays))
        def _():
            row_copy(q).start()

        @pl.when(stays)
        def _():
            pltpu.make_async_copy(ysend.at[q], yrecv.at[core, my_y], y_recv.at[core, my_y]).start()

    def final_copy(c, h):
        return remote_copy(
            fsend.at[c, h], frecv.at[my_z // 2], f_send.at[4 * c + h], f_recv.at[my_z // 2], final_to[c][h]
        )

    for c in range(2):
        for y in range(4):
            arrived(yrecv.at[c, y], y_recv.at[c, y])
        ysum[c] = (yrecv[c, 0] + yrecv[c, 1]) + (yrecv[c, 2] + yrecv[c, 3])
        for h in range(4):
            for out in range(2):
                start = 25 * out + (25 * h) // 4
                low, high = ysum[c, pl.ds(start, 8), :], ysum[c, pl.ds(start + 1, 8), :]
                if h == 0:
                    fsend[c, h, out] = low
                else:
                    fsend[c, h, out] = pltpu.roll(jnp.where(lane[0:8] >= 32 * h, low, high), 128 - 32 * h, 1)
            own = is_me(final_to[c][h])

            @pl.when(jnp.logical_not(own))
            def _():
                final_copy(c, h).start()

            @pl.when(own)
            def _():
                pltpu.make_async_copy(fsend.at[c, h], frecv.at[my_z // 2], f_recv.at[my_z // 2]).start()

    for x in range(4):

        @pl.when(jnp.logical_not(is_me(native_to[x])))
        def _():
            native_copy(x).wait_send()

    for q in range(OWN_PLANES):

        @pl.when(jnp.logical_not(is_me(row_to[q])))
        def _():
            row_copy(q).wait_send()

    for copy in sent:
        copy.wait_send()
    for m in range(8):
        arrived(frecv.at[m], f_recv.at[m])
    for out in range(2):
        total = frecv[0, out]
        for m in range(1, 8):
            total = total + frecv[m, out]
        for k in range(6):
            out_ref[out, 0:1, pl.ds(128 * k, 128)] = total[k : k + 1]
        out_ref[out, 0:1, pl.ds(768, 32)] = total[6:7, 0:32]
    for c in range(2):
        for h in range(4):

            @pl.when(jnp.logical_not(is_me(final_to[c][h])))
            def _():
                final_copy(c, h).wait_send()


def body(source_field, kappa, absorb, det_cell, pair_det, pair_count, measured):
    vmem = pl.BlockSpec(memory_space=pltpu.VMEM)
    hbm = pl.BlockSpec(memory_space=pltpu.HBM)
    out = jax.ShapeDtypeStruct((2, 1, 800), F32)
    dma = pltpu.SemaphoreType.DMA
    sums = pl.pallas_call(
        kernel,
        out_shape=out,
        in_specs=[hbm] * 7,
        out_specs=vmem,
        scratch_shapes=[
            pltpu.VMEM((3, PLANE_ROWS, LANES), F32),
            pltpu.SMEM((1,), jnp.int32),
            pltpu.VMEM((1, NDET), jnp.int32),
            pltpu.VMEM((1, PAIRS), jnp.int32),
            pltpu.VMEM((2, 1, PAIRS), F32),
            pltpu.VMEM((3, TALL, LANES), F32),
            pltpu.VMEM((8, 3, SLOT, LANES), F32),
            pltpu.VMEM((2, PLANES, SLOT, LANES), F32),
            pltpu.VMEM((PLANES, SLOT, LANES), F32),
            pltpu.VMEM((STACKED, LANES), F32),
            pltpu.VMEM((7, FLAT, LANES), F32),
            pltpu.VMEM((2, STACKED, LANES), F32),
            pltpu.VMEM((2, STACKED, LANES), F32),
            pltpu.VMEM((2, FLAT, LANES), F32),
            pltpu.VMEM((2, 2, STACKED, LANES), F32),
            pltpu.VMEM((OWN_PLANES, 2, SLOT, LANES), F32),
            pltpu.VMEM((FLAT, NDET), BF16),
            pltpu.VMEM((LANES, NDET), F32),
            pltpu.VMEM((NDET, PAIRS), BF16),
            pltpu.VMEM((8, PAIRS), F32),
            pltpu.VMEM((8, PAIRS), F32),
            pltpu.VMEM((SLABS, 2, NDET), F32),
            pltpu.VMEM((OWN_PLANES, 56, LANES), F32),
            pltpu.VMEM((2, 4, 56, LANES), F32),
            pltpu.VMEM((2, 56, LANES), F32),
            pltpu.VMEM((2, 4, 2, 8, LANES), F32),
            pltpu.VMEM((8, 2, 8, LANES), F32),
            dma((7,)), dma((8,)), dma((8,)), dma((4,)), dma((8,)), dma((1,)), dma((2,)),
            dma((3,)), dma((3,)), dma((1,)), dma((1,)),
            dma((6,)), dma((6,)), dma((6,)), dma((6,)),
            dma((15,)), dma((16,)), dma((8,)), dma((2, 4)), dma((8,)), dma((8,)),
        ],
        compiler_params=pltpu.CompilerParams(
            collective_id=0, has_side_effects=True, vmem_limit_bytes=60 * 1024 * 1024
        ),
    )(
        pair_count,
        source_field.reshape(PLANE_ROWS, LANES),
        kappa.reshape(PLANE_ROWS, LANES),
        absorb.reshape(PLANE_ROWS, LANES),
        det_cell.reshape(1, NDET),
        pair_det,
        measured,
    )
    return (-sums[0], -0.5 * sums[1])


def solution(mesh):
    placed = (
        P("src", "slab", None),
        P("slab", None),
        P("slab", None),
        P(),
        P("src", None),
        P("src"),
        P(None, "src", None),
    )
    return jax.shard_map(
        body,
        mesh=mesh,
        in_specs=placed,
        out_specs=(P("slab", "src"), P("slab", "src")),
        check_vma=False,
    )
```

```python
import jax
import jax.numpy as jnp
from jax import lax
from jax.experimental import pallas as pl
from jax.experimental.pallas import tpu as pltpu
from jax.sharding import PartitionSpec as P

NY = 160
SWEEPS = 6
NDET = 512
PAIRS = 256
SLABS = 16
HALO = 6
OWN_ROWS = 20
OWN_PLANES = 8
PLANES = OWN_PLANES + HALO
SLOT = 40
LANES = 128
FLAT = PLANES * SLOT
STACKED = FLAT + 2 * SLOT
PLANE_ROWS = 200
TALL = 216
MESH = pl.DeviceIdType.MESH
F32 = jnp.float32
BF16 = jnp.bfloat16

spectrum_low = 0.02
spectrum_high = 25.0
frequency_shift = 0.3


def chebyshev_terms():
    theta = (spectrum_high + spectrum_low) / 2.0
    delta = (spectrum_high - spectrum_low) / 2.0
    sigma = theta / delta
    rho = 1.0 / sigma
    keeps = []
    pushes = []
    for sweep in range(SWEEPS - 1):
        rho_new = 1.0 / (2.0 * sigma - rho)
        keeps.append(rho_new * rho)
        pushes.append(2.0 * rho_new / delta)
        rho = rho_new
    return (1.0 / theta, keeps, pushes)


def parts_of(value):
    high = value.astype(BF16)
    rest = value - high.astype(F32)
    middle = rest.astype(BF16)
    low = (rest - middle.astype(F32)).astype(BF16)
    return (high, middle, low)


def dot(lhs, rhs, dims):
    return lax.dot_general(lhs, rhs, (dims, ((), ())), preferred_element_type=F32)


def dot_rows(rows, table, dims):
    stack = jnp.concatenate([part.astype(F32) for part in parts_of(rows)], axis=0).astype(BF16)
    out = dot(stack, table, dims)
    return out[0:8] + (out[8:16] + out[16:24])


def slot_of(plane):
    return jnp.where(plane < OWN_PLANES, plane, SLABS - 1 - plane)


def kernel(
    count_hbm, source_hbm, kappa_hbm, absorb_hbm, cell_hbm, pair_hbm, measured_hbm,
    out_ref,
    planes, count_ref, cell_ref, pair_ref, measured_ref,
    half_lane, send, coef_recv, source, kappa, coef, direc_a, direc_b, resid, field, grads,
    place, lane_hot, pair_hot, pair_send, pair_recv, reads, ysend, yrecv, ysum, fsend, frecv,
    i_sem, s_send, s_recv, k_send, k_recv, o_send, o_recv, g_send, g_recv, p_send, p_recv,
    t_send, t_recv, u_send, u_recv, r_send, r_recv, y_send, y_recv, f_send, f_recv,
):
    src = lax.axis_index("src")
    slab = lax.axis_index("slab")
    my_y = src // 8
    my_z = (slab // 8) * 8 + src % 8
    my_x = (slab % 8) // 2
    core = slab % 2
    upper = my_z // 8
    parity = my_z % 2
    pair_z = my_z - parity
    group = my_x * 2 + parity
    member = group * 2 + core
    solved = jnp.where((pair_z >= 4) & (pair_z <= 10), pair_z - 4, lax.rem(pair_z + 5, 16))
    own_zlo = src % 8
    goal_z = jnp.where(own_zlo % 2 == 0, own_zlo + 4, lax.rem(own_zlo + 11, 16))
    swap_z = jnp.where(own_zlo < 4, lax.rem(my_z + 12, 16), lax.rem(my_z + 4, 16))
    my_spot = slab % 8
    native = core == upper

    def device(y, z, x, c):
        return (y * 8 + lax.rem(z, 8), (z // 8) * 8 + x * 2 + c)

    def is_me(dev):
        return (dev[0] == src) & (dev[1] == slab)

    source_groups = [lax.rem(my_spot + k, 8) for k in range(8)]
    source_from = [(my_y * 8 + solved, core * 8 + i) for i in range(8)]
    near = [device(my_y, my_z, lax.rem(slab % 8 + j, 8) // 2, lax.rem(slab % 8 + j, 8) % 2) for j in range(1, 8)]
    twin = []
    for i in range(8):
        spot = lax.rem(my_spot + i, 8)
        twin.append(device(my_y, pair_z + 1 - parity, spot // 2, spot % 2))
    native_x = [lax.rem(my_x + k, 4) for k in range(4)]
    native_to = [device(my_y, my_z, x, upper) for x in native_x]
    beyond_to = device(my_y, swap_z, lax.rem(my_x + 4 - my_y, 4), upper)
    beyond_from = [device(my_y, swap_z, lax.rem(my_x + my_y, 4), c) for c in range(2)]
    y_peers = [(lax.rem(my_y + j, 4) * 8 + own_zlo, slab) for j in range(1, 4)]
    other_core = (src, slab + 1 - 2 * core)

    def plane_of(slot, half):
        return jnp.where(half == 0, slot, SLABS - 1 - slot)

    row_slots = [lax.rem(2 * my_y + k, 8) for k in range(OWN_PLANES)]
    row_to = []
    for q in row_slots:
        p = plane_of(q, core) % 8
        row_to.append(device(my_x, my_z, p // 2, p % 2))
    row_from = [device(lax.rem(my_y + j, 4), my_z, my_y, c) for j in range(1, 4) for c in range(2)]
    final_h = [lax.rem(my_z // 2 + k, 4) for k in range(4)]
    final_to = [[device(my_y, 8 * c + 4 * parity + h, my_x, core) for h in final_h] for c in range(2)]
    final_from = [device(my_y, 2 * m + own_zlo // 4, my_x, core) for m in range(8)]

    barrier = pltpu.get_barrier_semaphore()
    to_self = jnp.int32(0)
    for dev in final_from:
        to_self = to_self + jnp.where(is_me(dev), 1, 0)

        @pl.when(jnp.logical_not(is_me(dev)))
        def _():
            pl.semaphore_signal(barrier, inc=1, device_id=dev, device_id_type=MESH)

    for dev in source_from:
        pl.semaphore_signal(barrier, inc=1, device_id=dev, device_id_type=MESH)

    @pl.when(jnp.logical_not(native))
    def _():
        for dev in beyond_from + y_peers:
            pl.semaphore_signal(barrier, inc=1, device_id=dev, device_id_type=MESH)

    for dev in row_from + twin + near:
        pl.semaphore_signal(barrier, inc=1, device_id=dev, device_id_type=MESH)

    loads = [
        pltpu.make_async_copy(ref, dst, i_sem.at[n])
        for n, (ref, dst) in enumerate((
            (kappa_hbm, planes.at[0]), (absorb_hbm, planes.at[1]), (source_hbm, planes.at[2]),
            (cell_hbm, cell_ref), (count_hbm, count_ref), (pair_hbm, pair_ref), (measured_hbm, measured_ref),
        ))
    ]
    for load in loads:
        load.start()

    lane = lax.broadcasted_iota(jnp.int32, (SLOT, LANES), 1)
    flat = lax.broadcasted_iota(jnp.int32, (SLOT, LANES), 0) * LANES + lane
    row = ((flat >> 5) * 205) >> 10
    col = flat - row * NY
    first_row = OWN_ROWS * group - HALO
    real_row = row + first_row
    row_in = (real_row >= 0) & (real_row < 160)
    xp_in = (row_in & (real_row < 159)).astype(F32)
    xm_in = (row_in & (real_row > 0)).astype(F32)
    yp_in = (col < NY - 1).astype(F32)
    ym_in = (col > 0).astype(F32)

    def x_plus(ref, base):
        near_row, far_row = ref[pl.ds(base + 1, SLOT), :], ref[pl.ds(base + 2, SLOT), :]
        return pltpu.roll(jnp.where(lane >= 32, near_row, far_row), 96, 1)

    def x_minus(ref, base):
        near_row, far_row = ref[pl.ds(base - 1, SLOT), :], ref[pl.ds(base - 2, SLOT), :]
        return pltpu.roll(jnp.where(lane < 96, near_row, far_row), 32, 1)

    def y_plus(ref, base, here):
        return pltpu.roll(jnp.where(lane >= 1, here, ref[pl.ds(base + 1, SLOT), :]), 127, 1)

    def y_minus(ref, base, here):
        return pltpu.roll(jnp.where(lane < 127, here, ref[pl.ds(base - 1, SLOT), :]), 1, 1)

    def at(p):
        return p * SLOT if isinstance(p, int) else pl.multiple_of(p * SLOT, 8)

    for load in loads:
        load.wait()
    for which in range(3):
        half_lane[which, pl.ds(0, 8), :] = jnp.zeros((8, LANES), F32)
        half_lane[which, pl.ds(8, PLANE_ROWS), :] = pltpu.roll(planes[which], 64, 1)
        half_lane[which, pl.ds(8 + PLANE_ROWS, 8), :] = jnp.zeros((8, LANES), F32)
        for g in range(8):
            send[g, which] = jnp.where(
                lane < 64, half_lane[which, pl.ds(25 * g, SLOT), :], half_lane[which, pl.ds(25 * g + 1, SLOT), :]
            )
    active = (lax.broadcasted_iota(jnp.int32, (1, PAIRS), 1) < count_ref[0]).astype(F32)
    pair_send[...] = jnp.concatenate(
        [pair_ref[...].astype(F32), measured_ref[0], measured_ref[1], active, jnp.zeros((4, PAIRS), F32)],
        axis=0,
    )

    def remote_copy(src_ref, dst_ref, send_sem, recv_sem, dev):
        return pltpu.make_async_remote_copy(
            src_ref=src_ref, dst_ref=dst_ref, send_sem=send_sem, recv_sem=recv_sem,
            device_id=dev, device_id_type=MESH,
        )

    def remote(*args):
        copy = remote_copy(*args)
        copy.start()
        return copy

    def arrived(ref, sem):
        pltpu.make_async_copy(ref, ref, sem).wait()

    def source_slot(slot):
        return source.at[pl.ds(at(slot + 1), SLOT), :]

    two = pl.ds(0, 2)
    my_slot = slot_of(slab)
    rows_leave = jnp.where(my_x == my_y, 0, 8)
    pl.semaphore_wait(barrier, 8 + 8 + 7 + 1 + 8 - to_self + rows_leave + jnp.where(native, 0, 3))
    sent = [remote(
        send.at[2 * lax.rem(my_x + 4 - my_y, 4) + parity, two], coef_recv.at[:, my_slot],
        o_send.at[0], o_recv.at[core], beyond_to,
    )]
    def native_copy(k):
        return remote_copy(
            send.at[2 * native_x[k] + parity, two], coef_recv.at[:, my_slot],
            k_send.at[k], k_recv.at[my_slot], native_to[k],
        )

    for k in range(4):

        @pl.when(jnp.logical_not(is_me(native_to[k])))
        def _():
            native_copy(k).start()

    for k, g in enumerate(source_groups):
        sent.append(remote(
            send.at[g, 2], source_slot(my_slot), s_send.at[k], s_recv.at[my_slot],
            device(my_y, goal_z + g % 2, g // 2, upper),
        ))
    sent.append(remote(
        pair_send, pair_recv, p_send.at[0], p_recv.at[0],
        device(my_y, goal_z + slab % 2, (slab % 8) // 2, upper),
    ))

    guard = jnp.zeros((SLOT, LANES), F32)
    last = (PLANES + 1) * SLOT
    for start in (0, last):
        kappa[pl.ds(start, SLOT), :] = guard
        source[pl.ds(start, SLOT), :] = guard
        for c in range(2):
            direc_a[c, pl.ds(start, SLOT), :] = guard
            direc_b[c, pl.ds(start, SLOT), :] = guard
            for a in range(2):
                field[a, c, pl.ds(start, SLOT), :] = guard

    cell = cell_ref[...]
    det_z = ((cell >> 10) * 1311) >> 15
    in_plane = cell - det_z * 25600
    det_x = ((in_plane >> 5) * 6554) >> 15
    det_y = in_plane - det_x * NY
    det_row = det_x - first_row
    det_slot = plane_of(det_z, core)
    in_window = (det_row >= 0) & (det_row < OWN_ROWS + 2 * HALO) & (det_slot < PLANES)
    owned = (
        (det_row >= HALO) & (det_row < HALO + OWN_ROWS) & (det_slot < OWN_PLANES)
    ).astype(F32)
    spot = det_row * NY + det_y
    det_sub = jnp.where(in_window, det_slot * SLOT + (spot >> 7), -1)
    det_lane = spot & 127

    @pl.loop(0, FLAT // 16, unroll=5)
    def _(p):
        subs = lax.broadcasted_iota(jnp.int32, (16, NDET), 0) + p * 16
        place[pl.ds(pl.multiple_of(p * 16, 16), 16), :] = (subs == det_sub).astype(F32).astype(BF16)

    lane_hot[...] = (lax.broadcasted_iota(jnp.int32, (LANES, NDET), 0) == det_lane).astype(F32)

    def coef_pass(slot):
        return remote_copy(
            coef_recv.at[:, slot], coef_recv.at[:, SLABS - 1 - slot],
            t_send.at[slot - 2], t_recv.at[slot - 2], other_core,
        )

    def coef_came(slot):
        @pl.when(slot >= 2)
        def _():
            coef_pass(slot).start()

    @pl.when(native)
    def _():
        coef_recv[:, my_slot] = send[group, 0:2]
        coef_came(my_slot)
        for j in range(1, 8):
            slot = lax.rem(my_slot + j, 8)
            arrived(coef_recv.at[:, slot], k_recv.at[slot])
            coef_came(slot)

    @pl.when(jnp.logical_not(native))
    def _():
        def first_slot(x):
            return jnp.where(core == 0, 2 * x, 6 - 2 * x)

        for c in range(2):
            slot = jnp.where(core == 0, 2 * lax.rem(my_x + my_y, 4) + c, 7 - 2 * lax.rem(my_x + my_y, 4) - c)
            arrived(coef_recv.at[:, slot], o_recv.at[c])
        slots = [pl.ds(first_slot(lax.rem(my_x + my_y + 4 - j, 4)), 2) for j in range(4)]
        strips = coef_recv.at[:, slots[0]]
        across = [remote(strips, strips, g_send.at[j], g_recv.at[j], dev) for j, dev in enumerate(y_peers)]
        for j in range(4):
            if j:
                arrived(coef_recv.at[:, slots[j]], g_recv.at[j - 1])
            low = first_slot(lax.rem(my_x + my_y + 4 - j, 4))
            for n in range(2):
                coef_came(low + n)
        for copy in across:
            copy.wait_send()

    for slot in range(8):
        arrived(source_slot(slot), s_recv.at[slot])
        if slot >= 2:
            sent.append(remote(
                source_slot(slot), source_slot(SLABS - 1 - slot), u_send.at[slot - 2], u_recv.at[slot - 2], other_core
            ))
    for n in range(6):
        arrived(coef_recv.at[:, OWN_PLANES + 5 - n], t_recv.at[n])

    @pl.loop(0, PLANES, unroll=7)
    def _(p):
        kappa[pl.ds(at(p + 1), SLOT), :] = coef_recv[0, p]

    @pl.loop(0, PLANES, unroll=7)
    def _(p):
        base, here = at(p + 1), at(p)
        k = kappa[pl.ds(base, SLOT), :]
        diagonal = coef_recv[1, p]
        beside = (
            (x_plus(kappa, base), xp_in),
            (x_minus(kappa, base), xm_in),
            (y_plus(kappa, base, k) * yp_in, yp_in),
            (y_minus(kappa, base, k) * ym_in, ym_in),
            (kappa[pl.ds(base + SLOT, SLOT), :], jnp.where(p < PLANES - 1, 1.0, 0.0).astype(F32)),
            (kappa[pl.ds(base - SLOT, SLOT), :], jnp.where(p > 0, 1.0, 0.0).astype(F32)),
        )
        for which, (side, inside) in enumerate(beside):
            face = (k + side) * 0.5
            diagonal = diagonal + face
            coef[which, pl.ds(here, SLOT), :] = face * inside
        coef[6, pl.ds(here, SLOT), :] = diagonal

    for n in range(6):
        arrived(source_slot(OWN_PLANES + 5 - n), u_recv.at[n])

    first, keeps, pushes = chebyshev_terms()

    def spread_of(ref, base, cs, here):
        up, down = ref[pl.ds(base + 1, SLOT), :], ref[pl.ds(base - 1, SLOT), :]
        up_far, down_far = ref[pl.ds(base + 2, SLOT), :], ref[pl.ds(base - 2, SLOT), :]
        return (
            cs[0] * pltpu.roll(jnp.where(lane >= 32, up, up_far), 96, 1)
            + cs[1] * pltpu.roll(jnp.where(lane < 96, down, down_far), 32, 1)
            + cs[2] * pltpu.roll(jnp.where(lane >= 1, here, up), 127, 1)
            + cs[3] * pltpu.roll(jnp.where(lane < 127, here, down), 1, 1)
            + cs[4] * ref[pl.ds(base + SLOT, SLOT), :]
            + cs[5] * ref[pl.ds(base - SLOT, SLOT), :]
        )

    def solve(out, rights):
        for sweep in range(SWEEPS - 1):
            keep, push = keeps[sweep], pushes[sweep]
            now, later = (direc_a, direc_b) if sweep % 2 == 0 else (direc_b, direc_a)
            count = PLANES - 1 - sweep

            def first_sweep(p, kept):
                here, base = at(p), at(p + 1)
                cs = [coef[which, pl.ds(here, SLOT), :] for which in range(7)]
                bs = [ref[pl.ds(base, SLOT), :] for ref in rights]
                for c in range(2):
                    if len(bs) == 1:
                        turned = 0.0 if c == 0 else bs[0]
                    else:
                        turned = -bs[1] if c == 0 else bs[0]
                    if c < len(bs):
                        off = spread_of(rights[c], base, cs, bs[c])
                        applied = cs[6] * bs[c] - off + frequency_shift * turned
                        left = bs[c] - first * applied
                        new = (keep * first) * bs[c] + push * left
                        start = first * bs[c]
                    else:
                        left = (-first * frequency_shift) * turned
                        new = push * left
                        start = 0.0
                    resid[c, pl.ds(here, SLOT), :] = left
                    later[c, pl.ds(base, SLOT), :] = new
                    if kept:
                        field[out, c, pl.ds(base, SLOT), :] = start + new

            def one_plane(p, kept):
                if sweep == 0:
                    first_sweep(p, kept)
                    return
                here, base = at(p), at(p + 1)
                cs = [coef[which, pl.ds(here, SLOT), :] for which in range(7)]
                ds = [now[c, pl.ds(base, SLOT), :] for c in range(2)]
                turned = (-ds[1], ds[0])
                for c in range(2):
                    off = spread_of(now.at[c], base, cs, ds[c])
                    applied = cs[6] * ds[c] - off + frequency_shift * turned[c]
                    left = resid[c, pl.ds(here, SLOT), :] - applied
                    new = keep * ds[c] + push * left
                    if sweep < SWEEPS - 2:
                        resid[c, pl.ds(here, SLOT), :] = left
                        later[c, pl.ds(base, SLOT), :] = new
                    if kept:
                        field[out, c, pl.ds(base, SLOT), :] = field[out, c, pl.ds(base, SLOT), :] + new

            @pl.loop(0, OWN_PLANES + 1, unroll=OWN_PLANES + 1)
            def _(p):
                one_plane(p, True)

            if count > OWN_PLANES + 1:

                @pl.loop(OWN_PLANES + 1, count, unroll=count - OWN_PLANES - 1)
                def _(p):
                    one_plane(p, False)

    solve(0, [source])

    whole = pl.ds(SLOT, FLAT)
    mine_rows = OWN_PLANES * SLOT
    mine_planes = pl.ds(SLOT, mine_rows)
    table = place[pl.ds(0, mine_rows), :]
    both = jnp.concatenate([field[0, 0, mine_planes, :], field[0, 1, mine_planes, :]], axis=1)
    high, middle, low = [dot(part, table, ((0,), (0,))) for part in parts_of(both)]
    found = high + (middle + low)
    for c in range(2):
        spread = found[LANES * c : LANES * (c + 1)] * lane_hot[...]
        reads[member, pl.ds(c, 1), :] = jnp.sum(spread, axis=0, keepdims=True) * owned
    mine = reads.at[member]
    for i, dev in enumerate(twin + near):
        sent.append(remote(mine, mine, r_send.at[i], r_recv.at[member], dev))
    arrived(pair_recv, p_recv.at[0])
    pair_hot[...] = (
        lax.broadcasted_iota(jnp.int32, (NDET, PAIRS), 0).astype(F32) == pair_recv[0:1]
    ).astype(F32).astype(BF16)
    for j in range(1, SLABS):
        other = lax.rem(member + j, SLABS)
        arrived(reads.at[other], r_recv.at[other])
    readings = jnp.sum(reads[...], axis=0)
    wide = jnp.concatenate([readings, jnp.zeros((6, NDET), F32)], axis=0)
    model = dot_rows(wide, pair_hot[...], ((1,), (0,)))
    active = pair_recv[3:4]
    conj = jnp.concatenate(
        [
            (model[0:1] - pair_recv[1:2]) * active,
            (pair_recv[2:3] - model[1:2]) * active,
            jnp.zeros((6, PAIRS), F32),
        ],
        axis=0,
    )
    weights = dot_rows(conj, pair_hot[...], ((1,), (1,)))
    hot = lane_hot[...]
    right = None
    for part in parts_of(weights):
        part = part.astype(F32)
        piece = jnp.concatenate([hot * part[0:1], hot * part[1:2]], axis=0).astype(BF16)
        term = dot(place[...], piece, ((1,), (1,)))
        right = term if right is None else right + term
    for c in range(2):
        direc_a[c, whole, :] = right[:, LANES * c : LANES * (c + 1)]

    solve(1, [direc_a.at[0], direc_a.at[1]])

    def row_copy(k):
        return remote_copy(
            ysend.at[k], yrecv.at[core, my_y], y_send.at[k], y_recv.at[core, my_y], row_to[k]
        )

    for k, q in enumerate(row_slots):
        base = at(q + 1)
        refs = [[field.at[a, c] for c in range(2)] for a in range(2)]
        here = [[refs[a][c][pl.ds(base, SLOT), :] for c in range(2)] for a in range(2)]
        sides = (
            x_plus,
            x_minus,
            lambda ref, b: y_plus(ref, b, ref[pl.ds(b, SLOT), :]) * yp_in,
            lambda ref, b: y_minus(ref, b, ref[pl.ds(b, SLOT), :]) * ym_in,
            lambda ref, b: ref[pl.ds(b + SLOT, SLOT), :],
            lambda ref, b: ref[pl.ds(b - SLOT, SLOT), :],
        )
        total = jnp.zeros((SLOT, LANES), F32)
        for side in sides:
            gap = [[here[a][c] - side(refs[a][c], base) for c in range(2)] for a in range(2)]
            total = total + gap[0][0] * gap[1][0] - gap[0][1] * gap[1][1]
        grads[k, 0] = here[0][0] * here[1][0] - here[0][1] * here[1][1]
        grads[k, 1] = total
        for out in range(2):
            low, high = grads[k, out, pl.ds(7, 32), :], grads[k, out, pl.ds(8, 32), :]
            rows = pltpu.roll(jnp.where(lane[0:32] >= 64, low, high), 64, 1)
            ysend[k, pl.ds(25 * out, 25), :] = rows[0:25]
        ysend[k, pl.ds(50, 6), :] = jnp.zeros((6, LANES), F32)
        stays = is_me(row_to[k])

        @pl.when(jnp.logical_not(stays))
        def _():
            row_copy(k).start()

        @pl.when(stays)
        def _():
            pltpu.make_async_copy(ysend.at[k], yrecv.at[core, my_y], y_recv.at[core, my_y]).start()

    def final_copy(c, k):
        return remote_copy(
            fsend.at[c, final_h[k]], frecv.at[my_z // 2], f_send.at[4 * c + k], f_recv.at[my_z // 2], final_to[c][k]
        )

    for c in range(2):
        for y in range(4):
            arrived(yrecv.at[c, y], y_recv.at[c, y])
        ysum[c] = (yrecv[c, 0] + yrecv[c, 1]) + (yrecv[c, 2] + yrecv[c, 3])
        for h in range(4):
            for out in range(2):
                start = 25 * out + (25 * h) // 4
                low, high = ysum[c, pl.ds(start, 8), :], ysum[c, pl.ds(start + 1, 8), :]
                if h == 0:
                    fsend[c, h, out] = low
                else:
                    fsend[c, h, out] = pltpu.roll(jnp.where(lane[0:8] >= 32 * h, low, high), 128 - 32 * h, 1)
        for k in range(4):
            own = is_me(final_to[c][k])

            @pl.when(jnp.logical_not(own))
            def _():
                final_copy(c, k).start()

            @pl.when(own)
            def _():
                pltpu.make_async_copy(fsend.at[c, final_h[k]], frecv.at[my_z // 2], f_recv.at[my_z // 2]).start()

    for k in range(4):

        @pl.when(jnp.logical_not(is_me(native_to[k])))
        def _():
            native_copy(k).wait_send()

    for k in range(OWN_PLANES):

        @pl.when(jnp.logical_not(is_me(row_to[k])))
        def _():
            row_copy(k).wait_send()

    for slot in range(2, 8):
        coef_pass(slot).wait_send()
    for copy in sent:
        copy.wait_send()
    for m in range(8):
        arrived(frecv.at[m], f_recv.at[m])
    for out in range(2):
        total = frecv[0, out]
        for m in range(1, 8):
            total = total + frecv[m, out]
        for k in range(6):
            out_ref[out, 0:1, pl.ds(128 * k, 128)] = total[k : k + 1]
        out_ref[out, 0:1, pl.ds(768, 32)] = total[6:7, 0:32]
    for c in range(2):
        for k in range(4):

            @pl.when(jnp.logical_not(is_me(final_to[c][k])))
            def _():
                final_copy(c, k).wait_send()


def body(source_field, kappa, absorb, det_cell, pair_det, pair_count, measured):
    vmem = pl.BlockSpec(memory_space=pltpu.VMEM)
    hbm = pl.BlockSpec(memory_space=pltpu.HBM)
    out = jax.ShapeDtypeStruct((2, 1, 800), F32)
    dma = pltpu.SemaphoreType.DMA
    sums = pl.pallas_call(
        kernel,
        out_shape=out,
        in_specs=[hbm] * 7,
        out_specs=vmem,
        scratch_shapes=[
            pltpu.VMEM((3, PLANE_ROWS, LANES), F32),
            pltpu.SMEM((1,), jnp.int32),
            pltpu.VMEM((1, NDET), jnp.int32),
            pltpu.VMEM((1, PAIRS), jnp.int32),
            pltpu.VMEM((2, 1, PAIRS), F32),
            pltpu.VMEM((3, TALL, LANES), F32),
            pltpu.VMEM((8, 3, SLOT, LANES), F32),
            pltpu.VMEM((2, PLANES, SLOT, LANES), F32),
            pltpu.VMEM((STACKED, LANES), F32),
            pltpu.VMEM((STACKED, LANES), F32),
            pltpu.VMEM((7, FLAT, LANES), F32),
            pltpu.VMEM((2, STACKED, LANES), F32),
            pltpu.VMEM((2, STACKED, LANES), F32),
            pltpu.VMEM((2, FLAT, LANES), F32),
            pltpu.VMEM((2, 2, STACKED, LANES), F32),
            pltpu.VMEM((OWN_PLANES, 2, SLOT, LANES), F32),
            pltpu.VMEM((FLAT, NDET), BF16),
            pltpu.VMEM((LANES, NDET), F32),
            pltpu.VMEM((NDET, PAIRS), BF16),
            pltpu.VMEM((8, PAIRS), F32),
            pltpu.VMEM((8, PAIRS), F32),
            pltpu.VMEM((SLABS, 2, NDET), F32),
            pltpu.VMEM((OWN_PLANES, 56, LANES), F32),
            pltpu.VMEM((2, 4, 56, LANES), F32),
            pltpu.VMEM((2, 56, LANES), F32),
            pltpu.VMEM((2, 4, 2, 8, LANES), F32),
            pltpu.VMEM((8, 2, 8, LANES), F32),
            dma((7,)), dma((8,)), dma((8,)), dma((4,)), dma((8,)), dma((1,)), dma((2,)),
            dma((3,)), dma((3,)), dma((1,)), dma((1,)),
            dma((6,)), dma((6,)), dma((6,)), dma((6,)),
            dma((15,)), dma((16,)), dma((8,)), dma((2, 4)), dma((8,)), dma((8,)),
        ],
        compiler_params=pltpu.CompilerParams(
            collective_id=0, has_side_effects=True, vmem_limit_bytes=60 * 1024 * 1024
        ),
    )(
        pair_count,
        source_field.reshape(PLANE_ROWS, LANES),
        kappa.reshape(PLANE_ROWS, LANES),
        absorb.reshape(PLANE_ROWS, LANES),
        det_cell.reshape(1, NDET),
        pair_det,
        measured,
    )
    return (-sums[0], -0.5 * sums[1])


def solution(mesh):
    placed = (
        P("src", "slab", None),
        P("slab", None),
        P("slab", None),
        P(),
        P("src", None),
        P("src"),
        P(None, "src", None),
    )
    return jax.shard_map(
        body,
        mesh=mesh,
        in_specs=placed,
        out_specs=(P("slab", "src"), P("slab", "src")),
        check_vma=False,
    )
```

```python
import jax
import jax.numpy as jnp
from jax import lax
from jax.experimental import pallas as pl
from jax.experimental.pallas import tpu as pltpu
from jax.sharding import PartitionSpec as P

NY = 160
SWEEPS = 6
NDET = 512
PAIRS = 256
SLABS = 16
HALO = 6
OWN_ROWS = 20
OWN_PLANES = 8
PLANES = OWN_PLANES + HALO
SLOT = 40
LANES = 128
FLAT = PLANES * SLOT
STACKED = FLAT + 2 * SLOT
PLANE_ROWS = 200
TALL = 216
MESH = pl.DeviceIdType.MESH
F32 = jnp.float32
BF16 = jnp.bfloat16

spectrum_low = 0.02
spectrum_high = 25.0
frequency_shift = 0.3


def chebyshev_terms():
    theta = (spectrum_high + spectrum_low) / 2.0
    delta = (spectrum_high - spectrum_low) / 2.0
    sigma = theta / delta
    rho = 1.0 / sigma
    keeps = []
    pushes = []
    for sweep in range(SWEEPS - 1):
        rho_new = 1.0 / (2.0 * sigma - rho)
        keeps.append(rho_new * rho)
        pushes.append(2.0 * rho_new / delta)
        rho = rho_new
    return (1.0 / theta, keeps, pushes)


def parts_of(value):
    high = value.astype(BF16)
    rest = value - high.astype(F32)
    middle = rest.astype(BF16)
    low = (rest - middle.astype(F32)).astype(BF16)
    return (high, middle, low)


def dot(lhs, rhs, dims):
    return lax.dot_general(lhs, rhs, (dims, ((), ())), preferred_element_type=F32)


def dot_rows(rows, table, dims):
    stack = jnp.concatenate([part.astype(F32) for part in parts_of(rows)], axis=0).astype(BF16)
    out = dot(stack, table, dims)
    return out[0:8] + (out[8:16] + out[16:24])


def slot_of(plane):
    return jnp.where(plane < OWN_PLANES, plane, SLABS - 1 - plane)


def kernel(
    count_hbm, source_hbm, kappa_hbm, absorb_hbm, cell_hbm, pair_hbm, measured_hbm,
    out_ref,
    planes, count_ref, cell_ref, pair_ref, measured_ref,
    half_lane, send, coef_recv, source, kappa, coef, direc_a, direc_b, resid, field, grads,
    place, lane_hot, pair_hot, pair_send, pair_recv, reads, ysend, yrecv, ysum, fsend, frecv,
    i_sem, s_send, s_recv, k_send, k_recv, o_send, o_recv, g_send, g_recv, p_send, p_recv,
    t_send, t_recv, u_send, u_recv, r_send, r_recv, y_send, y_recv, f_send, f_recv,
):
    src = lax.axis_index("src")
    slab = lax.axis_index("slab")
    my_y = src // 8
    my_z = (slab // 8) * 8 + src % 8
    my_x = (slab % 8) // 2
    core = slab % 2
    upper = my_z // 8
    odd = my_z % 2
    pair_z = my_z - odd
    parity = jnp.where(upper == 0, odd, 1 - odd)
    group = my_x * 2 + parity
    member = group * 2 + core
    solved = jnp.where((pair_z >= 4) & (pair_z <= 10), pair_z - 4, lax.rem(pair_z + 5, 16))
    own_zlo = src % 8
    goal_z = jnp.where(own_zlo % 2 == 0, own_zlo + 4, lax.rem(own_zlo + 11, 16))
    def goal_of(half):
        return goal_z + jnp.where(goal_z < 8, half, 1 - half)

    swap_z = jnp.where(own_zlo < 4, lax.rem(my_z + 12, 16), lax.rem(my_z + 4, 16))
    native = core == upper

    def device(y, z, x, c):
        return (y * 8 + lax.rem(z, 8), (z // 8) * 8 + x * 2 + c)

    def is_me(dev):
        return (dev[0] == src) & (dev[1] == slab)

    far_x = [lax.rem(my_x + step, 4) for step in (2, 1, 3, 0)]
    far_spots = [(x, c) for x in far_x for c in range(2)]
    source_groups = [2 * x + c for x, c in far_spots]
    source_from = [(my_y * 8 + solved, core * 8 + i) for i in range(8)]
    near = [device(my_y, my_z, x, c) for x, c in far_spots[:6]] + [device(my_y, my_z, my_x, 1 - core)]
    twin = [device(my_y, pair_z + 1 - odd, x, c) for x, c in far_spots]
    native_x = far_x
    native_to = [device(my_y, my_z, x, upper) for x in native_x]
    beyond_to = device(my_y, swap_z, lax.rem(my_x + 4 - my_y, 4), upper)
    beyond_from = [device(my_y, swap_z, lax.rem(my_x + my_y, 4), c) for c in range(2)]
    y_peers = [(lax.rem(my_y + j, 4) * 8 + own_zlo, slab) for j in range(1, 4)]
    other_core = (src, slab + 1 - 2 * core)

    def plane_of(slot, half):
        return jnp.where(half == 0, slot, SLABS - 1 - slot)

    row_slots = [jnp.where(core == 0, 2 * x + c, 7 - 2 * x - c) for x, c in far_spots]
    row_to = []
    for q in row_slots:
        p = plane_of(q, core) % 8
        row_to.append(device(my_x, my_z, p // 2, p % 2))
    row_from = [device(lax.rem(my_y + j, 4), my_z, my_y, c) for j in range(1, 4) for c in range(2)]
    final_h = list(range(4))
    final_to = [[device(my_y, 8 * c + 4 * parity + h, my_x, core) for h in final_h] for c in range(2)]
    final_half = own_zlo // 4
    final_from = [
        device(my_y, 2 * m + (final_half if m < 4 else 1 - final_half), my_x, core) for m in range(8)
    ]

    barrier = pltpu.get_barrier_semaphore()
    to_self = jnp.int32(0)
    for dev in final_from:
        to_self = to_self + jnp.where(is_me(dev), 1, 0)

        @pl.when(jnp.logical_not(is_me(dev)))
        def _():
            pl.semaphore_signal(barrier, inc=1, device_id=dev, device_id_type=MESH)

    for dev in source_from:
        pl.semaphore_signal(barrier, inc=1, device_id=dev, device_id_type=MESH)

    @pl.when(jnp.logical_not(native))
    def _():
        for dev in beyond_from + y_peers:
            pl.semaphore_signal(barrier, inc=1, device_id=dev, device_id_type=MESH)

    for dev in row_from + twin + near:
        pl.semaphore_signal(barrier, inc=1, device_id=dev, device_id_type=MESH)

    loads = [
        pltpu.make_async_copy(ref, dst, i_sem.at[n])
        for n, (ref, dst) in enumerate((
            (kappa_hbm, planes.at[0]), (absorb_hbm, planes.at[1]), (source_hbm, planes.at[2]),
            (cell_hbm, cell_ref), (count_hbm, count_ref), (pair_hbm, pair_ref), (measured_hbm, measured_ref),
        ))
    ]
    for load in loads:
        load.start()

    lane = lax.broadcasted_iota(jnp.int32, (SLOT, LANES), 1)
    flat = lax.broadcasted_iota(jnp.int32, (SLOT, LANES), 0) * LANES + lane
    row = ((flat >> 5) * 205) >> 10
    col = flat - row * NY
    first_row = OWN_ROWS * group - HALO
    real_row = row + first_row
    row_in = (real_row >= 0) & (real_row < 160)
    xp_in = (row_in & (real_row < 159)).astype(F32)
    xm_in = (row_in & (real_row > 0)).astype(F32)
    yp_in = (col < NY - 1).astype(F32)
    ym_in = (col > 0).astype(F32)

    def x_plus(ref, base):
        near_row, far_row = ref[pl.ds(base + 1, SLOT), :], ref[pl.ds(base + 2, SLOT), :]
        return pltpu.roll(jnp.where(lane >= 32, near_row, far_row), 96, 1)

    def x_minus(ref, base):
        near_row, far_row = ref[pl.ds(base - 1, SLOT), :], ref[pl.ds(base - 2, SLOT), :]
        return pltpu.roll(jnp.where(lane < 96, near_row, far_row), 32, 1)

    def y_plus(ref, base, here):
        return pltpu.roll(jnp.where(lane >= 1, here, ref[pl.ds(base + 1, SLOT), :]), 127, 1)

    def y_minus(ref, base, here):
        return pltpu.roll(jnp.where(lane < 127, here, ref[pl.ds(base - 1, SLOT), :]), 1, 1)

    def at(p):
        return p * SLOT if isinstance(p, int) else pl.multiple_of(p * SLOT, 8)

    for load in loads:
        load.wait()
    for which in range(3):
        half_lane[which, pl.ds(0, 8), :] = jnp.zeros((8, LANES), F32)
        half_lane[which, pl.ds(8, PLANE_ROWS), :] = pltpu.roll(planes[which], 64, 1)
        half_lane[which, pl.ds(8 + PLANE_ROWS, 8), :] = jnp.zeros((8, LANES), F32)
        for g in range(8):
            send[g, which] = jnp.where(
                lane < 64, half_lane[which, pl.ds(25 * g, SLOT), :], half_lane[which, pl.ds(25 * g + 1, SLOT), :]
            )
    active = (lax.broadcasted_iota(jnp.int32, (1, PAIRS), 1) < count_ref[0]).astype(F32)
    pair_send[...] = jnp.concatenate(
        [pair_ref[...].astype(F32), measured_ref[0], measured_ref[1], active, jnp.zeros((4, PAIRS), F32)],
        axis=0,
    )

    def remote_copy(src_ref, dst_ref, send_sem, recv_sem, dev):
        return pltpu.make_async_remote_copy(
            src_ref=src_ref, dst_ref=dst_ref, send_sem=send_sem, recv_sem=recv_sem,
            device_id=dev, device_id_type=MESH,
        )

    def remote(*args):
        copy = remote_copy(*args)
        copy.start()
        return copy

    def arrived(ref, sem):
        pltpu.make_async_copy(ref, ref, sem).wait()

    def source_slot(slot):
        return source.at[pl.ds(at(slot + 1), SLOT), :]

    two = pl.ds(0, 2)
    my_slot = slot_of(slab)
    rows_leave = jnp.where(my_x == my_y, 0, 8)
    pl.semaphore_wait(barrier, 8 + 8 + 7 + 1 + 8 - to_self + rows_leave + jnp.where(native, 0, 3))
    sent = [remote(
        send.at[2 * lax.rem(my_x + 4 - my_y, 4) + 1 - parity, two], coef_recv.at[:, my_slot],
        o_send.at[0], o_recv.at[core], beyond_to,
    )]
    def native_copy(k):
        return remote_copy(
            send.at[2 * native_x[k] + parity, two], coef_recv.at[:, my_slot],
            k_send.at[k], k_recv.at[my_slot], native_to[k],
        )

    for k in range(4):

        @pl.when(jnp.logical_not(is_me(native_to[k])))
        def _():
            native_copy(k).start()

    for k, g in enumerate(source_groups):
        sent.append(remote(
            send.at[g, 2], source_slot(my_slot), s_send.at[k], s_recv.at[my_slot],
            device(my_y, goal_of(g % 2), g // 2, upper),
        ))
    sent.append(remote(
        pair_send, pair_recv, p_send.at[0], p_recv.at[0],
        device(my_y, goal_of(slab % 2), (slab % 8) // 2, upper),
    ))

    guard = jnp.zeros((SLOT, LANES), F32)
    last = (PLANES + 1) * SLOT
    for start in (0, last):
        kappa[pl.ds(start, SLOT), :] = guard
        source[pl.ds(start, SLOT), :] = guard
        for c in range(2):
            direc_a[c, pl.ds(start, SLOT), :] = guard
            direc_b[c, pl.ds(start, SLOT), :] = guard
            for a in range(2):
                field[a, c, pl.ds(start, SLOT), :] = guard

    cell = cell_ref[...]
    det_z = ((cell >> 10) * 1311) >> 15
    in_plane = cell - det_z * 25600
    det_x = ((in_plane >> 5) * 6554) >> 15
    det_y = in_plane - det_x * NY
    det_row = det_x - first_row
    det_slot = plane_of(det_z, core)
    in_window = (det_row >= 0) & (det_row < OWN_ROWS + 2 * HALO) & (det_slot < PLANES)
    owned = (
        (det_row >= HALO) & (det_row < HALO + OWN_ROWS) & (det_slot < OWN_PLANES)
    ).astype(F32)
    spot = det_row * NY + det_y
    det_sub = jnp.where(in_window, det_slot * SLOT + (spot >> 7), -1)
    det_lane = spot & 127

    @pl.loop(0, FLAT // 16, unroll=5)
    def _(p):
        subs = lax.broadcasted_iota(jnp.int32, (16, NDET), 0) + p * 16
        place[pl.ds(pl.multiple_of(p * 16, 16), 16), :] = (subs == det_sub).astype(F32).astype(BF16)

    lane_hot[...] = (lax.broadcasted_iota(jnp.int32, (LANES, NDET), 0) == det_lane).astype(F32)

    def coef_pass(slot):
        return remote_copy(
            coef_recv.at[:, slot], coef_recv.at[:, SLABS - 1 - slot],
            t_send.at[slot - 2], t_recv.at[slot - 2], other_core,
        )

    def coef_came(slot):
        @pl.when(slot >= 2)
        def _():
            coef_pass(slot).start()

    @pl.when(native)
    def _():
        coef_recv[:, my_slot] = send[group, 0:2]
        coef_came(my_slot)
        for j in range(1, 8):
            slot = lax.rem(my_slot + j, 8)
            arrived(coef_recv.at[:, slot], k_recv.at[slot])
            coef_came(slot)

    @pl.when(jnp.logical_not(native))
    def _():
        def first_slot(x):
            return jnp.where(core == 0, 2 * x, 6 - 2 * x)

        for c in range(2):
            slot = jnp.where(core == 0, 2 * lax.rem(my_x + my_y, 4) + c, 7 - 2 * lax.rem(my_x + my_y, 4) - c)
            arrived(coef_recv.at[:, slot], o_recv.at[c])
        slots = [pl.ds(first_slot(lax.rem(my_x + my_y + 4 - j, 4)), 2) for j in range(4)]
        strips = coef_recv.at[:, slots[0]]
        across = [remote(strips, strips, g_send.at[j], g_recv.at[j], dev) for j, dev in enumerate(y_peers)]
        for j in range(4):
            if j:
                arrived(coef_recv.at[:, slots[j]], g_recv.at[j - 1])
            low = first_slot(lax.rem(my_x + my_y + 4 - j, 4))
            for n in range(2):
                coef_came(low + n)
        for copy in across:
            copy.wait_send()

    for slot in range(8):
        arrived(source_slot(slot), s_recv.at[slot])
        if slot >= 2:
            sent.append(remote(
                source_slot(slot), source_slot(SLABS - 1 - slot), u_send.at[slot - 2], u_recv.at[slot - 2], other_core
            ))
    for n in range(6):
        arrived(coef_recv.at[:, OWN_PLANES + 5 - n], t_recv.at[n])

    @pl.loop(0, PLANES, unroll=7)
    def _(p):
        kappa[pl.ds(at(p + 1), SLOT), :] = coef_recv[0, p]

    @pl.loop(0, PLANES, unroll=7)
    def _(p):
        base, here = at(p + 1), at(p)
        k = kappa[pl.ds(base, SLOT), :]
        diagonal = coef_recv[1, p]
        beside = (
            (x_plus(kappa, base), xp_in),
            (x_minus(kappa, base), xm_in),
            (y_plus(kappa, base, k) * yp_in, yp_in),
            (y_minus(kappa, base, k) * ym_in, ym_in),
            (kappa[pl.ds(base + SLOT, SLOT), :], jnp.where(p < PLANES - 1, 1.0, 0.0).astype(F32)),
            (kappa[pl.ds(base - SLOT, SLOT), :], jnp.where(p > 0, 1.0, 0.0).astype(F32)),
        )
        for which, (side, inside) in enumerate(beside):
            face = (k + side) * 0.5
            diagonal = diagonal + face
            coef[which, pl.ds(here, SLOT), :] = face * inside
        coef[6, pl.ds(here, SLOT), :] = diagonal

    for n in range(6):
        arrived(source_slot(OWN_PLANES + 5 - n), u_recv.at[n])

    first, keeps, pushes = chebyshev_terms()

    def spread_of(ref, base, cs, here):
        up, down = ref[pl.ds(base + 1, SLOT), :], ref[pl.ds(base - 1, SLOT), :]
        up_far, down_far = ref[pl.ds(base + 2, SLOT), :], ref[pl.ds(base - 2, SLOT), :]
        return (
            cs[0] * pltpu.roll(jnp.where(lane >= 32, up, up_far), 96, 1)
            + cs[1] * pltpu.roll(jnp.where(lane < 96, down, down_far), 32, 1)
            + cs[2] * pltpu.roll(jnp.where(lane >= 1, here, up), 127, 1)
            + cs[3] * pltpu.roll(jnp.where(lane < 127, here, down), 1, 1)
            + cs[4] * ref[pl.ds(base + SLOT, SLOT), :]
            + cs[5] * ref[pl.ds(base - SLOT, SLOT), :]
        )

    def solve(out, rights):
        for sweep in range(SWEEPS - 1):
            keep, push = keeps[sweep], pushes[sweep]
            now, later = (direc_a, direc_b) if sweep % 2 == 0 else (direc_b, direc_a)
            count = PLANES - 1 - sweep

            def first_sweep(p, kept):
                here, base = at(p), at(p + 1)
                cs = [coef[which, pl.ds(here, SLOT), :] for which in range(7)]
                bs = [ref[pl.ds(base, SLOT), :] for ref in rights]
                for c in range(2):
                    if len(bs) == 1:
                        turned = 0.0 if c == 0 else bs[0]
                    else:
                        turned = -bs[1] if c == 0 else bs[0]
                    if c < len(bs):
                        off = spread_of(rights[c], base, cs, bs[c])
                        applied = cs[6] * bs[c] - off + frequency_shift * turned
                        left = bs[c] - first * applied
                        new = (keep * first) * bs[c] + push * left
                        start = first * bs[c]
                    else:
                        left = (-first * frequency_shift) * turned
                        new = push * left
                        start = 0.0
                    resid[c, pl.ds(here, SLOT), :] = left
                    later[c, pl.ds(base, SLOT), :] = new
                    if kept:
                        field[out, c, pl.ds(base, SLOT), :] = start + new

            def one_plane(p, kept):
                if sweep == 0:
                    first_sweep(p, kept)
                    return
                here, base = at(p), at(p + 1)
                cs = [coef[which, pl.ds(here, SLOT), :] for which in range(7)]
                ds = [now[c, pl.ds(base, SLOT), :] for c in range(2)]
                turned = (-ds[1], ds[0])
                for c in range(2):
                    off = spread_of(now.at[c], base, cs, ds[c])
                    applied = cs[6] * ds[c] - off + frequency_shift * turned[c]
                    left = resid[c, pl.ds(here, SLOT), :] - applied
                    new = keep * ds[c] + push * left
                    if sweep < SWEEPS - 2:
                        resid[c, pl.ds(here, SLOT), :] = left
                        later[c, pl.ds(base, SLOT), :] = new
                    if kept:
                        field[out, c, pl.ds(base, SLOT), :] = field[out, c, pl.ds(base, SLOT), :] + new

            @pl.loop(0, OWN_PLANES + 1, unroll=OWN_PLANES + 1)
            def _(p):
                one_plane(p, True)

            if count > OWN_PLANES + 1:

                @pl.loop(OWN_PLANES + 1, count, unroll=count - OWN_PLANES - 1)
                def _(p):
                    one_plane(p, False)

    solve(0, [source])

    whole = pl.ds(SLOT, FLAT)
    mine_rows = OWN_PLANES * SLOT
    mine_planes = pl.ds(SLOT, mine_rows)
    table = place[pl.ds(0, mine_rows), :]
    both = jnp.concatenate([field[0, 0, mine_planes, :], field[0, 1, mine_planes, :]], axis=1)
    high, middle, low = [dot(part, table, ((0,), (0,))) for part in parts_of(both)]
    found = high + (middle + low)
    for c in range(2):
        spread = found[LANES * c : LANES * (c + 1)] * lane_hot[...]
        reads[member, pl.ds(c, 1), :] = jnp.sum(spread, axis=0, keepdims=True) * owned
    mine = reads.at[member]
    for i, dev in enumerate(twin + near):
        sent.append(remote(mine, mine, r_send.at[i], r_recv.at[member], dev))
    arrived(pair_recv, p_recv.at[0])
    pair_hot[...] = (
        lax.broadcasted_iota(jnp.int32, (NDET, PAIRS), 0).astype(F32) == pair_recv[0:1]
    ).astype(F32).astype(BF16)
    for j in range(1, SLABS):
        other = lax.rem(member + j, SLABS)
        arrived(reads.at[other], r_recv.at[other])
    readings = jnp.sum(reads[...], axis=0)
    wide = jnp.concatenate([readings, jnp.zeros((6, NDET), F32)], axis=0)
    model = dot_rows(wide, pair_hot[...], ((1,), (0,)))
    active = pair_recv[3:4]
    conj = jnp.concatenate(
        [
            (model[0:1] - pair_recv[1:2]) * active,
            (pair_recv[2:3] - model[1:2]) * active,
            jnp.zeros((6, PAIRS), F32),
        ],
        axis=0,
    )
    weights = dot_rows(conj, pair_hot[...], ((1,), (1,)))
    hot = lane_hot[...]
    right = None
    for part in parts_of(weights):
        part = part.astype(F32)
        piece = jnp.concatenate([hot * part[0:1], hot * part[1:2]], axis=0).astype(BF16)
        term = dot(place[...], piece, ((1,), (1,)))
        right = term if right is None else right + term
    for c in range(2):
        direc_a[c, whole, :] = right[:, LANES * c : LANES * (c + 1)]

    solve(1, [direc_a.at[0], direc_a.at[1]])

    def row_copy(k):
        return remote_copy(
            ysend.at[k], yrecv.at[core, my_y], y_send.at[k], y_recv.at[core, my_y], row_to[k]
        )

    for k, q in enumerate(row_slots):
        base = at(q + 1)
        refs = [[field.at[a, c] for c in range(2)] for a in range(2)]
        here = [[refs[a][c][pl.ds(base, SLOT), :] for c in range(2)] for a in range(2)]
        sides = (
            x_plus,
            x_minus,
            lambda ref, b: y_plus(ref, b, ref[pl.ds(b, SLOT), :]) * yp_in,
            lambda ref, b: y_minus(ref, b, ref[pl.ds(b, SLOT), :]) * ym_in,
            lambda ref, b: ref[pl.ds(b + SLOT, SLOT), :],
            lambda ref, b: ref[pl.ds(b - SLOT, SLOT), :],
        )
        total = jnp.zeros((SLOT, LANES), F32)
        for side in sides:
            gap = [[here[a][c] - side(refs[a][c], base) for c in range(2)] for a in range(2)]
            total = total + gap[0][0] * gap[1][0] - gap[0][1] * gap[1][1]
        grads[k, 0] = here[0][0] * here[1][0] - here[0][1] * here[1][1]
        grads[k, 1] = total
        for out in range(2):
            low, high = grads[k, out, pl.ds(7, 32), :], grads[k, out, pl.ds(8, 32), :]
            rows = pltpu.roll(jnp.where(lane[0:32] >= 64, low, high), 64, 1)
            ysend[k, pl.ds(25 * out, 25), :] = rows[0:25]
        ysend[k, pl.ds(50, 6), :] = jnp.zeros((6, LANES), F32)
        stays = is_me(row_to[k])

        @pl.when(jnp.logical_not(stays))
        def _():
            row_copy(k).start()

        @pl.when(stays)
        def _():
            pltpu.make_async_copy(ysend.at[k], yrecv.at[core, my_y], y_recv.at[core, my_y]).start()

    def final_copy(c, k):
        return remote_copy(
            fsend.at[c, final_h[k]], frecv.at[my_z // 2], f_send.at[4 * c + k], f_recv.at[my_z // 2], final_to[c][k]
        )

    for c in range(2):
        for y in range(4):
            arrived(yrecv.at[c, y], y_recv.at[c, y])
        ysum[c] = (yrecv[c, 0] + yrecv[c, 1]) + (yrecv[c, 2] + yrecv[c, 3])
        for h in range(4):
            for out in range(2):
                start = 25 * out + (25 * h) // 4
                low, high = ysum[c, pl.ds(start, 8), :], ysum[c, pl.ds(start + 1, 8), :]
                if h == 0:
                    fsend[c, h, out] = low
                else:
                    fsend[c, h, out] = pltpu.roll(jnp.where(lane[0:8] >= 32 * h, low, high), 128 - 32 * h, 1)
        for k in range(4):
            own = is_me(final_to[c][k])

            @pl.when(jnp.logical_not(own))
            def _():
                final_copy(c, k).start()

            @pl.when(own)
            def _():
                pltpu.make_async_copy(fsend.at[c, final_h[k]], frecv.at[my_z // 2], f_recv.at[my_z // 2]).start()

    for k in range(4):

        @pl.when(jnp.logical_not(is_me(native_to[k])))
        def _():
            native_copy(k).wait_send()

    for k in range(OWN_PLANES):

        @pl.when(jnp.logical_not(is_me(row_to[k])))
        def _():
            row_copy(k).wait_send()

    for slot in range(2, 8):
        coef_pass(slot).wait_send()
    for copy in sent:
        copy.wait_send()
    for m in range(8):
        arrived(frecv.at[m], f_recv.at[m])
    for out in range(2):
        total = frecv[0, out]
        for m in range(1, 8):
            total = total + frecv[m, out]
        for k in range(6):
            out_ref[out, 0:1, pl.ds(128 * k, 128)] = total[k : k + 1]
        out_ref[out, 0:1, pl.ds(768, 32)] = total[6:7, 0:32]
    for c in range(2):
        for k in range(4):

            @pl.when(jnp.logical_not(is_me(final_to[c][k])))
            def _():
                final_copy(c, k).wait_send()


def body(source_field, kappa, absorb, det_cell, pair_det, pair_count, measured):
    vmem = pl.BlockSpec(memory_space=pltpu.VMEM)
    hbm = pl.BlockSpec(memory_space=pltpu.HBM)
    out = jax.ShapeDtypeStruct((2, 1, 800), F32)
    dma = pltpu.SemaphoreType.DMA
    sums = pl.pallas_call(
        kernel,
        out_shape=out,
        in_specs=[hbm] * 7,
        out_specs=vmem,
        scratch_shapes=[
            pltpu.VMEM((3, PLANE_ROWS, LANES), F32),
            pltpu.SMEM((1,), jnp.int32),
            pltpu.VMEM((1, NDET), jnp.int32),
            pltpu.VMEM((1, PAIRS), jnp.int32),
            pltpu.VMEM((2, 1, PAIRS), F32),
            pltpu.VMEM((3, TALL, LANES), F32),
            pltpu.VMEM((8, 3, SLOT, LANES), F32),
            pltpu.VMEM((2, PLANES, SLOT, LANES), F32),
            pltpu.VMEM((STACKED, LANES), F32),
            pltpu.VMEM((STACKED, LANES), F32),
            pltpu.VMEM((7, FLAT, LANES), F32),
            pltpu.VMEM((2, STACKED, LANES), F32),
            pltpu.VMEM((2, STACKED, LANES), F32),
            pltpu.VMEM((2, FLAT, LANES), F32),
            pltpu.VMEM((2, 2, STACKED, LANES), F32),
            pltpu.VMEM((OWN_PLANES, 2, SLOT, LANES), F32),
            pltpu.VMEM((FLAT, NDET), BF16),
            pltpu.VMEM((LANES, NDET), F32),
            pltpu.VMEM((NDET, PAIRS), BF16),
            pltpu.VMEM((8, PAIRS), F32),
            pltpu.VMEM((8, PAIRS), F32),
            pltpu.VMEM((SLABS, 2, NDET), F32),
            pltpu.VMEM((OWN_PLANES, 56, LANES), F32),
            pltpu.VMEM((2, 4, 56, LANES), F32),
            pltpu.VMEM((2, 56, LANES), F32),
            pltpu.VMEM((2, 4, 2, 8, LANES), F32),
            pltpu.VMEM((8, 2, 8, LANES), F32),
            dma((7,)), dma((8,)), dma((8,)), dma((4,)), dma((8,)), dma((1,)), dma((2,)),
            dma((3,)), dma((3,)), dma((1,)), dma((1,)),
            dma((6,)), dma((6,)), dma((6,)), dma((6,)),
            dma((15,)), dma((16,)), dma((8,)), dma((2, 4)), dma((8,)), dma((8,)),
        ],
        compiler_params=pltpu.CompilerParams(
            collective_id=0, has_side_effects=True, vmem_limit_bytes=60 * 1024 * 1024
        ),
    )(
        pair_count,
        source_field.reshape(PLANE_ROWS, LANES),
        kappa.reshape(PLANE_ROWS, LANES),
        absorb.reshape(PLANE_ROWS, LANES),
        det_cell.reshape(1, NDET),
        pair_det,
        measured,
    )
    return (-sums[0], -0.5 * sums[1])


def solution(mesh):
    placed = (
        P("src", "slab", None),
        P("slab", None),
        P("slab", None),
        P(),
        P("src", None),
        P("src"),
        P(None, "src", None),
    )
    return jax.shard_map(
        body,
        mesh=mesh,
        in_specs=placed,
        out_specs=(P("slab", "src"), P("slab", "src")),
        check_vma=False,
    )
```

```python
import jax
import jax.numpy as jnp
from jax import lax
from jax.experimental import pallas as pl
from jax.experimental.pallas import tpu as pltpu
from jax.sharding import PartitionSpec as P

NY = 160
SWEEPS = 6
NDET = 512
PAIRS = 256
SLABS = 16
HALO = 6
INNER = 32
INNER_AT = 4
OWN_ROWS = 20
OWN_PLANES = 8
PLANES = OWN_PLANES + HALO
SLOT = 40
LANES = 128
FLAT = PLANES * SLOT
STACKED = FLAT + 2 * SLOT
PLANE_ROWS = 200
TALL = 216
MESH = pl.DeviceIdType.MESH
F32 = jnp.float32
BF16 = jnp.bfloat16

spectrum_low = 0.02
spectrum_high = 25.0
frequency_shift = 0.3


def chebyshev_terms():
    theta = (spectrum_high + spectrum_low) / 2.0
    delta = (spectrum_high - spectrum_low) / 2.0
    sigma = theta / delta
    rho = 1.0 / sigma
    keeps = []
    pushes = []
    for sweep in range(SWEEPS - 1):
        rho_new = 1.0 / (2.0 * sigma - rho)
        keeps.append(rho_new * rho)
        pushes.append(2.0 * rho_new / delta)
        rho = rho_new
    return (1.0 / theta, keeps, pushes)


def parts_of(value):
    high = value.astype(BF16)
    rest = value - high.astype(F32)
    middle = rest.astype(BF16)
    low = (rest - middle.astype(F32)).astype(BF16)
    return (high, middle, low)


def dot(lhs, rhs, dims):
    return lax.dot_general(lhs, rhs, (dims, ((), ())), preferred_element_type=F32)


def dot_rows(rows, table, dims):
    stack = jnp.concatenate([part.astype(F32) for part in parts_of(rows)], axis=0).astype(BF16)
    out = dot(stack, table, dims)
    return out[0:8] + (out[8:16] + out[16:24])


def slot_of(plane):
    return jnp.where(plane < OWN_PLANES, plane, SLABS - 1 - plane)


def kernel(
    count_hbm, source_hbm, kappa_hbm, absorb_hbm, cell_hbm, pair_hbm, measured_hbm,
    out_ref,
    planes, count_ref, cell_ref, pair_ref, measured_ref,
    half_lane, send, coef_recv, source, kappa, coef, direc_a, direc_b, resid, field, grads,
    place, lane_hot, pair_hot, pair_send, pair_recv, reads, ysend, yrecv, ysum, fsend, frecv,
    i_sem, s_send, s_recv, k_send, k_recv, o_send, o_recv, g_send, g_recv, p_send, p_recv,
    t_send, t_recv, u_send, u_recv, r_send, r_recv, y_send, y_recv, f_send, f_recv,
):
    src = lax.axis_index("src")
    slab = lax.axis_index("slab")
    my_y = src // 8
    my_z = (slab // 8) * 8 + src % 8
    my_x = (slab % 8) // 2
    core = slab % 2
    upper = my_z // 8
    odd = my_z % 2
    pair_z = my_z - odd
    parity = jnp.where(upper == 0, odd, 1 - odd)
    group = my_x * 2 + parity
    member = group * 2 + core
    solved = jnp.where((pair_z >= 4) & (pair_z <= 10), pair_z - 4, lax.rem(pair_z + 5, 16))
    own_zlo = src % 8
    goal_z = jnp.where(own_zlo % 2 == 0, own_zlo + 4, lax.rem(own_zlo + 11, 16))
    def goal_of(half):
        return goal_z + jnp.where(goal_z < 8, half, 1 - half)

    swap_z = jnp.where(own_zlo < 4, lax.rem(my_z + 12, 16), lax.rem(my_z + 4, 16))
    native = core == upper

    def device(y, z, x, c):
        return (y * 8 + lax.rem(z, 8), (z // 8) * 8 + x * 2 + c)

    def is_me(dev):
        return (dev[0] == src) & (dev[1] == slab)

    far_x = [lax.rem(my_x + step, 4) for step in (2, 1, 3, 0)]
    far_spots = [(x, c) for x in far_x for c in range(2)]
    source_groups = [2 * x + c for x, c in far_spots]
    source_from = [(my_y * 8 + solved, core * 8 + i) for i in range(8)]
    near = [device(my_y, my_z, x, c) for x, c in far_spots[:6]] + [device(my_y, my_z, my_x, 1 - core)]
    twin = [device(my_y, pair_z + 1 - odd, x, c) for x, c in far_spots]
    native_x = far_x
    native_to = [device(my_y, my_z, x, upper) for x in native_x]
    beyond_to = device(my_y, swap_z, lax.rem(my_x + 4 - my_y, 4), upper)
    beyond_from = [device(my_y, swap_z, lax.rem(my_x + my_y, 4), c) for c in range(2)]
    y_peers = [(lax.rem(my_y + j, 4) * 8 + own_zlo, slab) for j in range(1, 4)]
    other_core = (src, slab + 1 - 2 * core)

    def plane_of(slot, half):
        return jnp.where(half == 0, slot, SLABS - 1 - slot)

    row_slots = [jnp.where(core == 0, 2 * x + c, 7 - 2 * x - c) for x, c in far_spots]
    row_to = []
    for q in row_slots:
        p = plane_of(q, core) % 8
        row_to.append(device(my_x, my_z, p // 2, p % 2))
    row_from = [device(lax.rem(my_y + j, 4), my_z, my_y, c) for j in range(1, 4) for c in range(2)]
    final_h = list(range(4))
    final_to = [[device(my_y, 8 * c + 4 * parity + h, my_x, core) for h in final_h] for c in range(2)]
    final_half = own_zlo // 4
    final_from = [
        device(my_y, 2 * m + (final_half if m < 4 else 1 - final_half), my_x, core) for m in range(8)
    ]

    barrier = pltpu.get_barrier_semaphore()
    to_self = jnp.int32(0)
    for dev in final_from:
        to_self = to_self + jnp.where(is_me(dev), 1, 0)

        @pl.when(jnp.logical_not(is_me(dev)))
        def _():
            pl.semaphore_signal(barrier, inc=1, device_id=dev, device_id_type=MESH)

    for dev in source_from:
        pl.semaphore_signal(barrier, inc=1, device_id=dev, device_id_type=MESH)

    @pl.when(jnp.logical_not(native))
    def _():
        for dev in beyond_from + y_peers:
            pl.semaphore_signal(barrier, inc=1, device_id=dev, device_id_type=MESH)

    for dev in row_from + twin + near:
        pl.semaphore_signal(barrier, inc=1, device_id=dev, device_id_type=MESH)

    loads = [
        pltpu.make_async_copy(ref, dst, i_sem.at[n])
        for n, (ref, dst) in enumerate((
            (kappa_hbm, planes.at[0]), (absorb_hbm, planes.at[1]), (source_hbm, planes.at[2]),
            (cell_hbm, cell_ref), (count_hbm, count_ref), (pair_hbm, pair_ref), (measured_hbm, measured_ref),
        ))
    ]
    for load in loads:
        load.start()

    lane = lax.broadcasted_iota(jnp.int32, (SLOT, LANES), 1)
    flat = lax.broadcasted_iota(jnp.int32, (SLOT, LANES), 0) * LANES + lane
    row = ((flat >> 5) * 205) >> 10
    col = flat - row * NY
    first_row = OWN_ROWS * group - HALO
    real_row = row + first_row
    row_in = (real_row >= 0) & (real_row < 160)
    xp_in = (row_in & (real_row < 159)).astype(F32)
    xm_in = (row_in & (real_row > 0)).astype(F32)
    yp_in = (col < NY - 1).astype(F32)
    ym_in = (col > 0).astype(F32)
    inner_flat = flat[0:INNER] + INNER_AT * LANES
    inner_col = inner_flat - (((inner_flat >> 5) * 205) >> 10) * NY
    yp_inner = (inner_col < NY - 1).astype(F32)
    ym_inner = (inner_col > 0).astype(F32)

    def x_plus(ref, base, size=SLOT):
        near_row, far_row = ref[pl.ds(base + 1, size), :], ref[pl.ds(base + 2, size), :]
        return pltpu.roll(jnp.where(lane[0:size] >= 32, near_row, far_row), 96, 1)

    def x_minus(ref, base, size=SLOT):
        near_row, far_row = ref[pl.ds(base - 1, size), :], ref[pl.ds(base - 2, size), :]
        return pltpu.roll(jnp.where(lane[0:size] < 96, near_row, far_row), 32, 1)

    def y_plus(ref, base, here, size=SLOT):
        return pltpu.roll(jnp.where(lane[0:size] >= 1, here, ref[pl.ds(base + 1, size), :]), 127, 1)

    def y_minus(ref, base, here, size=SLOT):
        return pltpu.roll(jnp.where(lane[0:size] < 127, here, ref[pl.ds(base - 1, size), :]), 1, 1)

    def at(p):
        return p * SLOT if isinstance(p, int) else pl.multiple_of(p * SLOT, 8)

    for load in loads:
        load.wait()
    for which in range(3):
        half_lane[which, pl.ds(0, 8), :] = jnp.zeros((8, LANES), F32)
        half_lane[which, pl.ds(8, PLANE_ROWS), :] = pltpu.roll(planes[which], 64, 1)
        half_lane[which, pl.ds(8 + PLANE_ROWS, 8), :] = jnp.zeros((8, LANES), F32)
        for g in range(8):
            send[g, which] = jnp.where(
                lane < 64, half_lane[which, pl.ds(25 * g, SLOT), :], half_lane[which, pl.ds(25 * g + 1, SLOT), :]
            )
    active = (lax.broadcasted_iota(jnp.int32, (1, PAIRS), 1) < count_ref[0]).astype(F32)
    pair_send[...] = jnp.concatenate(
        [pair_ref[...].astype(F32), measured_ref[0], measured_ref[1], active, jnp.zeros((4, PAIRS), F32)],
        axis=0,
    )

    def remote_copy(src_ref, dst_ref, send_sem, recv_sem, dev):
        return pltpu.make_async_remote_copy(
            src_ref=src_ref, dst_ref=dst_ref, send_sem=send_sem, recv_sem=recv_sem,
            device_id=dev, device_id_type=MESH,
        )

    def remote(*args):
        copy = remote_copy(*args)
        copy.start()
        return copy

    def arrived(ref, sem):
        pltpu.make_async_copy(ref, ref, sem).wait()

    def source_slot(slot):
        return source.at[pl.ds(at(slot + 1), SLOT), :]

    two = pl.ds(0, 2)
    my_slot = slot_of(slab)
    rows_leave = jnp.where(my_x == my_y, 0, 8)
    pl.semaphore_wait(barrier, 8 + 8 + 7 + 1 + 8 - to_self + rows_leave + jnp.where(native, 0, 3))
    sent = [remote(
        send.at[2 * lax.rem(my_x + 4 - my_y, 4) + 1 - parity, two], coef_recv.at[:, my_slot],
        o_send.at[0], o_recv.at[core], beyond_to,
    )]
    def native_copy(k):
        return remote_copy(
            send.at[2 * native_x[k] + parity, two], coef_recv.at[:, my_slot],
            k_send.at[k], k_recv.at[my_slot], native_to[k],
        )

    for k in range(4):

        @pl.when(jnp.logical_not(is_me(native_to[k])))
        def _():
            native_copy(k).start()

    for k, g in enumerate(source_groups):
        sent.append(remote(
            send.at[g, 2], source_slot(my_slot), s_send.at[k], s_recv.at[my_slot],
            device(my_y, goal_of(g % 2), g // 2, upper),
        ))
    sent.append(remote(
        pair_send, pair_recv, p_send.at[0], p_recv.at[0],
        device(my_y, goal_of(slab % 2), (slab % 8) // 2, upper),
    ))

    guard = jnp.zeros((SLOT, LANES), F32)
    last = (PLANES + 1) * SLOT
    for start in (0, last):
        kappa[pl.ds(start, SLOT), :] = guard
        source[pl.ds(start, SLOT), :] = guard
        for c in range(2):
            direc_a[c, pl.ds(start, SLOT), :] = guard
            direc_b[c, pl.ds(start, SLOT), :] = guard
            for a in range(2):
                field[a, c, pl.ds(start, SLOT), :] = guard

    cell = cell_ref[...]
    det_z = ((cell >> 10) * 1311) >> 15
    in_plane = cell - det_z * 25600
    det_x = ((in_plane >> 5) * 6554) >> 15
    det_y = in_plane - det_x * NY
    det_row = det_x - first_row
    det_slot = plane_of(det_z, core)
    in_window = (det_row >= 0) & (det_row < OWN_ROWS + 2 * HALO) & (det_slot < PLANES)
    owned = (
        (det_row >= HALO) & (det_row < HALO + OWN_ROWS) & (det_slot < OWN_PLANES)
    ).astype(F32)
    spot = det_row * NY + det_y
    det_sub = jnp.where(in_window, det_slot * SLOT + (spot >> 7), -1)
    det_lane = spot & 127

    @pl.loop(0, FLAT // 16, unroll=5)
    def _(p):
        subs = lax.broadcasted_iota(jnp.int32, (16, NDET), 0) + p * 16
        place[pl.ds(pl.multiple_of(p * 16, 16), 16), :] = (subs == det_sub).astype(F32).astype(BF16)

    lane_hot[...] = (lax.broadcasted_iota(jnp.int32, (LANES, NDET), 0) == det_lane).astype(F32)

    def coef_pass(slot):
        return remote_copy(
            coef_recv.at[:, slot], coef_recv.at[:, SLABS - 1 - slot],
            t_send.at[slot - 2], t_recv.at[slot - 2], other_core,
        )

    def coef_came(slot):
        @pl.when(slot >= 2)
        def _():
            coef_pass(slot).start()

    @pl.when(native)
    def _():
        coef_recv[:, my_slot] = send[group, 0:2]
        coef_came(my_slot)
        for j in range(1, 8):
            slot = lax.rem(my_slot + j, 8)
            arrived(coef_recv.at[:, slot], k_recv.at[slot])
            coef_came(slot)

    @pl.when(jnp.logical_not(native))
    def _():
        def first_slot(x):
            return jnp.where(core == 0, 2 * x, 6 - 2 * x)

        for c in range(2):
            slot = jnp.where(core == 0, 2 * lax.rem(my_x + my_y, 4) + c, 7 - 2 * lax.rem(my_x + my_y, 4) - c)
            arrived(coef_recv.at[:, slot], o_recv.at[c])
        slots = [pl.ds(first_slot(lax.rem(my_x + my_y + 4 - j, 4)), 2) for j in range(4)]
        strips = coef_recv.at[:, slots[0]]
        across = [remote(strips, strips, g_send.at[j], g_recv.at[j], dev) for j, dev in enumerate(y_peers)]
        for j in range(4):
            if j:
                arrived(coef_recv.at[:, slots[j]], g_recv.at[j - 1])
            low = first_slot(lax.rem(my_x + my_y + 4 - j, 4))
            for n in range(2):
                coef_came(low + n)
        for copy in across:
            copy.wait_send()

    for slot in range(8):
        arrived(source_slot(slot), s_recv.at[slot])
        if slot >= 2:
            sent.append(remote(
                source_slot(slot), source_slot(SLABS - 1 - slot), u_send.at[slot - 2], u_recv.at[slot - 2], other_core
            ))
    for n in range(6):
        arrived(coef_recv.at[:, OWN_PLANES + 5 - n], t_recv.at[n])

    @pl.loop(0, PLANES, unroll=7)
    def _(p):
        kappa[pl.ds(at(p + 1), SLOT), :] = coef_recv[0, p]

    @pl.loop(0, PLANES, unroll=7)
    def _(p):
        base, here = at(p + 1), at(p)
        k = kappa[pl.ds(base, SLOT), :]
        diagonal = coef_recv[1, p]
        beside = (
            (x_plus(kappa, base), xp_in),
            (x_minus(kappa, base), xm_in),
            (y_plus(kappa, base, k) * yp_in, yp_in),
            (y_minus(kappa, base, k) * ym_in, ym_in),
            (kappa[pl.ds(base + SLOT, SLOT), :], jnp.where(p < PLANES - 1, 1.0, 0.0).astype(F32)),
            (kappa[pl.ds(base - SLOT, SLOT), :], jnp.where(p > 0, 1.0, 0.0).astype(F32)),
        )
        for which, (side, inside) in enumerate(beside):
            face = (k + side) * 0.5
            diagonal = diagonal + face
            coef[which, pl.ds(here, SLOT), :] = face * inside
        coef[6, pl.ds(here, SLOT), :] = diagonal

    for n in range(6):
        arrived(source_slot(OWN_PLANES + 5 - n), u_recv.at[n])

    first, keeps, pushes = chebyshev_terms()

    def spread_of(ref, base, cs, here, size=SLOT):
        return (
            cs[0] * x_plus(ref, base, size)
            + cs[1] * x_minus(ref, base, size)
            + cs[2] * y_plus(ref, base, here, size)
            + cs[3] * y_minus(ref, base, here, size)
            + cs[4] * ref[pl.ds(base + SLOT, size), :]
            + cs[5] * ref[pl.ds(base - SLOT, size), :]
        )

    def solve(out, rights):
        for sweep in range(SWEEPS - 1):
            keep, push = keeps[sweep], pushes[sweep]
            now, later = (direc_a, direc_b) if sweep % 2 == 0 else (direc_b, direc_a)
            count = PLANES - 1 - sweep

            def first_sweep(p, kept):
                here, base = at(p), at(p + 1)
                cs = [coef[which, pl.ds(here, SLOT), :] for which in range(7)]
                bs = [ref[pl.ds(base, SLOT), :] for ref in rights]
                for c in range(2):
                    if len(bs) == 1:
                        turned = 0.0 if c == 0 else bs[0]
                    else:
                        turned = -bs[1] if c == 0 else bs[0]
                    if c < len(bs):
                        off = spread_of(rights[c], base, cs, bs[c])
                        applied = cs[6] * bs[c] - off + frequency_shift * turned
                        left = bs[c] - first * applied
                        new = (keep * first) * bs[c] + push * left
                        start = first * bs[c]
                    else:
                        left = (-first * frequency_shift) * turned
                        new = push * left
                        start = 0.0
                    resid[c, pl.ds(here, SLOT), :] = left
                    later[c, pl.ds(base, SLOT), :] = new
                    if kept:
                        field[out, c, pl.ds(base, SLOT), :] = start + new

            def one_plane(p, kept):
                if sweep == 0:
                    first_sweep(p, kept)
                    return
                skip, size = (INNER_AT, INNER) if sweep >= SWEEPS - 3 else (0, SLOT)
                here, base = at(p) + skip, at(p + 1) + skip
                cs = [coef[which, pl.ds(here, size), :] for which in range(7)]
                ds = [now[c, pl.ds(base, size), :] for c in range(2)]
                turned = (-ds[1], ds[0])
                for c in range(2):
                    off = spread_of(now.at[c], base, cs, ds[c], size)
                    applied = cs[6] * ds[c] - off + frequency_shift * turned[c]
                    left = resid[c, pl.ds(here, size), :] - applied
                    new = keep * ds[c] + push * left
                    if sweep < SWEEPS - 2:
                        resid[c, pl.ds(here, size), :] = left
                        later[c, pl.ds(base, size), :] = new
                    if kept:
                        field[out, c, pl.ds(base, size), :] = field[out, c, pl.ds(base, size), :] + new

            @pl.loop(0, OWN_PLANES + 1, unroll=OWN_PLANES + 1)
            def _(p):
                one_plane(p, True)

            if count > OWN_PLANES + 1:

                @pl.loop(OWN_PLANES + 1, count, unroll=count - OWN_PLANES - 1)
                def _(p):
                    one_plane(p, False)

    solve(0, [source])

    whole = pl.ds(SLOT, FLAT)
    mine_rows = OWN_PLANES * SLOT
    mine_planes = pl.ds(SLOT, mine_rows)
    table = place[pl.ds(0, mine_rows), :]
    both = jnp.concatenate([field[0, 0, mine_planes, :], field[0, 1, mine_planes, :]], axis=1)
    high, middle, low = [dot(part, table, ((0,), (0,))) for part in parts_of(both)]
    found = high + (middle + low)
    for c in range(2):
        spread = found[LANES * c : LANES * (c + 1)] * lane_hot[...]
        reads[member, pl.ds(c, 1), :] = jnp.sum(spread, axis=0, keepdims=True) * owned
    mine = reads.at[member]
    for i, dev in enumerate(twin + near):
        sent.append(remote(mine, mine, r_send.at[i], r_recv.at[member], dev))
    arrived(pair_recv, p_recv.at[0])
    pair_hot[...] = (
        lax.broadcasted_iota(jnp.int32, (NDET, PAIRS), 0).astype(F32) == pair_recv[0:1]
    ).astype(F32).astype(BF16)
    for j in range(1, SLABS):
        other = lax.rem(member + j, SLABS)
        arrived(reads.at[other], r_recv.at[other])
    readings = jnp.sum(reads[...], axis=0)
    wide = jnp.concatenate([readings, jnp.zeros((6, NDET), F32)], axis=0)
    model = dot_rows(wide, pair_hot[...], ((1,), (0,)))
    active = pair_recv[3:4]
    conj = jnp.concatenate(
        [
            (model[0:1] - pair_recv[1:2]) * active,
            (pair_recv[2:3] - model[1:2]) * active,
            jnp.zeros((6, PAIRS), F32),
        ],
        axis=0,
    )
    weights = dot_rows(conj, pair_hot[...], ((1,), (1,)))
    hot = lane_hot[...]
    right = None
    for part in parts_of(weights):
        part = part.astype(F32)
        piece = jnp.concatenate([hot * part[0:1], hot * part[1:2]], axis=0).astype(BF16)
        term = dot(place[...], piece, ((1,), (1,)))
        right = term if right is None else right + term
    for c in range(2):
        direc_a[c, whole, :] = right[:, LANES * c : LANES * (c + 1)]

    solve(1, [direc_a.at[0], direc_a.at[1]])

    def row_copy(k):
        return remote_copy(
            ysend.at[k], yrecv.at[core, my_y], y_send.at[k], y_recv.at[core, my_y], row_to[k]
        )

    for k, q in enumerate(row_slots):
        base = at(q + 1) + INNER_AT
        refs = [[field.at[a, c] for c in range(2)] for a in range(2)]
        here = [[refs[a][c][pl.ds(base, INNER), :] for c in range(2)] for a in range(2)]
        sides = (
            lambda ref, b: x_plus(ref, b, INNER),
            lambda ref, b: x_minus(ref, b, INNER),
            lambda ref, b: y_plus(ref, b, ref[pl.ds(b, INNER), :], INNER) * yp_inner,
            lambda ref, b: y_minus(ref, b, ref[pl.ds(b, INNER), :], INNER) * ym_inner,
            lambda ref, b: ref[pl.ds(b + SLOT, INNER), :],
            lambda ref, b: ref[pl.ds(b - SLOT, INNER), :],
        )
        total = jnp.zeros((INNER, LANES), F32)
        for side in sides:
            gap = [[here[a][c] - side(refs[a][c], base) for c in range(2)] for a in range(2)]
            total = total + gap[0][0] * gap[1][0] - gap[0][1] * gap[1][1]
        grads[k, 0] = here[0][0] * here[1][0] - here[0][1] * here[1][1]
        grads[k, 1] = total
        for out in range(2):
            low, high = grads[k, out, pl.ds(3, 28), :], grads[k, out, pl.ds(4, 28), :]
            rows = pltpu.roll(jnp.where(lane[0:28] >= 64, low, high), 64, 1)
            ysend[k, pl.ds(25 * out, 25), :] = rows[0:25]
        ysend[k, pl.ds(50, 6), :] = jnp.zeros((6, LANES), F32)
        stays = is_me(row_to[k])

        @pl.when(jnp.logical_not(stays))
        def _():
            row_copy(k).start()

        @pl.when(stays)
        def _():
            pltpu.make_async_copy(ysend.at[k], yrecv.at[core, my_y], y_recv.at[core, my_y]).start()

    def final_copy(c, k):
        return remote_copy(
            fsend.at[c, final_h[k]], frecv.at[my_z // 2], f_send.at[4 * c + k], f_recv.at[my_z // 2], final_to[c][k]
        )

    for c in range(2):
        for y in range(4):
            arrived(yrecv.at[c, y], y_recv.at[c, y])
        ysum[c] = (yrecv[c, 0] + yrecv[c, 1]) + (yrecv[c, 2] + yrecv[c, 3])
        for h in range(4):
            for out in range(2):
                start = 25 * out + (25 * h) // 4
                low, high = ysum[c, pl.ds(start, 8), :], ysum[c, pl.ds(start + 1, 8), :]
                if h == 0:
                    fsend[c, h, out] = low
                else:
                    fsend[c, h, out] = pltpu.roll(jnp.where(lane[0:8] >= 32 * h, low, high), 128 - 32 * h, 1)
        for k in range(4):
            own = is_me(final_to[c][k])

            @pl.when(jnp.logical_not(own))
            def _():
                final_copy(c, k).start()

            @pl.when(own)
            def _():
                pltpu.make_async_copy(fsend.at[c, final_h[k]], frecv.at[my_z // 2], f_recv.at[my_z // 2]).start()

    for k in range(4):

        @pl.when(jnp.logical_not(is_me(native_to[k])))
        def _():
            native_copy(k).wait_send()

    for k in range(OWN_PLANES):

        @pl.when(jnp.logical_not(is_me(row_to[k])))
        def _():
            row_copy(k).wait_send()

    for slot in range(2, 8):
        coef_pass(slot).wait_send()
    for copy in sent:
        copy.wait_send()
    for m in range(8):
        arrived(frecv.at[m], f_recv.at[m])
    for out in range(2):
        total = frecv[0, out]
        for m in range(1, 8):
            total = total + frecv[m, out]
        for k in range(6):
            out_ref[out, 0:1, pl.ds(128 * k, 128)] = total[k : k + 1]
        out_ref[out, 0:1, pl.ds(768, 32)] = total[6:7, 0:32]
    for c in range(2):
        for k in range(4):

            @pl.when(jnp.logical_not(is_me(final_to[c][k])))
            def _():
                final_copy(c, k).wait_send()


def body(source_field, kappa, absorb, det_cell, pair_det, pair_count, measured):
    vmem = pl.BlockSpec(memory_space=pltpu.VMEM)
    hbm = pl.BlockSpec(memory_space=pltpu.HBM)
    out = jax.ShapeDtypeStruct((2, 1, 800), F32)
    dma = pltpu.SemaphoreType.DMA
    sums = pl.pallas_call(
        kernel,
        out_shape=out,
        in_specs=[hbm] * 7,
        out_specs=vmem,
        scratch_shapes=[
            pltpu.VMEM((3, PLANE_ROWS, LANES), F32),
            pltpu.SMEM((1,), jnp.int32),
            pltpu.VMEM((1, NDET), jnp.int32),
            pltpu.VMEM((1, PAIRS), jnp.int32),
            pltpu.VMEM((2, 1, PAIRS), F32),
            pltpu.VMEM((3, TALL, LANES), F32),
            pltpu.VMEM((8, 3, SLOT, LANES), F32),
            pltpu.VMEM((2, PLANES, SLOT, LANES), F32),
            pltpu.VMEM((STACKED, LANES), F32),
            pltpu.VMEM((STACKED, LANES), F32),
            pltpu.VMEM((7, FLAT, LANES), F32),
            pltpu.VMEM((2, STACKED, LANES), F32),
            pltpu.VMEM((2, STACKED, LANES), F32),
            pltpu.VMEM((2, FLAT, LANES), F32),
            pltpu.VMEM((2, 2, STACKED, LANES), F32),
            pltpu.VMEM((OWN_PLANES, 2, INNER, LANES), F32),
            pltpu.VMEM((FLAT, NDET), BF16),
            pltpu.VMEM((LANES, NDET), F32),
            pltpu.VMEM((NDET, PAIRS), BF16),
            pltpu.VMEM((8, PAIRS), F32),
            pltpu.VMEM((8, PAIRS), F32),
            pltpu.VMEM((SLABS, 2, NDET), F32),
            pltpu.VMEM((OWN_PLANES, 56, LANES), F32),
            pltpu.VMEM((2, 4, 56, LANES), F32),
            pltpu.VMEM((2, 56, LANES), F32),
            pltpu.VMEM((2, 4, 2, 8, LANES), F32),
            pltpu.VMEM((8, 2, 8, LANES), F32),
            dma((7,)), dma((8,)), dma((8,)), dma((4,)), dma((8,)), dma((1,)), dma((2,)),
            dma((3,)), dma((3,)), dma((1,)), dma((1,)),
            dma((6,)), dma((6,)), dma((6,)), dma((6,)),
            dma((15,)), dma((16,)), dma((8,)), dma((2, 4)), dma((8,)), dma((8,)),
        ],
        compiler_params=pltpu.CompilerParams(
            collective_id=0, has_side_effects=True, vmem_limit_bytes=60 * 1024 * 1024
        ),
    )(
        pair_count,
        source_field.reshape(PLANE_ROWS, LANES),
        kappa.reshape(PLANE_ROWS, LANES),
        absorb.reshape(PLANE_ROWS, LANES),
        det_cell.reshape(1, NDET),
        pair_det,
        measured,
    )
    return (-sums[0], -0.5 * sums[1])


def solution(mesh):
    placed = (
        P("src", "slab", None),
        P("slab", None),
        P("slab", None),
        P(),
        P("src", None),
        P("src"),
        P(None, "src", None),
    )
    return jax.shard_map(
        body,
        mesh=mesh,
        in_specs=placed,
        out_specs=(P("slab", "src"), P("slab", "src")),
        check_vma=False,
    )
```

```python
import jax
import jax.numpy as jnp
from jax import lax
from jax.experimental import pallas as pl
from jax.experimental.pallas import tpu as pltpu
from jax.sharding import PartitionSpec as P

NY = 160
SWEEPS = 6
NDET = 512
PAIRS = 256
SLABS = 16
HALO = 6
INNER = 32
INNER_AT = 4
OWN_ROWS = 20
OWN_PLANES = 8
PLANES = OWN_PLANES + HALO
SLOT = 40
LANES = 128
FLAT = PLANES * SLOT
STACKED = FLAT + 2 * SLOT
PLANE_ROWS = 200
TALL = 216
MESH = pl.DeviceIdType.MESH
F32 = jnp.float32
BF16 = jnp.bfloat16

spectrum_low = 0.02
spectrum_high = 25.0
frequency_shift = 0.3


def chebyshev_terms():
    theta = (spectrum_high + spectrum_low) / 2.0
    delta = (spectrum_high - spectrum_low) / 2.0
    sigma = theta / delta
    rho = 1.0 / sigma
    keeps = []
    pushes = []
    for sweep in range(SWEEPS - 1):
        rho_new = 1.0 / (2.0 * sigma - rho)
        keeps.append(rho_new * rho)
        pushes.append(2.0 * rho_new / delta)
        rho = rho_new
    return (1.0 / theta, keeps, pushes)


def parts_of(value):
    high = value.astype(BF16)
    rest = value - high.astype(F32)
    middle = rest.astype(BF16)
    low = (rest - middle.astype(F32)).astype(BF16)
    return (high, middle, low)


def dot(lhs, rhs, dims):
    return lax.dot_general(lhs, rhs, (dims, ((), ())), preferred_element_type=F32)


def dot_rows(rows, table, dims):
    stack = jnp.concatenate([part.astype(F32) for part in parts_of(rows)], axis=0).astype(BF16)
    out = dot(stack, table, dims)
    return out[0:8] + (out[8:16] + out[16:24])


def slot_of(plane):
    return jnp.where(plane < OWN_PLANES, plane, SLABS - 1 - plane)


def kernel(
    count_hbm, source_hbm, kappa_hbm, absorb_hbm, cell_hbm, pair_hbm, measured_hbm,
    out_ref,
    planes, count_ref, cell_ref, pair_ref, measured_ref,
    half_lane, send, coef_recv, source, kappa, coef, direc_a, direc_b, resid, field, grads,
    place, lane_hot, pair_hot, pair_send, pair_recv, reads, ysend, yrecv, ysum, fsend, frecv,
    i_sem, s_send, s_recv, k_send, k_recv, o_send, o_recv, g_send, g_recv, p_send, p_recv,
    t_send, t_recv, u_send, u_recv, r_send, r_recv, y_send, y_recv, f_send, f_recv,
):
    src = lax.axis_index("src")
    slab = lax.axis_index("slab")
    my_y = src // 8
    my_z = (slab // 8) * 8 + src % 8
    my_x = (slab % 8) // 2
    core = slab % 2
    upper = my_z // 8
    odd = my_z % 2
    pair_z = my_z - odd
    parity = jnp.where(upper == 0, odd, 1 - odd)
    group = my_x * 2 + parity
    member = group * 2 + core
    solved = jnp.where((pair_z >= 4) & (pair_z <= 10), pair_z - 4, lax.rem(pair_z + 5, 16))
    own_zlo = src % 8
    goal_z = jnp.where(own_zlo % 2 == 0, own_zlo + 4, lax.rem(own_zlo + 11, 16))
    def goal_of(half):
        return goal_z + jnp.where(goal_z < 8, half, 1 - half)

    swap_z = jnp.where(own_zlo < 4, lax.rem(my_z + 12, 16), lax.rem(my_z + 4, 16))
    native = core == upper

    def device(y, z, x, c):
        return (y * 8 + lax.rem(z, 8), (z // 8) * 8 + x * 2 + c)

    def is_me(dev):
        return (dev[0] == src) & (dev[1] == slab)

    far_x = [lax.rem(my_x + step, 4) for step in (2, 1, 3, 0)]
    far_spots = [(x, c) for x in far_x for c in range(2)]
    source_groups = [2 * x + c for x, c in far_spots]
    source_from = [(my_y * 8 + solved, core * 8 + i) for i in range(8)]
    near = [device(my_y, my_z, x, c) for x, c in far_spots[:6]] + [device(my_y, my_z, my_x, 1 - core)]
    twin = [device(my_y, pair_z + 1 - odd, x, c) for x, c in far_spots]
    native_x = far_x
    native_to = [device(my_y, my_z, x, upper) for x in native_x]
    beyond_to = device(my_y, swap_z, lax.rem(my_x + 4 - my_y, 4), upper)
    beyond_from = [device(my_y, swap_z, lax.rem(my_x + my_y, 4), c) for c in range(2)]
    y_peers = [(lax.rem(my_y + j, 4) * 8 + own_zlo, slab) for j in range(1, 4)]
    other_core = (src, slab + 1 - 2 * core)

    def plane_of(slot, half):
        return jnp.where(half == 0, slot, SLABS - 1 - slot)

    row_slots = [jnp.where(core == 0, 2 * x + c, 7 - 2 * x - c) for x, c in far_spots]
    row_to = []
    for q in row_slots:
        p = plane_of(q, core) % 8
        row_to.append(device(my_x, my_z, p // 2, p % 2))
    row_from = [device(lax.rem(my_y + j, 4), my_z, my_y, c) for j in range(1, 4) for c in range(2)]
    final_h = list(range(4))
    final_to = [[device(my_y, 8 * c + 4 * parity + h, my_x, core) for h in final_h] for c in range(2)]
    final_half = own_zlo // 4
    final_from = [
        device(my_y, 2 * m + (final_half if m < 4 else 1 - final_half), my_x, core) for m in range(8)
    ]

    barrier = pltpu.get_barrier_semaphore()
    to_self = jnp.int32(0)
    for dev in final_from:
        to_self = to_self + jnp.where(is_me(dev), 1, 0)

        @pl.when(jnp.logical_not(is_me(dev)))
        def _():
            pl.semaphore_signal(barrier, inc=1, device_id=dev, device_id_type=MESH)

    for dev in source_from:
        pl.semaphore_signal(barrier, inc=1, device_id=dev, device_id_type=MESH)

    @pl.when(jnp.logical_not(native))
    def _():
        for dev in beyond_from + y_peers:
            pl.semaphore_signal(barrier, inc=1, device_id=dev, device_id_type=MESH)

    for dev in row_from + twin + near:
        pl.semaphore_signal(barrier, inc=1, device_id=dev, device_id_type=MESH)

    loads = [
        pltpu.make_async_copy(ref, dst, i_sem.at[n])
        for n, (ref, dst) in enumerate((
            (kappa_hbm, planes.at[0]), (absorb_hbm, planes.at[1]), (source_hbm, planes.at[2]),
            (cell_hbm, cell_ref), (count_hbm, count_ref), (pair_hbm, pair_ref), (measured_hbm, measured_ref),
        ))
    ]
    for load in loads:
        load.start()

    lane = lax.broadcasted_iota(jnp.int32, (SLOT, LANES), 1)
    flat = lax.broadcasted_iota(jnp.int32, (SLOT, LANES), 0) * LANES + lane
    row = ((flat >> 5) * 205) >> 10
    col = flat - row * NY
    first_row = OWN_ROWS * group - HALO
    real_row = row + first_row
    row_in = (real_row >= 0) & (real_row < 160)
    xp_in = (row_in & (real_row < 159)).astype(F32)
    xm_in = (row_in & (real_row > 0)).astype(F32)
    yp_in = (col < NY - 1).astype(F32)
    ym_in = (col > 0).astype(F32)
    inner_flat = flat[0:INNER] + INNER_AT * LANES
    inner_col = inner_flat - (((inner_flat >> 5) * 205) >> 10) * NY
    yp_inner = (inner_col < NY - 1).astype(F32)
    ym_inner = (inner_col > 0).astype(F32)

    def x_plus(ref, base, size=SLOT):
        near_row, far_row = ref[pl.ds(base + 1, size), :], ref[pl.ds(base + 2, size), :]
        return pltpu.roll(jnp.where(lane[0:size] >= 32, near_row, far_row), 96, 1)

    def x_minus(ref, base, size=SLOT):
        near_row, far_row = ref[pl.ds(base - 1, size), :], ref[pl.ds(base - 2, size), :]
        return pltpu.roll(jnp.where(lane[0:size] < 96, near_row, far_row), 32, 1)

    def y_plus(ref, base, here, size=SLOT):
        return pltpu.roll(jnp.where(lane[0:size] >= 1, here, ref[pl.ds(base + 1, size), :]), 127, 1)

    def y_minus(ref, base, here, size=SLOT):
        return pltpu.roll(jnp.where(lane[0:size] < 127, here, ref[pl.ds(base - 1, size), :]), 1, 1)

    def at(p):
        return p * SLOT if isinstance(p, int) else pl.multiple_of(p * SLOT, 8)

    for load in loads:
        load.wait()
    for which in range(3):
        half_lane[which, pl.ds(0, 8), :] = jnp.zeros((8, LANES), F32)
        half_lane[which, pl.ds(8, PLANE_ROWS), :] = pltpu.roll(planes[which], 64, 1)
        half_lane[which, pl.ds(8 + PLANE_ROWS, 8), :] = jnp.zeros((8, LANES), F32)
        for g in range(8):
            send[g, which] = jnp.where(
                lane < 64, half_lane[which, pl.ds(25 * g, SLOT), :], half_lane[which, pl.ds(25 * g + 1, SLOT), :]
            )
    active = (lax.broadcasted_iota(jnp.int32, (1, PAIRS), 1) < count_ref[0]).astype(F32)
    pair_send[...] = jnp.concatenate(
        [pair_ref[...].astype(F32), measured_ref[0], measured_ref[1], active, jnp.zeros((4, PAIRS), F32)],
        axis=0,
    )

    def remote_copy(src_ref, dst_ref, send_sem, recv_sem, dev):
        return pltpu.make_async_remote_copy(
            src_ref=src_ref, dst_ref=dst_ref, send_sem=send_sem, recv_sem=recv_sem,
            device_id=dev, device_id_type=MESH,
        )

    def remote(*args):
        copy = remote_copy(*args)
        copy.start()
        return copy

    def arrived(ref, sem):
        pltpu.make_async_copy(ref, ref, sem).wait()

    def source_slot(slot):
        return source.at[pl.ds(at(slot + 1), SLOT), :]

    two = pl.ds(0, 2)
    my_slot = slot_of(slab)
    rows_leave = jnp.where(my_x == my_y, 0, 8)
    pl.semaphore_wait(barrier, 8 + 8 + 7 + 1 + 8 - to_self + rows_leave + jnp.where(native, 0, 3))
    sent = [remote(
        send.at[2 * lax.rem(my_x + 4 - my_y, 4) + 1 - parity, two], coef_recv.at[:, my_slot],
        o_send.at[0], o_recv.at[core], beyond_to,
    )]
    def native_copy(k):
        return remote_copy(
            send.at[2 * native_x[k] + parity, two], coef_recv.at[:, my_slot],
            k_send.at[k], k_recv.at[my_slot], native_to[k],
        )

    for k in range(4):

        @pl.when(jnp.logical_not(is_me(native_to[k])))
        def _():
            native_copy(k).start()

    for k, g in enumerate(source_groups):
        sent.append(remote(
            send.at[g, 2], source_slot(my_slot), s_send.at[k], s_recv.at[my_slot],
            device(my_y, goal_of(g % 2), g // 2, upper),
        ))
    sent.append(remote(
        pair_send, pair_recv, p_send.at[0], p_recv.at[0],
        device(my_y, goal_of(slab % 2), (slab % 8) // 2, upper),
    ))

    guard = jnp.zeros((SLOT, LANES), F32)
    last = (PLANES + 1) * SLOT
    for start in (0, last):
        kappa[pl.ds(start, SLOT), :] = guard
        source[pl.ds(start, SLOT), :] = guard
        for c in range(2):
            direc_a[c, pl.ds(start, SLOT), :] = guard
            direc_b[c, pl.ds(start, SLOT), :] = guard
            for a in range(2):
                field[a, c, pl.ds(start, SLOT), :] = guard

    cell = cell_ref[...]
    det_z = ((cell >> 10) * 1311) >> 15
    in_plane = cell - det_z * 25600
    det_x = ((in_plane >> 5) * 6554) >> 15
    det_y = in_plane - det_x * NY
    det_row = det_x - first_row
    det_slot = plane_of(det_z, core)
    in_window = (det_row >= 0) & (det_row < OWN_ROWS + 2 * HALO) & (det_slot < PLANES)
    owned = (
        (det_row >= HALO) & (det_row < HALO + OWN_ROWS) & (det_slot < OWN_PLANES)
    ).astype(F32)
    spot = det_row * NY + det_y
    det_sub = jnp.where(in_window, det_slot * SLOT + (spot >> 7), -1)
    det_lane = spot & 127

    @pl.loop(0, FLAT // 16, unroll=5)
    def _(p):
        subs = lax.broadcasted_iota(jnp.int32, (16, NDET), 0) + p * 16
        place[pl.ds(pl.multiple_of(p * 16, 16), 16), :] = (subs == det_sub).astype(F32).astype(BF16)

    lane_hot[...] = (lax.broadcasted_iota(jnp.int32, (LANES, NDET), 0) == det_lane).astype(F32)

    def coef_pass(slot):
        return remote_copy(
            coef_recv.at[:, slot], coef_recv.at[:, SLABS - 1 - slot],
            t_send.at[slot - 2], t_recv.at[slot - 2], other_core,
        )

    def coef_came(slot):
        @pl.when(slot >= 2)
        def _():
            coef_pass(slot).start()

    @pl.when(native)
    def _():
        coef_recv[:, my_slot] = send[group, 0:2]
        coef_came(my_slot)
        for j in range(1, 8):
            slot = lax.rem(my_slot + j, 8)
            arrived(coef_recv.at[:, slot], k_recv.at[slot])
            coef_came(slot)

    @pl.when(jnp.logical_not(native))
    def _():
        def first_slot(x):
            return jnp.where(core == 0, 2 * x, 6 - 2 * x)

        for c in range(2):
            slot = jnp.where(core == 0, 2 * lax.rem(my_x + my_y, 4) + c, 7 - 2 * lax.rem(my_x + my_y, 4) - c)
            arrived(coef_recv.at[:, slot], o_recv.at[c])
        slots = [pl.ds(first_slot(lax.rem(my_x + my_y + 4 - j, 4)), 2) for j in range(4)]
        strips = coef_recv.at[:, slots[0]]
        across = [remote(strips, strips, g_send.at[j], g_recv.at[j], dev) for j, dev in enumerate(y_peers)]
        for j in range(4):
            if j:
                arrived(coef_recv.at[:, slots[j]], g_recv.at[j - 1])
            low = first_slot(lax.rem(my_x + my_y + 4 - j, 4))
            for n in range(2):
                coef_came(low + n)
        for copy in across:
            copy.wait_send()

    for slot in range(8):
        arrived(source_slot(slot), s_recv.at[slot])
        if slot >= 2:
            sent.append(remote(
                source_slot(slot), source_slot(SLABS - 1 - slot), u_send.at[slot - 2], u_recv.at[slot - 2], other_core
            ))
    for n in range(6):
        arrived(coef_recv.at[:, OWN_PLANES + 5 - n], t_recv.at[n])

    @pl.loop(0, PLANES, unroll=7)
    def _(p):
        kappa[pl.ds(at(p + 1), SLOT), :] = coef_recv[0, p]

    @pl.loop(0, PLANES, unroll=7)
    def _(p):
        base, here = at(p + 1), at(p)
        k = kappa[pl.ds(base, SLOT), :]
        diagonal = coef_recv[1, p]
        beside = (
            (x_plus(kappa, base), xp_in),
            (x_minus(kappa, base), xm_in),
            (y_plus(kappa, base, k) * yp_in, yp_in),
            (y_minus(kappa, base, k) * ym_in, ym_in),
            (kappa[pl.ds(base + SLOT, SLOT), :], jnp.where(p < PLANES - 1, 1.0, 0.0).astype(F32)),
            (kappa[pl.ds(base - SLOT, SLOT), :], jnp.where(p > 0, 1.0, 0.0).astype(F32)),
        )
        for which, (side, inside) in enumerate(beside):
            face = (k + side) * 0.5
            diagonal = diagonal + face
            coef[which, pl.ds(here, SLOT), :] = face * inside
        coef[6, pl.ds(here, SLOT), :] = diagonal

    for n in range(6):
        arrived(source_slot(OWN_PLANES + 5 - n), u_recv.at[n])

    first, keeps, pushes = chebyshev_terms()

    def spread_of(ref, base, cs, here, size=SLOT):
        return (
            cs[0] * x_plus(ref, base, size)
            + cs[1] * x_minus(ref, base, size)
            + cs[2] * y_plus(ref, base, here, size)
            + cs[3] * y_minus(ref, base, here, size)
            + cs[4] * ref[pl.ds(base + SLOT, size), :]
            + cs[5] * ref[pl.ds(base - SLOT, size), :]
        )

    def solve(out, rights):
        for sweep in range(SWEEPS - 1):
            keep, push = keeps[sweep], pushes[sweep]
            now, later = (direc_a, direc_b) if sweep % 2 == 0 else (direc_b, direc_a)
            count = PLANES - 1 - sweep

            def first_sweep(p, kept):
                here, base = at(p), at(p + 1)
                cs = [coef[which, pl.ds(here, SLOT), :] for which in range(7)]
                bs = [ref[pl.ds(base, SLOT), :] for ref in rights]
                for c in range(2):
                    if len(bs) == 1:
                        turned = 0.0 if c == 0 else bs[0]
                    else:
                        turned = -bs[1] if c == 0 else bs[0]
                    if c < len(bs):
                        off = spread_of(rights[c], base, cs, bs[c])
                        applied = cs[6] * bs[c] - off + frequency_shift * turned
                        left = bs[c] - first * applied
                        new = (keep * first) * bs[c] + push * left
                        start = first * bs[c]
                    else:
                        left = (-first * frequency_shift) * turned
                        new = push * left
                        start = 0.0
                    resid[c, pl.ds(here, SLOT), :] = left
                    later[c, pl.ds(base, SLOT), :] = new
                    if kept:
                        field[out, c, pl.ds(base, SLOT), :] = start + new

            def one_plane(p, kept):
                if sweep == 0:
                    first_sweep(p, kept)
                    return
                skip, size = (INNER_AT, INNER) if sweep >= SWEEPS - 3 else (0, SLOT)
                here, base = at(p) + skip, at(p + 1) + skip
                cs = [coef[which, pl.ds(here, size), :] for which in range(7)]
                ds = [now[c, pl.ds(base, size), :] for c in range(2)]
                turned = (-ds[1], ds[0])
                for c in range(2):
                    off = spread_of(now.at[c], base, cs, ds[c], size)
                    applied = cs[6] * ds[c] - off + frequency_shift * turned[c]
                    left = resid[c, pl.ds(here, size), :] - applied
                    new = keep * ds[c] + push * left
                    if sweep < SWEEPS - 2:
                        resid[c, pl.ds(here, size), :] = left
                        later[c, pl.ds(base, size), :] = new
                    if kept:
                        field[out, c, pl.ds(base, size), :] = field[out, c, pl.ds(base, size), :] + new

            @pl.loop(0, OWN_PLANES + 1, unroll=OWN_PLANES + 1)
            def _(p):
                one_plane(p, True)

            if count > OWN_PLANES + 1:

                @pl.loop(OWN_PLANES + 1, count, unroll=count - OWN_PLANES - 1)
                def _(p):
                    one_plane(p, False)

    solve(0, [source])

    whole = pl.ds(SLOT, FLAT)
    mine_rows = OWN_PLANES * SLOT
    mine_planes = pl.ds(SLOT, mine_rows)
    table = place[pl.ds(0, mine_rows), :]
    both = jnp.concatenate([field[0, 0, mine_planes, :], field[0, 1, mine_planes, :]], axis=1)
    high, middle, low = [dot(part, table, ((0,), (0,))) for part in parts_of(both)]
    found = high + (middle + low)
    for c in range(2):
        spread = found[LANES * c : LANES * (c + 1)] * lane_hot[...]
        reads[member, pl.ds(c, 1), :] = jnp.sum(spread, axis=0, keepdims=True) * owned
    mine = reads.at[member]
    for i, dev in enumerate(twin + near):
        sent.append(remote(mine, mine, r_send.at[i], r_recv.at[member], dev))
    arrived(pair_recv, p_recv.at[0])
    pair_hot[...] = (
        lax.broadcasted_iota(jnp.int32, (NDET, PAIRS), 0).astype(F32) == pair_recv[0:1]
    ).astype(F32).astype(BF16)
    for j in range(1, SLABS):
        other = lax.rem(member + j, SLABS)
        arrived(reads.at[other], r_recv.at[other])
    readings = jnp.sum(reads[...], axis=0)
    wide = jnp.concatenate([readings, jnp.zeros((6, NDET), F32)], axis=0)
    model = dot_rows(wide, pair_hot[...], ((1,), (0,)))
    active = pair_recv[3:4]
    conj = jnp.concatenate(
        [
            (model[0:1] - pair_recv[1:2]) * active,
            (pair_recv[2:3] - model[1:2]) * active,
            jnp.zeros((6, PAIRS), F32),
        ],
        axis=0,
    )
    weights = dot_rows(conj, pair_hot[...], ((1,), (1,)))
    hot = lane_hot[...]
    right = None
    for part in parts_of(weights)[:2]:
        part = part.astype(F32)
        piece = jnp.concatenate([hot * part[0:1], hot * part[1:2]], axis=0).astype(BF16)
        term = dot(place[...], piece, ((1,), (1,)))
        right = term if right is None else right + term
    for c in range(2):
        direc_a[c, whole, :] = right[:, LANES * c : LANES * (c + 1)]

    solve(1, [direc_a.at[0], direc_a.at[1]])

    def row_copy(k):
        return remote_copy(
            ysend.at[k], yrecv.at[core, my_y], y_send.at[k], y_recv.at[core, my_y], row_to[k]
        )

    for k, q in enumerate(row_slots):
        base = at(q + 1) + INNER_AT
        refs = [[field.at[a, c] for c in range(2)] for a in range(2)]
        here = [[refs[a][c][pl.ds(base, INNER), :] for c in range(2)] for a in range(2)]
        sides = (
            lambda ref, b: x_plus(ref, b, INNER),
            lambda ref, b: x_minus(ref, b, INNER),
            lambda ref, b: y_plus(ref, b, ref[pl.ds(b, INNER), :], INNER) * yp_inner,
            lambda ref, b: y_minus(ref, b, ref[pl.ds(b, INNER), :], INNER) * ym_inner,
            lambda ref, b: ref[pl.ds(b + SLOT, INNER), :],
            lambda ref, b: ref[pl.ds(b - SLOT, INNER), :],
        )
        total = jnp.zeros((INNER, LANES), F32)
        for side in sides:
            gap = [[here[a][c] - side(refs[a][c], base) for c in range(2)] for a in range(2)]
            total = total + gap[0][0] * gap[1][0] - gap[0][1] * gap[1][1]
        grads[k, 0] = here[0][0] * here[1][0] - here[0][1] * here[1][1]
        grads[k, 1] = total
        for out in range(2):
            low, high = grads[k, out, pl.ds(3, 28), :], grads[k, out, pl.ds(4, 28), :]
            rows = pltpu.roll(jnp.where(lane[0:28] >= 64, low, high), 64, 1)
            ysend[k, pl.ds(25 * out, 25), :] = rows[0:25]
        ysend[k, pl.ds(50, 6), :] = jnp.zeros((6, LANES), F32)
        stays = is_me(row_to[k])

        @pl.when(jnp.logical_not(stays))
        def _():
            row_copy(k).start()

        @pl.when(stays)
        def _():
            pltpu.make_async_copy(ysend.at[k], yrecv.at[core, my_y], y_recv.at[core, my_y]).start()

    def final_copy(c, k):
        return remote_copy(
            fsend.at[c, final_h[k]], frecv.at[my_z // 2], f_send.at[4 * c + k], f_recv.at[my_z // 2], final_to[c][k]
        )

    for c in range(2):
        for y in range(4):
            arrived(yrecv.at[c, y], y_recv.at[c, y])
        ysum[c] = (yrecv[c, 0] + yrecv[c, 1]) + (yrecv[c, 2] + yrecv[c, 3])
        for h in range(4):
            for out in range(2):
                start = 25 * out + (25 * h) // 4
                low, high = ysum[c, pl.ds(start, 8), :], ysum[c, pl.ds(start + 1, 8), :]
                if h == 0:
                    fsend[c, h, out] = low
                else:
                    fsend[c, h, out] = pltpu.roll(jnp.where(lane[0:8] >= 32 * h, low, high), 128 - 32 * h, 1)
        for k in range(4):
            own = is_me(final_to[c][k])

            @pl.when(jnp.logical_not(own))
            def _():
                final_copy(c, k).start()

            @pl.when(own)
            def _():
                pltpu.make_async_copy(fsend.at[c, final_h[k]], frecv.at[my_z // 2], f_recv.at[my_z // 2]).start()

    for k in range(4):

        @pl.when(jnp.logical_not(is_me(native_to[k])))
        def _():
            native_copy(k).wait_send()

    for k in range(OWN_PLANES):

        @pl.when(jnp.logical_not(is_me(row_to[k])))
        def _():
            row_copy(k).wait_send()

    for slot in range(2, 8):
        coef_pass(slot).wait_send()
    for copy in sent:
        copy.wait_send()
    for m in range(8):
        arrived(frecv.at[m], f_recv.at[m])
    for out in range(2):
        total = frecv[0, out]
        for m in range(1, 8):
            total = total + frecv[m, out]
        for k in range(6):
            out_ref[out, 0:1, pl.ds(128 * k, 128)] = total[k : k + 1]
        out_ref[out, 0:1, pl.ds(768, 32)] = total[6:7, 0:32]
    for c in range(2):
        for k in range(4):

            @pl.when(jnp.logical_not(is_me(final_to[c][k])))
            def _():
                final_copy(c, k).wait_send()


def body(source_field, kappa, absorb, det_cell, pair_det, pair_count, measured):
    vmem = pl.BlockSpec(memory_space=pltpu.VMEM)
    hbm = pl.BlockSpec(memory_space=pltpu.HBM)
    out = jax.ShapeDtypeStruct((2, 1, 800), F32)
    dma = pltpu.SemaphoreType.DMA
    sums = pl.pallas_call(
        kernel,
        out_shape=out,
        in_specs=[hbm] * 7,
        out_specs=vmem,
        scratch_shapes=[
            pltpu.VMEM((3, PLANE_ROWS, LANES), F32),
            pltpu.SMEM((1,), jnp.int32),
            pltpu.VMEM((1, NDET), jnp.int32),
            pltpu.VMEM((1, PAIRS), jnp.int32),
            pltpu.VMEM((2, 1, PAIRS), F32),
            pltpu.VMEM((3, TALL, LANES), F32),
            pltpu.VMEM((8, 3, SLOT, LANES), F32),
            pltpu.VMEM((2, PLANES, SLOT, LANES), F32),
            pltpu.VMEM((STACKED, LANES), F32),
            pltpu.VMEM((STACKED, LANES), F32),
            pltpu.VMEM((7, FLAT, LANES), F32),
            pltpu.VMEM((2, STACKED, LANES), F32),
            pltpu.VMEM((2, STACKED, LANES), F32),
            pltpu.VMEM((2, FLAT, LANES), F32),
            pltpu.VMEM((2, 2, STACKED, LANES), F32),
            pltpu.VMEM((OWN_PLANES, 2, INNER, LANES), F32),
            pltpu.VMEM((FLAT, NDET), BF16),
            pltpu.VMEM((LANES, NDET), F32),
            pltpu.VMEM((NDET, PAIRS), BF16),
            pltpu.VMEM((8, PAIRS), F32),
            pltpu.VMEM((8, PAIRS), F32),
            pltpu.VMEM((SLABS, 2, NDET), F32),
            pltpu.VMEM((OWN_PLANES, 56, LANES), F32),
            pltpu.VMEM((2, 4, 56, LANES), F32),
            pltpu.VMEM((2, 56, LANES), F32),
            pltpu.VMEM((2, 4, 2, 8, LANES), F32),
            pltpu.VMEM((8, 2, 8, LANES), F32),
            dma((7,)), dma((8,)), dma((8,)), dma((4,)), dma((8,)), dma((1,)), dma((2,)),
            dma((3,)), dma((3,)), dma((1,)), dma((1,)),
            dma((6,)), dma((6,)), dma((6,)), dma((6,)),
            dma((15,)), dma((16,)), dma((8,)), dma((2, 4)), dma((8,)), dma((8,)),
        ],
        compiler_params=pltpu.CompilerParams(
            collective_id=0, has_side_effects=True, vmem_limit_bytes=60 * 1024 * 1024
        ),
    )(
        pair_count,
        source_field.reshape(PLANE_ROWS, LANES),
        kappa.reshape(PLANE_ROWS, LANES),
        absorb.reshape(PLANE_ROWS, LANES),
        det_cell.reshape(1, NDET),
        pair_det,
        measured,
    )
    return (-sums[0], -0.5 * sums[1])


def solution(mesh):
    placed = (
        P("src", "slab", None),
        P("slab", None),
        P("slab", None),
        P(),
        P("src", None),
        P("src"),
        P(None, "src", None),
    )
    return jax.shard_map(
        body,
        mesh=mesh,
        in_specs=placed,
        out_specs=(P("slab", "src"), P("slab", "src")),
        check_vma=False,
    )
```
